32 devices in a mesh: seq: 4 (over y, x), head: 8 (over z, core).
Axes of the slice: x: 2, y: 2, z: 4, core: 2. Of those that a mesh axis runs over, the one named last changes fastest.
Arguments:
- queries: bfloat16 [2048, 1024], P('seq', 'head'), may hold values from -5 to 5
- keys: bfloat16 [2048, 1024], P('seq', 'head'), may hold values from -5 to 5
- values: bfloat16 [2048, 1024], P('seq', 'head'), may hold values from -5 to 5
- grad_out: bfloat16 [2048, 1024], P('seq', 'head'), may hold values from -6 to 6
Outputs:
- attended: bfloat16 [2048, 1024], P('seq', 'head')
- grad_query: bfloat16 [2048, 1024], P(('seq', 'head'))
- grad_key: bfloat16 [2048, 1024], P(('seq', 'head'))
- grad_value: bfloat16 [2048, 1024], P(('seq', 'head'))
The draws below stay inside these ranges and needn't reach their ends.
All inputs are finite; a program needn't handle non-finite values.
Results may differ from the reference program's by a relative error of at most 0.024.
Values may be sent and summed in bfloat16 or wider, within the bound.
No kernel may reach another device: no remote copies, remote signals or barrier semaphores. Data moves between devices by JAX's collectives and lax.ppermute only.
A program may use at most 64 MiB of HBM per device.

```python
from functools import reduce
import jax
import jax.numpy as jnp
from jax import lax

HEAD_DIM = 128
BLOCK = 128
HEADS = 8
WIDTH = 1024
TOKENS = 2048


def region_means(key):
    means = jax.random.normal(key, (64, WIDTH), jnp.float32)
    return jnp.repeat(means, TOKENS // 64, axis=0)


def rough_rows(key, salt):
    return jax.random.normal(jax.random.fold_in(key, salt), (TOKENS, WIDTH), jnp.float32)


def draw_queries(key, part):
    base = jnp.clip(rough_rows(key, 1) + region_means(jax.random.fold_in(key, 2)), -5.0, 5.0)
    return base.astype(jnp.bfloat16)


def draw_keys(key, part):
    base = jnp.clip(rough_rows(key, 11) + region_means(jax.random.fold_in(key, 12)), -5.0, 5.0)
    return base.astype(jnp.bfloat16)


def draw_values(key, part):
    return jnp.clip(rough_rows(key, 21) + region_means(jax.random.fold_in(key, 22)), -5.0, 5.0).astype(jnp.bfloat16)


def level_of(key, shape, shards, least, top_value):
    gain = 1.0
    for position, shards_of in shards:
        heights = jax.random.uniform(jax.random.fold_in(jax.random.fold_in(key, 6), position), (shards_of,), jnp.float32, least / len(shards), top_value / len(shards))
        gain = gain * jnp.repeat(jnp.exp(heights), shape[position] // shards_of).reshape((-1,) + (1,) * (len(shape) - 1 - position))
    return gain


def bell_draw(stream_key, shape, width, bound, split=(), kind=jnp.bfloat16):
    drawn = width * jax.random.normal(stream_key, shape, jnp.float32)
    if split:
        drawn = drawn * level_of(stream_key, shape, split, -0.22, 0.18)
    return jnp.clip(drawn, -bound, bound).astype(kind)


def setup_inputs(seed: int = 0) -> dict:
    arg_keys = jax.random.split(jax.random.key(seed), 5)
    return {
        "queries": draw_queries(jax.random.fold_in(arg_keys[4], 71), 0),
        "keys": draw_keys(jax.random.fold_in(arg_keys[4], 71), 0),
        "values": draw_values(jax.random.fold_in(arg_keys[4], 71), 0),
        "grad_out": bell_draw(arg_keys[3], (TOKENS, WIDTH), 1.0, 6.0, ((0, 4), (1, 8))),
    }


MASKED = -1e+30

def coarsen(stacked):
    in_shape = stacked.shape
    paired = stacked.astype(jnp.float32).reshape(in_shape[:-2] + (in_shape[-2] // 2, 2, in_shape[-1]))
    halved = ((paired[..., 0, :] + paired[..., 1, :]) * 0.5).astype(jnp.bfloat16)
    return lax.optimization_barrier(halved)

def unit_stats(query_rows, query_index, key_rows, value_rows, key_index, block_count, coarse_level, block_rows):
    scale = query_rows.shape[-1] ** (-0.5)
    scores = jnp.einsum('urd,ukd->urk', query_rows.astype(jnp.float32), key_rows.astype(jnp.float32)) * scale
    row_block = query_index // block_rows
    key_block = key_index // block_rows
    block_gap = jnp.abs(row_block[:, :, None] - key_block[:, None, :])
    if coarse_level == 0:
        allowed = block_gap <= 1
    else:
        parent_gap = jnp.abs(row_block[:, :, None] // 2 - key_block[:, None, :] // 2)
        allowed = (block_gap >= 2) & (parent_gap <= 1)
    allowed = allowed & (key_block[:, None, :] >= 0) & (key_block[:, None, :] < block_count)
    scores = jnp.where(allowed, scores, MASKED)
    row_peak = lax.optimization_barrier(jnp.max(scores, axis=-1))
    exp_scores = jnp.exp(scores - row_peak[..., None])
    multiple = float(2 ** coarse_level)
    row_total = lax.optimization_barrier(jnp.sum(exp_scores, axis=-1)) * multiple
    rounded = lax.optimization_barrier(exp_scores.astype(jnp.bfloat16))
    mixed_rows = jnp.einsum('urk,ukd->urd', rounded.astype(jnp.float32), value_rows.astype(jnp.float32)) * multiple
    return (row_peak, row_total, mixed_rows)

def windowed(coarse_query, padded, first_row, span_rows, block_count, coarse_level, block_rows):
    row_count, head_width = coarse_query.shape
    unit_count = row_count // span_rows
    unit_rows = padded.reshape(2, unit_count + 2, span_rows, head_width)
    window = jnp.concatenate([unit_rows[:, :-2], unit_rows[:, 1:-1], unit_rows[:, 2:]], axis=2)
    query_index = (first_row + jnp.arange(row_count, dtype=jnp.int32)).reshape(unit_count, span_rows)
    key_index = first_row - span_rows + jnp.arange(unit_count, dtype=jnp.int32)[:, None] * span_rows + jnp.arange(3 * span_rows, dtype=jnp.int32)[None, :]
    return unit_stats(coarse_query.reshape(unit_count, span_rows, head_width), query_index, window[0], window[1], key_index, block_count, coarse_level, block_rows)

def expand(stats, coarse_level, head_width):
    repeats = 2 ** coarse_level
    return (jnp.repeat(stats[0].reshape(-1), repeats), jnp.repeat(stats[1].reshape(-1), repeats), jnp.repeat(stats[2].reshape(-1, head_width), repeats, axis=0))

def combine(level_stats):
    overall_peak = reduce(jnp.maximum, [entry[0] for entry in level_stats])
    factors = [jnp.exp(entry[0] - overall_peak) for entry in level_stats]
    denominator = reduce(jnp.add, [factor * entry[1] for factor, entry in zip(factors, level_stats)])
    numerator = reduce(jnp.add, [factor[:, None] * entry[2] for factor, entry in zip(factors, level_stats)])
    return (numerator / denominator[:, None]).astype(jnp.bfloat16)

def attend_head(query_rows, key_rows, value_rows):
    token_count, head_width = query_rows.shape
    fine_blocks = token_count // BLOCK
    top_level = (fine_blocks // 4).bit_length() - 1
    key_value = jnp.stack([key_rows, value_rows])
    coarse_query = query_rows
    level_stats = []
    for coarse_level in range(top_level + 1):
        span_rows = BLOCK if coarse_level == 0 else 2 * BLOCK
        if coarse_level > 0:
            coarse_query = coarsen(coarse_query)
            key_value = coarsen(key_value)
        padded = jnp.pad(key_value, ((0, 0), (span_rows, span_rows), (0, 0)))
        stats = windowed(coarse_query, padded, 0, span_rows, fine_blocks >> coarse_level, coarse_level, BLOCK)
        level_stats.append(expand(stats, coarse_level, head_width))
    return combine(level_stats)

def one_head(inputs):
    query_rows, key_rows, value_rows, cotangent = inputs
    attended, pullback = jax.vjp(attend_head, query_rows, key_rows, value_rows)
    grad_query, grad_key, grad_value = pullback(cotangent)
    return (attended, grad_query, grad_key, grad_value)

def reference(queries, keys, values, grad_out):

    def by_head(matrix):
        return matrix.reshape(TOKENS, HEADS, HEAD_DIM).transpose(1, 0, 2)

    def from_head(stacked):
        return stacked.transpose(1, 0, 2).reshape(TOKENS, WIDTH)
    results = lax.map(one_head, (by_head(queries), by_head(keys), by_head(values), by_head(grad_out)))
    return (from_head(results[0]), from_head(results[1]), from_head(results[2]), from_head(results[3]))
```

```python
import functools

import jax
import jax.numpy as jnp
from jax import lax
from jax.experimental import pallas as pl
from jax.experimental.pallas import tpu as pltpu
from jax.sharding import PartitionSpec as P

BLOCK = 128
EDGE = BLOCK // 2
REST = 2 * BLOCK - EDGE
MASKED = -1e30
LOG2E = 1.4426950408889634
F32 = jnp.float32
BF16 = jnp.bfloat16
VMEM = pl.BlockSpec(memory_space=pltpu.VMEM)


def nt(a, b):
    return lax.dot_general(a, b, (((1,), (1,)), ((), ())), preferred_element_type=F32)


def nn(a, b):
    return lax.dot_general(a, b, (((1,), (0,)), ((), ())), preferred_element_type=F32)


def tn(a, b):
    return lax.dot_general(a, b, (((0,), (0,)), ((), ())), preferred_element_type=F32)


def pair_sum(x, scratch):
    rows = x.shape[0]
    scratch[:rows] = x
    return scratch[pl.ds(0, rows // 2, stride=2), :] + scratch[pl.ds(1, rows // 2, stride=2), :]


def coarse(x, scratch):
    return (pair_sum(x.astype(F32), scratch) * 0.5).astype(BF16)


def spread(x, scratch):
    rows = x.shape[0]
    scratch[pl.ds(0, rows, stride=2), :] = x
    scratch[pl.ds(1, rows, stride=2), :] = x
    return scratch[: 2 * rows]


def wide_distances(seq_count):
    return sorted({i ^ (i + 1) for i in range(seq_count - 1)})


def prep_kernel(seq_count, key_ref, value_ref, *refs):
    sends, scratches = refs[: seq_count - 1], refs[seq_count - 1 :]
    seq_index = lax.axis_index("seq")
    wides = wide_distances(seq_count)
    rows = key_ref.shape[0]
    for i, ref in enumerate((key_ref, value_ref)):
        level_1 = coarse(ref[...], scratches[2 * i])
        level_2 = coarse(level_1, scratches[2 * i + 1])
        for d in range(1, seq_count):
            out = sends[d - 1]
            partner = seq_index ^ d
            if d not in wides:
                out[i] = level_2
                continue

            @pl.when(partner == seq_index + 1)
            def _():
                out[i, :BLOCK] = ref[rows - BLOCK :]
                out[i, BLOCK:] = level_1[:REST]

            @pl.when(partner == seq_index - 1)
            def _():
                out[i, :BLOCK] = ref[:BLOCK]
                out[i, BLOCK:] = level_1[EDGE:]

            @pl.when((partner != seq_index + 1) & (partner != seq_index - 1))
            def _():
                out[i, :BLOCK] = level_2
                out[i, BLOCK:] = level_1[:REST]


def slots_of(block, block_count):
    parent, odd = block // 2, block % 2
    if block_count == 4:
        first = parent == 0
        return [
            (jnp.where(first, 3, 0), None),
            (jnp.where(first, 2, 1), jnp.where(first, odd == 0, odd == 1)),
        ]
    near = jnp.where(odd == 0, 2 * parent + 2, 2 * parent - 1)
    raw = [2 * parent - 2, near, 2 * parent + 3]
    return [(jnp.clip(j, 0, block_count - 1), (j >= 0) & (j < block_count)) for j in raw]


def softmax_parts(parts):
    peak = functools.reduce(jnp.maximum, [jnp.max(p, axis=-1, keepdims=True) for p in parts])
    exps = [jnp.exp2(p - peak) for p in parts]
    total = functools.reduce(jnp.add, [jnp.sum(e, axis=-1, keepdims=True) for e in exps])
    return peak, exps, total


def wide_lanes(column, width):
    return jnp.broadcast_to(column, (column.shape[0], width))


def main_kernel(seq_count, top_level, *refs):
    refs = list(refs)

    def take(count):
        taken = refs[:count]
        del refs[:count]
        return taken

    query_ref, key_ref, value_ref, cot_ref = take(4)
    received = take(seq_count - 1)
    (attended_ref,) = take(1)
    sends = take(seq_count - 1)
    grad_query_ref, local_ref = take(2)
    ext, near = take(2)
    panels = take(top_level - 1)
    panel_grads = take(top_level - 1)
    pools = refs

    def pool():
        return pools.pop(0)

    seq_index = lax.axis_index("seq")
    wides = wide_distances(seq_count)
    rows, width = query_ref.shape
    blocks = rows // BLOCK
    scale = width ** (-0.5)
    factor = scale * LOG2E
    has_prev, has_next = seq_index > 0, seq_index < seq_count - 1

    for panel in panels:
        panel[...] = jnp.zeros(panel.shape, BF16)
    for i, ref in enumerate((key_ref, value_ref)):
        ext[i, BLOCK : BLOCK + rows] = ref[...]

    @pl.when(seq_index == 0)
    def _():
        ext[:, :BLOCK] = jnp.zeros((2, BLOCK, width), BF16)
        near[:, : 2 * BLOCK] = jnp.zeros((2, 2 * BLOCK, width), BF16)

    @pl.when(seq_index == seq_count - 1)
    def _():
        ext[:, BLOCK + rows :] = jnp.zeros((2, BLOCK, width), BF16)
        near[:, 2 * BLOCK :] = jnp.zeros((2, 2 * BLOCK, width), BF16)

    halo_scratch = pool()
    for d in range(1, seq_count):
        got = received[d - 1]
        partner = seq_index ^ d
        at = pl.ds(pl.multiple_of(partner * BLOCK, BLOCK), BLOCK)
        if d not in wides:
            for i in range(2):
                panels[0][i, at] = got[i]
            continue

        @pl.when(partner == seq_index - 1)
        def _():
            for i in range(2):
                ext[i, :BLOCK] = got[i, :BLOCK]
                near[i, :REST] = got[i, BLOCK:]
                near[i, REST : 2 * BLOCK] = coarse(got[i, :BLOCK], halo_scratch)

        @pl.when(partner == seq_index + 1)
        def _():
            for i in range(2):
                ext[i, BLOCK + rows :] = got[i, :BLOCK]
                near[i, 2 * BLOCK : 2 * BLOCK + EDGE] = coarse(got[i, :BLOCK], halo_scratch)
                near[i, 2 * BLOCK + EDGE :] = got[i, BLOCK:]

        @pl.when((partner != seq_index + 1) & (partner != seq_index - 1))
        def _():
            for i in range(2):
                panels[0][i, at] = got[i, :BLOCK]

    panel_scratch = pool()
    for level in range(3, top_level + 1):
        for i in range(2):
            panels[level - 2][i] = coarse(panels[level - 3][i], panel_scratch)

    level_queries = [query_ref[...]]
    for level in range(1, top_level + 1):
        level_queries.append(coarse(level_queries[-1], pool()))

    def masked(scores, valid):
        return scores if valid is None else jnp.where(valid, scores, MASKED)

    def unit(query, pieces):
        scores = []
        for key, _, valid in pieces:
            scores.append(masked(nt(query, key) * factor, valid))
        peak, exps, total = softmax_parts(scores)
        rounded = [e.astype(BF16) for e in exps]
        sums = functools.reduce(jnp.add, [nn(r, p[1]) for r, p in zip(rounded, pieces)])
        return wide_lanes(peak, width), wide_lanes(total, width), sums, exps, rounded

    def window(ref, lo, hi):
        return ref[0, lo * BLOCK : hi * BLOCK], ref[1, lo * BLOCK : hi * BLOCK]

    level_pieces = []
    fine = []
    for a in range(blocks):
        if a == 0:
            cuts = [(0, 1, has_prev), (1, 3, None)]
        elif a == blocks - 1:
            cuts = [(a, a + 2, None), (a + 2, a + 3, has_next)]
        else:
            cuts = [(a, a + 3, None)]
        fine.append([window(ext, lo, hi) + (valid, (lo, hi)) for lo, hi, valid in cuts])
    level_pieces.append(fine)
    level_pieces.append(
        [
            [
                window(near, 0, 1) + (has_prev, (0, 1)),
                window(near, 2, 4) + (has_next, (2, 4)),
            ],
            [
                window(near, 0, 2) + (has_prev, (0, 2)),
                window(near, 3, 4) + (has_next, (3, 4)),
            ],
        ]
    )
    for level in range(2, top_level + 1):
        block_count = seq_count >> (level - 2)
        pieces = []
        for index, valid in slots_of(seq_index >> (level - 2), block_count):
            at = pl.ds(pl.multiple_of(index * BLOCK, BLOCK), BLOCK)
            panel = panels[level - 2]
            pieces.append((panel[0, at], panel[1, at], valid, at))
        level_pieces.append([pieces])

    level_units = []
    for level, pieces_of in enumerate(level_pieces):
        query = level_queries[level]
        step = query.shape[0] // len(pieces_of)
        level_units.append(
            [
                unit(query[a * step : (a + 1) * step], [p[:3] for p in pieces])
                for a, pieces in enumerate(pieces_of)
            ]
        )

    def stacked(units, which):
        return jnp.concatenate([u[which] for u in units], axis=0)

    run = [stacked(level_units[top_level], w) for w in range(3)]
    own_factors, run_factors = [None] * top_level, [None] * top_level
    for level in range(top_level - 1, -1, -1):
        up_peak, up_total, up_sums = [spread(x, pool()) for x in run]
        peak, total, sums = [stacked(level_units[level], w) for w in range(3)]
        both = jnp.maximum(peak, up_peak)
        own = jnp.exp2(peak - both)
        up = 2.0 * jnp.exp2(up_peak - both)
        own_factors[level], run_factors[level] = own, up
        run = [both, own * total + up * up_total, own * sums + up * up_sums]

    inverse = 1.0 / run[1]
    attended = run[2] * inverse
    attended_ref[...] = attended.astype(BF16)

    cot = cot_ref[...].astype(F32)
    inner = wide_lanes(jnp.sum(cot * attended, axis=-1, keepdims=True), width)
    grad, shift = cot * inverse, inner * inverse
    level_grads = []
    for level in range(top_level):
        level_grads.append((own_factors[level] * grad, own_factors[level] * shift))
        grad = pair_sum(run_factors[level] * grad, pool())
        shift = pair_sum(run_factors[level] * shift, pool())
    level_grads.append((grad, shift))

    def unit_back(query, grad, shift, pieces, exps, rounded):
        grad_rounded = grad.astype(BF16)
        grad_scaled = (grad * scale).astype(BF16)
        shift_scaled = shift[:, :1] * scale
        grad_query = None
        outs = []
        for piece, e, r in zip(pieces, exps, rounded):
            key, value = piece[0], piece[1]
            score_grad = (e * (nt(grad_scaled, value) - shift_scaled)).astype(BF16)
            part = nn(score_grad, key)
            grad_query = part if grad_query is None else grad_query + part
            outs.append((tn(score_grad, query), tn(r, grad_rounded)))
        return grad_query, outs

    for panel_grad in panel_grads:
        panel_grad[...] = jnp.zeros(panel_grad.shape, F32)

    grad_queries = []
    fine_parts = [[[] for _ in range(blocks + 2)] for _ in range(2)]
    near_parts = [[[] for _ in range(4)] for _ in range(2)]
    for level, pieces_of in reversed(list(enumerate(level_pieces))):
        query = level_queries[level]
        step = query.shape[0] // len(pieces_of)
        grad, shift = level_grads[level]
        parts = []
        for a, pieces in enumerate(pieces_of):
            cut = slice(a * step, (a + 1) * step)
            exps, rounded = level_units[level][a][3:]
            grad_query, outs = unit_back(query[cut], grad[cut], shift[cut], pieces, exps, rounded)
            parts.append(grad_query)
            for piece, out in zip(pieces, outs):
                for i in range(2):
                    if level >= 2:
                        panel_grads[level - 2][i, piece[3]] += out[i]
                        continue
                    into = fine_parts if level == 0 else near_parts
                    lo, hi = piece[3]
                    for b in range(lo, hi):
                        into[i][b].append(out[i][(b - lo) * BLOCK : (b - lo + 1) * BLOCK])
        grad_queries.append(jnp.concatenate(parts, axis=0))

    run_grad = grad_queries[0]
    for grad_query in grad_queries[1:]:
        run_grad = grad_query + 0.5 * spread(run_grad, pool())
    grad_query_ref[...] = run_grad.astype(BF16)

    for level in range(top_level, 2, -1):
        for i in range(2):
            panel_grads[level - 3][i] += 0.5 * spread(panel_grads[level - 2][i], panel_scratch)

    def total_of(parts):
        return functools.reduce(jnp.add, parts)

    for i in range(2):
        for b in range(blocks):
            local_ref[i, b * BLOCK : (b + 1) * BLOCK] = total_of(fine_parts[i][b + 1])
    near_grads = [[total_of(p) for p in near_parts[i]] for i in range(2)]
    to_prev = [
        total_of(fine_parts[i][0]) + 0.5 * spread(near_grads[i][1][EDGE:], pool()) for i in range(2)
    ]
    to_next = [
        total_of(fine_parts[i][blocks + 1]) + 0.5 * spread(near_grads[i][2][:EDGE], pool())
        for i in range(2)
    ]
    for d in range(1, seq_count):
        out = sends[d - 1]
        partner = seq_index ^ d
        at = pl.ds(pl.multiple_of(partner * BLOCK, BLOCK), BLOCK)
        if d not in wides:
            for i in range(2):
                out[i] = panel_grads[0][i, at].astype(BF16)
            continue

        @pl.when(partner == seq_index - 1)
        def _():
            for i in range(2):
                out[i, :BLOCK] = to_prev[i].astype(BF16)
                out[i, BLOCK : 2 * BLOCK] = near_grads[i][0].astype(BF16)
                out[i, 2 * BLOCK :] = near_grads[i][1][:EDGE].astype(BF16)

        @pl.when(partner == seq_index + 1)
        def _():
            for i in range(2):
                out[i, :BLOCK] = to_next[i].astype(BF16)
                out[i, BLOCK : BLOCK + EDGE] = near_grads[i][2][EDGE:].astype(BF16)
                out[i, BLOCK + EDGE :] = near_grads[i][3].astype(BF16)

        @pl.when((partner != seq_index + 1) & (partner != seq_index - 1))
        def _():
            for i in range(2):
                out[i, :BLOCK] = panel_grads[0][i, at].astype(BF16)
                out[i, BLOCK:] = jnp.zeros((REST, width), BF16)


def combine_kernel(seq_count, head_count, grad_query_ref, local_ref, *refs):
    received, refs = refs[: seq_count - 1], refs[seq_count - 1 :]
    outs, refs = refs[:head_count], refs[head_count:]
    total, level_1, level_2 = refs
    seq_index, head_index = lax.axis_index("seq"), lax.axis_index("head")
    wides = wide_distances(seq_count)
    rows, width = local_ref.shape[1:]
    share = rows // head_count

    level_1[...] = jnp.zeros(level_1.shape, F32)
    level_2[...] = jnp.zeros(level_2.shape, F32)
    for i in range(2):
        total[i] = local_ref[i]
    for d in range(1, seq_count):
        got = received[d - 1]
        partner = seq_index ^ d
        if d not in wides:
            for i in range(2):
                level_2[i] += got[i].astype(F32)
            continue

        @pl.when(partner == seq_index - 1)
        def _():
            for i in range(2):
                total[i, :BLOCK] += got[i, :BLOCK].astype(F32)
                level_1[i, EDGE:] += got[i, BLOCK:].astype(F32)

        @pl.when(partner == seq_index + 1)
        def _():
            for i in range(2):
                total[i, rows - BLOCK :] += got[i, :BLOCK].astype(F32)
                level_1[i, :REST] += got[i, BLOCK:].astype(F32)

        @pl.when((partner != seq_index + 1) & (partner != seq_index - 1))
        def _():
            for i in range(2):
                level_2[i] += got[i, :BLOCK].astype(F32)

    for i in range(2):
        half = level_2[i] * 0.5
        for phase in range(2):
            level_1[i, pl.ds(phase, half.shape[0], stride=2), :] += half
        half = level_1[i] * 0.5
        for phase in range(2):
            total[i, pl.ds(phase, half.shape[0], stride=2), :] += half
    for d in range(head_count):
        at = pl.ds(pl.multiple_of((head_index ^ d) * share, share), share)
        outs[d][0] = grad_query_ref[at, :]
        outs[d][1] = total[0, at].astype(BF16)
        outs[d][2] = total[1, at].astype(BF16)


def place_kernel(head_count, *refs):
    parts, outs = refs[:head_count], refs[head_count:]
    head_index = lax.axis_index("head")
    width = parts[0].shape[-1]
    for d in range(head_count):
        at = pl.ds(pl.multiple_of((head_index ^ d) * width, width), width)
        for i in range(3):
            outs[i][:, at] = parts[d][i]


def call(kernel, outs, scratch, args):
    return pl.pallas_call(
        kernel,
        out_shape=outs,
        in_specs=[VMEM] * len(args),
        out_specs=[VMEM] * len(outs),
        scratch_shapes=scratch,
        compiler_params=pltpu.CompilerParams(vmem_limit_bytes=48 * 2**20),
    )(*args)


def swap(x, axis, distance):
    return lax.ppermute(x, axis, [(i, i ^ distance) for i in range(lax.axis_size(axis))])


def per_device(queries, keys, values, grad_out):
    seq_count, head_count = lax.axis_size("seq"), lax.axis_size("head")
    rows, width = queries.shape
    assert rows == 4 * BLOCK
    fine_blocks = rows * seq_count // BLOCK
    top_level = (fine_blocks // 4).bit_length() - 1
    wides = wide_distances(seq_count)
    distances = range(1, seq_count)

    def shape(dims, dtype=BF16):
        return jax.ShapeDtypeStruct(dims, dtype)

    def f32(*dims):
        return pltpu.VMEM(dims, F32)

    payloads = [shape((2, BLOCK + REST if d in wides else BLOCK, width)) for d in distances]
    sends = call(
        functools.partial(prep_kernel, seq_count),
        payloads,
        [f32(rows, width), f32(rows // 2, width)] * 2,
        (keys, values),
    )
    received = [swap(x, "seq", d) for d, x in zip(distances, sends)]

    panel_rows = [(seq_count >> (level - 2)) * BLOCK for level in range(2, top_level + 1)]
    pools = [f32(BLOCK, width), f32(max(seq_count * BLOCK, rows), width)]
    pools += [f32(rows >> level, width) for level in range(top_level)]
    for level in range(top_level - 1, -1, -1):
        pools += [f32(rows >> level, width)] * 3
    for level in range(top_level):
        pools += [f32(rows >> level, width)] * 2
    for level in range(top_level - 1, -1, -1):
        pools += [f32(rows >> level, width)]
    pools += [f32(BLOCK, width)] * 4
    main = call(
        functools.partial(main_kernel, seq_count, top_level),
        [shape((rows, width))] + payloads + [shape((rows, width)), shape((2, rows, width), F32)],
        [pltpu.VMEM((2, rows + 2 * BLOCK, width), BF16), pltpu.VMEM((2, 4 * BLOCK, width), BF16)]
        + [pltpu.VMEM((2, r, width), BF16) for r in panel_rows]
        + [f32(2, r, width) for r in panel_rows]
        + pools,
        (queries, keys, values, grad_out, *received),
    )
    attended, sends, grad_query, local = main[0], main[1:seq_count], main[-2], main[-1]
    returned = [swap(x, "seq", d) for d, x in zip(distances, sends)]

    share = rows // head_count
    parts = call(
        functools.partial(combine_kernel, seq_count, head_count),
        [shape((3, share, width))] * head_count,
        [f32(2, rows, width), f32(2, rows // 2, width), f32(2, rows // 4, width)],
        (grad_query, local, *returned),
    )
    parts = [parts[0]] + [swap(parts[d], "head", d) for d in range(1, head_count)]
    grads = call(
        functools.partial(place_kernel, head_count),
        [shape((share, head_count * width))] * 3,
        [],
        parts,
    )
    return (attended, *grads)


def solution(mesh):
    return jax.shard_map(
        per_device,
        mesh=mesh,
        in_specs=(P("seq", "head"),) * 4,
        out_specs=(P("seq", "head"),) + (P(("seq", "head"), None),) * 3,
        check_vma=False,
    )
```

```python
import functools

import jax
import jax.numpy as jnp
from jax import lax
from jax.experimental import pallas as pl
from jax.experimental.pallas import tpu as pltpu
from jax.sharding import PartitionSpec as P

BLOCK = 128
EDGE = BLOCK // 2
REST = 2 * BLOCK - EDGE
MASKED = -1e30
LOG2E = 1.4426950408889634
F32 = jnp.float32
BF16 = jnp.bfloat16
VMEM = pl.BlockSpec(memory_space=pltpu.VMEM)


def nt(a, b):
    return lax.dot_general(a, b, (((1,), (1,)), ((), ())), preferred_element_type=F32)


def nn(a, b):
    return lax.dot_general(a, b, (((1,), (0,)), ((), ())), preferred_element_type=F32)


def tn(a, b):
    return lax.dot_general(a, b, (((0,), (0,)), ((), ())), preferred_element_type=F32)


def pair_sum(x, scratch):
    rows = x.shape[0]
    scratch[:rows] = x
    return scratch[pl.ds(0, rows // 2, stride=2), :] + scratch[pl.ds(1, rows // 2, stride=2), :]


def coarse(x, scratch):
    return (pair_sum(x.astype(F32), scratch) * 0.5).astype(BF16)


def spread(x, scratch):
    rows = x.shape[0]
    scratch[pl.ds(0, rows, stride=2), :] = x
    scratch[pl.ds(1, rows, stride=2), :] = x
    return scratch[: 2 * rows]


def wide_distances(seq_count):
    return sorted({i ^ (i + 1) for i in range(seq_count - 1)})


def seq_order(seq_count):
    wides = wide_distances(seq_count)
    return wides[::-1] + [d for d in range(1, seq_count) if d not in wides]


def head_order(head_count):
    return [d for d in range(4, head_count)] + [d for d in (2, 3, 1) if d < head_count]


def prep_kernel(seq_count, *refs):
    sources, refs = refs[:4], refs[4:]
    held, refs = refs[0], refs[1:]
    sends, scratches, sems = refs[: seq_count - 1], refs[seq_count - 1 : -1], refs[-1]
    sends = dict(zip(seq_order(seq_count), sends))
    seq_index = lax.axis_index("seq")
    wides = wide_distances(seq_count)
    rows = held.shape[1]
    copies = [
        pltpu.make_async_copy(source, held.at[i], sems.at[i]) for i, source in enumerate(sources)
    ]
    for i in (1, 2, 0, 3):
        copies[i].start()
    for i in range(2):
        copies[1 + i].wait()
        ref = held.at[1 + i]
        level_1 = coarse(ref[...], scratches[2 * i])
        level_2 = coarse(level_1, scratches[2 * i + 1])
        for d in range(1, seq_count):
            out = sends[d]
            partner = seq_index ^ d
            if d not in wides:
                out[i] = level_2
                continue

            @pl.when(partner == seq_index + 1)
            def _():
                out[i, :BLOCK] = ref[rows - BLOCK :]
                out[i, BLOCK:] = level_1[:REST]

            @pl.when(partner == seq_index - 1)
            def _():
                out[i, :BLOCK] = ref[:BLOCK]
                out[i, BLOCK:] = level_1[EDGE:]

            @pl.when((partner != seq_index + 1) & (partner != seq_index - 1))
            def _():
                out[i, :BLOCK] = level_2
                out[i, BLOCK:] = level_1[:REST]

    copies[0].wait()
    copies[3].wait()


def slots_of(block, block_count):
    parent, odd = block // 2, block % 2
    if block_count == 4:
        first = parent == 0
        return [
            (jnp.where(first, 3, 0), None),
            (jnp.where(first, 2, 1), jnp.where(first, odd == 0, odd == 1)),
        ]
    near = jnp.where(odd == 0, 2 * parent + 2, 2 * parent - 1)
    raw = [2 * parent - 2, near, 2 * parent + 3]
    return [(jnp.clip(j, 0, block_count - 1), (j >= 0) & (j < block_count)) for j in raw]


def across(x, width):
    return jnp.concatenate([x] * (width // x.shape[1]), axis=1)


def lanes(column):
    return jnp.broadcast_to(column, (column.shape[0], BLOCK))


def row_max(x):
    return lanes(jnp.max(x, axis=-1, keepdims=True))


def row_sum(x):
    return lanes(jnp.sum(x, axis=-1, keepdims=True))


def total_of(parts):
    return functools.reduce(jnp.add, parts)


def rows_of(block, count=1):
    return slice(block * BLOCK, (block + count) * BLOCK)


def own_window(a, blocks):
    return max(a - 1, 0), min(a + 2, blocks)


def fine_kernel(held, stats, *refs):
    levels = len(refs) // 2
    blocks, width = held.shape[1] // BLOCK, held.shape[2]
    factor = width ** (-0.5) * LOG2E
    for a in range(blocks):
        lo, hi = own_window(a, blocks)
        window = rows_of(lo, hi - lo)
        scores = nt(held[0, rows_of(a)], held[1, window]) * factor
        peak = row_max(scores)
        exps = jnp.exp2(scores - across(peak, scores.shape[1]))
        stats[0, rows_of(a)] = peak
        stats[1, rows_of(a)] = row_sum(exps)
        stats[2, rows_of(a)] = nn(exps.astype(BF16), held[2, window])
    query = held[0]
    for level in range(levels):
        query = coarse(query, refs[levels + level])
        refs[level][...] = query


def main_kernel(seq_count, top_level, *refs):
    refs = list(refs)

    def take(count):
        taken = refs[:count]
        del refs[:count]
        return taken

    held, stats = take(2)
    query_refs = take(top_level)
    received = dict(zip(seq_order(seq_count), take(seq_count - 1)))
    (attended_ref,) = take(1)
    sends = dict(zip(seq_order(seq_count), take(seq_count - 1)))
    back, partial_ref = take(2)
    halo, near = take(2)
    panels = take(top_level - 1)
    panel_grads = take(top_level - 1)
    pools = refs

    def pool():
        return pools.pop(0)

    seq_index = lax.axis_index("seq")
    wides = wide_distances(seq_count)
    rows, width = held.shape[1:]
    blocks = rows // BLOCK
    scale = width ** (-0.5)
    factor = scale * LOG2E
    has_prev, has_next = seq_index > 0, seq_index < seq_count - 1

    for panel in panels:
        panel[...] = jnp.zeros(panel.shape, BF16)

    @pl.when(seq_index == 0)
    def _():
        halo[:, :BLOCK] = jnp.zeros((2, BLOCK, width), BF16)
        near[:, : 2 * BLOCK] = jnp.zeros((2, 2 * BLOCK, width), BF16)

    @pl.when(seq_index == seq_count - 1)
    def _():
        halo[:, BLOCK:] = jnp.zeros((2, BLOCK, width), BF16)
        near[:, 2 * BLOCK :] = jnp.zeros((2, 2 * BLOCK, width), BF16)

    halo_scratch = pool()
    for d in range(1, seq_count):
        got = received[d]
        partner = seq_index ^ d
        at = pl.ds(pl.multiple_of(partner * BLOCK, BLOCK), BLOCK)
        if d not in wides:
            for i in range(2):
                panels[0][i, at] = got[i]
            continue

        @pl.when(partner == seq_index - 1)
        def _():
            for i in range(2):
                halo[i, :BLOCK] = got[i, :BLOCK]
                near[i, :REST] = got[i, BLOCK:]
                near[i, REST : 2 * BLOCK] = coarse(got[i, :BLOCK], halo_scratch)

        @pl.when(partner == seq_index + 1)
        def _():
            for i in range(2):
                halo[i, BLOCK:] = got[i, :BLOCK]
                near[i, 2 * BLOCK : 2 * BLOCK + EDGE] = coarse(got[i, :BLOCK], halo_scratch)
                near[i, 2 * BLOCK + EDGE :] = got[i, BLOCK:]

        @pl.when((partner != seq_index + 1) & (partner != seq_index - 1))
        def _():
            for i in range(2):
                panels[0][i, at] = got[i, :BLOCK]

    panel_scratch = pool()
    for level in range(3, top_level + 1):
        for i in range(2):
            panels[level - 2][i] = coarse(panels[level - 3][i], panel_scratch)

    def window(ref, lo, hi, valid):
        return ref[0, rows_of(lo, hi - lo)], ref[1, rows_of(lo, hi - lo)], valid, (lo, hi)

    level_pieces = [
        [[window(halo, 0, 1, has_prev)], [window(halo, 1, 2, has_next)]],
        [
            [window(near, 0, 1, has_prev), window(near, 2, 4, has_next)],
            [window(near, 0, 2, has_prev), window(near, 3, 4, has_next)],
        ],
    ]
    for level in range(2, top_level + 1):
        pieces = []
        for index, valid in slots_of(seq_index >> (level - 2), seq_count >> (level - 2)):
            at = pl.ds(pl.multiple_of(index * BLOCK, BLOCK), BLOCK)
            panel = panels[level - 2]
            pieces.append((panel[0, at], panel[1, at], valid, at))
        level_pieces.append([pieces])
    level_queries = [[held[0, rows_of(0)], held[0, rows_of(blocks - 1)]]]
    for level in range(1, top_level + 1):
        query = query_refs[level - 1][...]
        step = query.shape[0] // len(level_pieces[level])
        level_queries.append(
            [query[a * step : (a + 1) * step] for a in range(len(level_pieces[level]))]
        )

    def unit(query, pieces, before=None):
        scores = []
        for key, _, valid, _ in pieces:
            score = nt(query, key) * factor
            scores.append(score if valid is None else jnp.where(valid, score, MASKED))
        peak = functools.reduce(jnp.maximum, [row_max(score) for score in scores])
        if before is not None:
            peak = jnp.maximum(peak, before[0])
        exps = [jnp.exp2(score - across(peak, score.shape[1])) for score in scores]
        rounded = [e.astype(BF16) for e in exps]
        total = total_of([row_sum(e) for e in exps])
        sums = total_of([nn(r, piece[1]) for r, piece in zip(rounded, pieces)])
        if before is not None:
            keep = jnp.exp2(before[0] - peak)
            total, sums = total + keep * before[1], sums + keep * before[2]
        return peak, total, sums, exps, rounded

    def before_of(block):
        return [stats[w, rows_of(block)] for w in range(3)]

    level_units = [
        [
            unit(query, pieces, before_of(block))
            for query, pieces, block in zip(level_queries[0], level_pieces[0], (0, blocks - 1))
        ]
    ]
    for level in range(1, top_level + 1):
        level_units.append(
            [unit(q, pieces) for q, pieces in zip(level_queries[level], level_pieces[level])]
        )

    def stacked(level, which):
        units = [u[which] for u in level_units[level]]
        if level == 0:
            units = [units[0], stats[which, rows_of(1, blocks - 2)], units[1]]
        return jnp.concatenate(units, axis=0)

    run = [stacked(top_level, w) for w in range(3)]
    own_factors, run_factors = [None] * top_level, [None] * top_level
    for level in range(top_level - 1, -1, -1):
        up_peak, up_total, up_sums = [spread(x, pool()) for x in run]
        peak, total, sums = [stacked(level, w) for w in range(3)]
        both = jnp.maximum(peak, up_peak)
        own = jnp.exp2(peak - both)
        up = 2.0 * jnp.exp2(up_peak - both)
        own_factors[level], run_factors[level] = own, up
        run = [both, own * total + up * up_total, own * sums + up * up_sums]

    inverse = 1.0 / run[1]
    attended = run[2] * inverse
    attended_ref[...] = attended.astype(BF16)

    cot = held[3].astype(F32)
    grad, shift = cot * inverse, row_sum(cot * attended) * inverse
    level_grads = []
    for level in range(top_level):
        level_grads.append((own_factors[level] * grad, own_factors[level] * shift))
        grad = pair_sum(run_factors[level] * grad, pool())
        shift = pair_sum(run_factors[level] * shift, pool())
    level_grads.append((grad, shift))
    back[0] = stacked(0, 0)
    back[1], back[2] = level_grads[0]

    for panel_grad in panel_grads:
        panel_grad[...] = jnp.zeros(panel_grad.shape, F32)

    grad_queries = []
    parts_of = [[[[] for _ in range(4)] for _ in range(2)] for _ in range(2)]
    for level in range(top_level, -1, -1):
        grad, shift = level_grads[level]
        step = level_queries[level][0].shape[0]
        level_parts = []
        for a, (query, pieces) in enumerate(zip(level_queries[level], level_pieces[level])):
            at = a if level > 0 else a * (blocks - 1)
            cut = slice(at * step, (at + 1) * step)
            grad_rounded = grad[cut].astype(BF16)
            grad_scaled = (grad[cut] * scale).astype(BF16)
            shift_scaled = shift[cut] * scale
            exps, rounded = level_units[level][a][3:]
            query_parts = []
            for piece, e, r in zip(pieces, exps, rounded):
                key, value, _, where = piece
                score_grad = nt(grad_scaled, value) - across(shift_scaled, e.shape[1])
                score_grad = (e * score_grad).astype(BF16)
                query_parts.append(nn(score_grad, key))
                outs = tn(score_grad, query), tn(r, grad_rounded)
                for i in range(2):
                    if level >= 2:
                        panel_grads[level - 2][i, where] += outs[i]
                        continue
                    lo, hi = where
                    for b in range(lo, hi):
                        parts_of[level][i][b].append(outs[i][rows_of(b - lo)])
            level_parts.append(total_of(query_parts))
        grad_queries.append(level_parts)

    run_grad = grad_queries[0][0]
    for level_parts in grad_queries[1:-1]:
        run_grad = jnp.concatenate(level_parts, axis=0) + 0.5 * spread(run_grad, pool())
    partial_ref[...] = 0.5 * spread(run_grad, pool())
    for a, block in enumerate((0, blocks - 1)):
        partial_ref[rows_of(block)] += grad_queries[-1][a]

    for level in range(top_level, 2, -1):
        for i in range(2):
            panel_grads[level - 3][i] += 0.5 * spread(panel_grads[level - 2][i], panel_scratch)

    near_grads = [[total_of(p) for p in parts_of[1][i]] for i in range(2)]
    halo_grads = [[total_of(p) for p in parts_of[0][i][:2]] for i in range(2)]
    to_prev = [halo_grads[i][0] + 0.5 * spread(near_grads[i][1][EDGE:], pool()) for i in range(2)]
    to_next = [halo_grads[i][1] + 0.5 * spread(near_grads[i][2][:EDGE], pool()) for i in range(2)]
    for d in range(1, seq_count):
        out = sends[d]
        partner = seq_index ^ d
        at = pl.ds(pl.multiple_of(partner * BLOCK, BLOCK), BLOCK)
        if d not in wides:
            for i in range(2):
                out[i] = panel_grads[0][i, at].astype(BF16)
            continue

        @pl.when(partner == seq_index - 1)
        def _():
            for i in range(2):
                out[i, :BLOCK] = to_prev[i].astype(BF16)
                out[i, BLOCK : 2 * BLOCK] = near_grads[i][0].astype(BF16)
                out[i, 2 * BLOCK :] = near_grads[i][1][:EDGE].astype(BF16)

        @pl.when(partner == seq_index + 1)
        def _():
            for i in range(2):
                out[i, :BLOCK] = to_next[i].astype(BF16)
                out[i, BLOCK : BLOCK + EDGE] = near_grads[i][2][EDGE:].astype(BF16)
                out[i, BLOCK + EDGE :] = near_grads[i][3].astype(BF16)

        @pl.when((partner != seq_index + 1) & (partner != seq_index - 1))
        def _():
            for i in range(2):
                out[i, :BLOCK] = panel_grads[0][i, at].astype(BF16)
                out[i, BLOCK:] = jnp.zeros((REST, width), BF16)


def local_kernel(held, back, partial_ref, grad_query_ref, local_ref):
    blocks, width = held.shape[1] // BLOCK, held.shape[2]
    scale = width ** (-0.5)
    factor = scale * LOG2E
    parts = [[[] for _ in range(blocks)] for _ in range(2)]
    for a in range(blocks):
        lo, hi = own_window(a, blocks)
        window = rows_of(lo, hi - lo)
        query, key, value = held[0, rows_of(a)], held[1, window], held[2, window]
        peak, grad, shift = [back[w, rows_of(a)] for w in range(3)]
        wide = key.shape[0]
        exps = jnp.exp2(nt(query, key) * factor - across(peak, wide))
        score_grad = nt((grad * scale).astype(BF16), value) - across(shift * scale, wide)
        score_grad = (exps * score_grad).astype(BF16)
        grad_query_ref[rows_of(a)] = (nn(score_grad, key) + partial_ref[rows_of(a)]).astype(BF16)
        outs = tn(score_grad, query), tn(exps.astype(BF16), grad.astype(BF16))
        for i in range(2):
            for b in range(lo, hi):
                parts[i][b].append(outs[i][rows_of(b - lo)])
    for i in range(2):
        for b in range(blocks):
            local_ref[i, rows_of(b)] = total_of(parts[i][b])


def combine_kernel(seq_count, head_count, grad_query_ref, local_ref, *refs):
    received, refs = refs[: seq_count - 1], refs[seq_count - 1 :]
    received = dict(zip(seq_order(seq_count), received))
    outs, refs = refs[:head_count], refs[head_count:]
    outs = dict(zip([0] + head_order(head_count), outs))
    total, level_1, level_2 = refs
    seq_index, head_index = lax.axis_index("seq"), lax.axis_index("head")
    wides = wide_distances(seq_count)
    rows, width = local_ref.shape[1:]
    share = rows // head_count

    level_1[...] = jnp.zeros(level_1.shape, F32)
    level_2[...] = jnp.zeros(level_2.shape, F32)
    for i in range(2):
        total[i] = local_ref[i]
    for d in range(1, seq_count):
        got = received[d]
        partner = seq_index ^ d
        if d not in wides:
            for i in range(2):
                level_2[i] += got[i].astype(F32)
            continue

        @pl.when(partner == seq_index - 1)
        def _():
            for i in range(2):
                total[i, :BLOCK] += got[i, :BLOCK].astype(F32)
                level_1[i, EDGE:] += got[i, BLOCK:].astype(F32)

        @pl.when(partner == seq_index + 1)
        def _():
            for i in range(2):
                total[i, rows - BLOCK :] += got[i, :BLOCK].astype(F32)
                level_1[i, :REST] += got[i, BLOCK:].astype(F32)

        @pl.when((partner != seq_index + 1) & (partner != seq_index - 1))
        def _():
            for i in range(2):
                level_2[i] += got[i, :BLOCK].astype(F32)

    for i in range(2):
        half = level_2[i] * 0.5
        for phase in range(2):
            level_1[i, pl.ds(phase, half.shape[0], stride=2), :] += half
        half = level_1[i] * 0.5
        for phase in range(2):
            total[i, pl.ds(phase, half.shape[0], stride=2), :] += half
    for d in range(head_count):
        at = pl.ds(pl.multiple_of((head_index ^ d) * share, share), share)
        outs[d][0] = grad_query_ref[at, :]
        outs[d][1] = total[0, at].astype(BF16)
        outs[d][2] = total[1, at].astype(BF16)


def place_kernel(head_count, *refs):
    parts, outs = refs[:head_count], refs[head_count:]
    parts = dict(zip([0] + head_order(head_count), parts))
    head_index = lax.axis_index("head")
    width = parts[0].shape[-1]
    for d in range(head_count):
        at = pl.ds(pl.multiple_of((head_index ^ d) * width, width), width)
        for i in range(3):
            outs[i][:, at] = parts[d][i]


def call(kernel, outs, scratch, args, space=pltpu.VMEM, flops=0):
    return pl.pallas_call(
        kernel,
        out_shape=outs,
        in_specs=[pl.BlockSpec(memory_space=space)] * len(args),
        out_specs=[VMEM] * len(outs),
        scratch_shapes=scratch,
        compiler_params=pltpu.CompilerParams(vmem_limit_bytes=48 * 2**20),
        cost_estimate=pl.CostEstimate(flops=flops, bytes_accessed=2**20, transcendentals=0),
    )(*args)


def swap_all(arrays, axis, distances):
    size = lax.axis_size(axis)
    return [
        lax.ppermute(x, axis, [(i, i ^ d) for i in range(size)]) for x, d in zip(arrays, distances)
    ]


def per_device(queries, keys, values, grad_out):
    seq_count, head_count = lax.axis_size("seq"), lax.axis_size("head")
    rows, width = queries.shape
    assert rows == 4 * BLOCK and width == BLOCK
    fine_blocks = rows * seq_count // BLOCK
    top_level = (fine_blocks // 4).bit_length() - 1
    wides = wide_distances(seq_count)
    distances = seq_order(seq_count)

    def shape(*dims, dtype=BF16):
        return jax.ShapeDtypeStruct(dims, dtype)

    def f32(*dims):
        return pltpu.VMEM(dims, F32)

    payloads = [shape(2, BLOCK + REST if d in wides else BLOCK, width) for d in distances]
    arguments = [
        pltpu.with_memory_space_constraint(x, pltpu.HBM) for x in (queries, keys, values, grad_out)
    ]
    held, *sends = call(
        functools.partial(prep_kernel, seq_count),
        [shape(4, rows, width)] + payloads,
        [f32(rows, width), f32(rows // 2, width)] * 2 + [pltpu.SemaphoreType.DMA((4,))],
        arguments,
        pltpu.HBM,
    )
    received = swap_all(sends, "seq", distances)

    unit_flops = 2 * BLOCK * BLOCK * width
    stats, *level_queries = call(
        fine_kernel,
        [shape(3, rows, width, dtype=F32)]
        + [shape(rows >> level, width) for level in range(1, top_level + 1)],
        [f32(rows >> level, width) for level in range(top_level)],
        (held,),
        flops=20 * unit_flops,
    )

    panel_rows = [(seq_count >> (level - 2)) * BLOCK for level in range(2, top_level + 1)]
    pools = [f32(BLOCK, width), f32(max(seq_count * BLOCK, rows), width)]
    for level in range(top_level - 1, -1, -1):
        pools += [f32(rows >> level, width)] * 3
    for level in range(top_level):
        pools += [f32(rows >> level, width)] * 2
    for level in range(top_level - 1, -1, -1):
        pools += [f32(rows >> level, width)]
    pools += [f32(BLOCK, width)] * 4
    main = call(
        functools.partial(main_kernel, seq_count, top_level),
        [shape(rows, width)]
        + payloads
        + [shape(3, rows, width, dtype=F32), shape(rows, width, dtype=F32)],
        [pltpu.VMEM((2, 2 * BLOCK, width), BF16), pltpu.VMEM((2, 4 * BLOCK, width), BF16)]
        + [pltpu.VMEM((2, r, width), BF16) for r in panel_rows]
        + [f32(2, r, width) for r in panel_rows]
        + pools,
        (held, stats, *level_queries, *received),
        flops=70 * unit_flops,
    )
    attended, sends, back, partial = main[0], main[1:seq_count], main[-2], main[-1]
    returned = swap_all(sends, "seq", distances)

    grad_query, local = call(
        local_kernel,
        [shape(rows, width), shape(2, rows, width, dtype=F32)],
        [],
        (held, back, partial),
        flops=50 * unit_flops,
    )

    share = rows // head_count
    parts = call(
        functools.partial(combine_kernel, seq_count, head_count),
        [shape(3, share, width)] * head_count,
        [f32(2, rows, width), f32(2, rows // 2, width), f32(2, rows // 4, width)],
        (grad_query, local, *returned),
    )
    parts = [parts[0]] + swap_all(parts[1:], "head", head_order(head_count))
    grads = call(
        functools.partial(place_kernel, head_count),
        [shape(share, head_count * width)] * 3,
        [],
        parts,
    )
    return (attended, *grads)


def solution(mesh):
    return jax.shard_map(
        per_device,
        mesh=mesh,
        in_specs=(P("seq", "head"),) * 4,
        out_specs=(P("seq", "head"),) + (P(("seq", "head"), None),) * 3,
        check_vma=False,
    )
```

```python
import functools

import jax
import jax.numpy as jnp
from jax import lax
from jax.experimental import pallas as pl
from jax.experimental.pallas import tpu as pltpu
from jax.sharding import PartitionSpec as P

BLOCK = 128
EDGE = BLOCK // 2
REST = 2 * BLOCK - EDGE
MASKED = -1e30
LOG2E = 1.4426950408889634
F32 = jnp.float32
BF16 = jnp.bfloat16
VMEM = pl.BlockSpec(memory_space=pltpu.VMEM)


def nt(a, b):
    return lax.dot_general(a, b, (((1,), (1,)), ((), ())), preferred_element_type=F32)


def nn(a, b):
    return lax.dot_general(a, b, (((1,), (0,)), ((), ())), preferred_element_type=F32)


def tn(a, b):
    return lax.dot_general(a, b, (((0,), (0,)), ((), ())), preferred_element_type=F32)


def pair_sum(x, scratch):
    rows = x.shape[0]
    scratch[:rows] = x
    return scratch[pl.ds(0, rows // 2, stride=2), :] + scratch[pl.ds(1, rows // 2, stride=2), :]


def coarse(x, scratch):
    return (pair_sum(x.astype(F32), scratch) * 0.5).astype(BF16)


def spread(x, scratch):
    rows = x.shape[0]
    scratch[pl.ds(0, rows, stride=2), :] = x
    scratch[pl.ds(1, rows, stride=2), :] = x
    return scratch[: 2 * rows]


def wide_distances(seq_count):
    return sorted({i ^ (i + 1) for i in range(seq_count - 1)})


def seq_order(seq_count):
    wides = wide_distances(seq_count)
    return wides[::-1] + [d for d in range(1, seq_count) if d not in wides]


def head_order(head_count):
    return [d for d in range(4, head_count)] + [d for d in (2, 3, 1) if d < head_count]


def prep_kernel(seq_count, *refs):
    sources, refs = refs[:4], refs[4:]
    held, refs = refs[0], refs[1:]
    sends, scratches, sems = refs[: seq_count - 1], refs[seq_count - 1 : -1], refs[-1]
    sends = dict(zip(seq_order(seq_count), sends))
    seq_index = lax.axis_index("seq")
    wides = wide_distances(seq_count)
    rows = held.shape[1]
    copies = [
        pltpu.make_async_copy(source, held.at[i], sems.at[i]) for i, source in enumerate(sources)
    ]
    for i in (1, 2, 0, 3):
        copies[i].start()
    for i in range(2):
        copies[1 + i].wait()
        ref = held.at[1 + i]
        level_1 = coarse(ref[...], scratches[2 * i])
        level_2 = coarse(level_1, scratches[2 * i + 1])
        for d in range(1, seq_count):
            out = sends[d]
            partner = seq_index ^ d
            if d not in wides:
                out[i] = level_2
                continue

            @pl.when(partner == seq_index + 1)
            def _():
                out[i, :BLOCK] = ref[rows - BLOCK :]
                out[i, BLOCK:] = level_1[:REST]

            @pl.when(partner == seq_index - 1)
            def _():
                out[i, :BLOCK] = ref[:BLOCK]
                out[i, BLOCK:] = level_1[EDGE:]

            @pl.when((partner != seq_index + 1) & (partner != seq_index - 1))
            def _():
                out[i, :BLOCK] = level_2
                out[i, BLOCK:] = level_1[:REST]

    copies[0].wait()
    copies[3].wait()


def slots_of(block, block_count):
    parent, odd = block // 2, block % 2
    if block_count == 4:
        first = parent == 0
        return [
            (jnp.where(first, 3, 0), None),
            (jnp.where(first, 2, 1), jnp.where(first, odd == 0, odd == 1)),
        ]
    near = jnp.where(odd == 0, 2 * parent + 2, 2 * parent - 1)
    raw = [2 * parent - 2, near, 2 * parent + 3]
    return [(jnp.clip(j, 0, block_count - 1), (j >= 0) & (j < block_count)) for j in raw]


def across(x, width):
    return jnp.concatenate([x] * (width // x.shape[1]), axis=1)


def lanes(column):
    return jnp.broadcast_to(column, (column.shape[0], BLOCK))


def row_max(x):
    return lanes(jnp.max(x, axis=-1, keepdims=True))


def row_sum(x):
    return lanes(jnp.sum(x, axis=-1, keepdims=True))


def total_of(parts):
    return functools.reduce(jnp.add, parts)


def rows_of(block, count=1):
    return slice(block * BLOCK, (block + count) * BLOCK)


def own_window(a, blocks):
    return max(a - 1, 0), min(a + 2, blocks)


def fine_kernel(held, stats, *refs):
    levels = len(refs) // 2
    blocks, width = held.shape[1] // BLOCK, held.shape[2]
    factor = width ** (-0.5) * LOG2E
    for a in range(blocks):
        lo, hi = own_window(a, blocks)
        window = rows_of(lo, hi - lo)
        scores = nt(held[0, rows_of(a)], held[1, window]) * factor
        peak = row_max(scores)
        exps = jnp.exp2(scores - across(peak, scores.shape[1]))
        stats[0, rows_of(a)] = peak
        stats[1, rows_of(a)] = row_sum(exps)
        stats[2, rows_of(a)] = nn(exps.astype(BF16), held[2, window])
    query = held[0]
    for level in range(levels):
        query = coarse(query, refs[levels + level])
        refs[level][...] = query


def main_kernel(seq_count, top_level, *refs):
    refs = list(refs)

    def take(count):
        taken = refs[:count]
        del refs[:count]
        return taken

    held, stats = take(2)
    query_refs = take(top_level)
    received = dict(zip(seq_order(seq_count), take(seq_count - 1)))
    (attended_ref,) = take(1)
    sends = dict(zip(seq_order(seq_count), take(seq_count - 1)))
    back, partial_ref = take(2)
    halo, near = take(2)
    panels = take(top_level - 1)
    panel_grads = take(top_level - 1)
    pools = refs

    def pool():
        return pools.pop(0)

    seq_index = lax.axis_index("seq")
    wides = wide_distances(seq_count)
    rows, width = held.shape[1:]
    blocks = rows // BLOCK
    scale = width ** (-0.5)
    factor = scale * LOG2E
    has_prev, has_next = seq_index > 0, seq_index < seq_count - 1

    for panel in panels:
        panel[...] = jnp.zeros(panel.shape, BF16)

    @pl.when(seq_index == 0)
    def _():
        halo[:, :BLOCK] = jnp.zeros((2, BLOCK, width), BF16)
        near[:, : 2 * BLOCK] = jnp.zeros((2, 2 * BLOCK, width), BF16)

    @pl.when(seq_index == seq_count - 1)
    def _():
        halo[:, BLOCK:] = jnp.zeros((2, BLOCK, width), BF16)
        near[:, 2 * BLOCK :] = jnp.zeros((2, 2 * BLOCK, width), BF16)

    halo_scratch = pool()
    for d in range(1, seq_count):
        got = received[d]
        partner = seq_index ^ d
        at = pl.ds(pl.multiple_of(partner * BLOCK, BLOCK), BLOCK)
        if d not in wides:
            for i in range(2):
                panels[0][i, at] = got[i]
            continue

        @pl.when(partner == seq_index - 1)
        def _():
            for i in range(2):
                halo[i, :BLOCK] = got[i, :BLOCK]
                near[i, :REST] = got[i, BLOCK:]
                near[i, REST : 2 * BLOCK] = coarse(got[i, :BLOCK], halo_scratch)

        @pl.when(partner == seq_index + 1)
        def _():
            for i in range(2):
                halo[i, BLOCK:] = got[i, :BLOCK]
                near[i, 2 * BLOCK : 2 * BLOCK + EDGE] = coarse(got[i, :BLOCK], halo_scratch)
                near[i, 2 * BLOCK + EDGE :] = got[i, BLOCK:]

        @pl.when((partner != seq_index + 1) & (partner != seq_index - 1))
        def _():
            for i in range(2):
                panels[0][i, at] = got[i, :BLOCK]

    panel_scratch = pool()
    for level in range(3, top_level + 1):
        for i in range(2):
            panels[level - 2][i] = coarse(panels[level - 3][i], panel_scratch)

    def window(ref, lo, hi, valid):
        return ref[0, rows_of(lo, hi - lo)], ref[1, rows_of(lo, hi - lo)], valid, (lo, hi)

    level_pieces = [
        [[window(halo, 0, 1, has_prev)], [window(halo, 1, 2, has_next)]],
        [
            [window(near, 0, 1, has_prev), window(near, 2, 4, has_next)],
            [window(near, 0, 2, has_prev), window(near, 3, 4, has_next)],
        ],
    ]
    for level in range(2, top_level + 1):
        pieces = []
        for index, valid in slots_of(seq_index >> (level - 2), seq_count >> (level - 2)):
            at = pl.ds(pl.multiple_of(index * BLOCK, BLOCK), BLOCK)
            panel = panels[level - 2]
            pieces.append((panel[0, at], panel[1, at], valid, at))
        level_pieces.append([pieces])
    level_queries = [[held[0, rows_of(0)], held[0, rows_of(blocks - 1)]]]
    for level in range(1, top_level + 1):
        query = query_refs[level - 1][...]
        step = query.shape[0] // len(level_pieces[level])
        level_queries.append(
            [query[a * step : (a + 1) * step] for a in range(len(level_pieces[level]))]
        )

    def unit(query, pieces, before=None):
        scores = []
        for key, _, valid, _ in pieces:
            score = nt(query, key) * factor
            scores.append(score if valid is None else jnp.where(valid, score, MASKED))
        peak = functools.reduce(jnp.maximum, [row_max(score) for score in scores])
        if before is not None:
            peak = jnp.maximum(peak, before[0])
        exps = [jnp.exp2(score - across(peak, score.shape[1])) for score in scores]
        rounded = [e.astype(BF16) for e in exps]
        ones = jnp.ones((BLOCK, width), BF16)
        both = []
        for r, piece in zip(rounded, pieces):
            count = piece[1].shape[0] // BLOCK
            both.append(nn(r, jnp.concatenate([piece[1], jnp.concatenate([ones] * count, axis=0)], axis=1)))
        both = total_of(both)
        sums, total = both[:, :width], both[:, width:]
        if before is not None:
            keep = jnp.exp2(before[0] - peak)
            total, sums = total + keep * before[1], sums + keep * before[2]
        return peak, total, sums, exps, rounded

    def before_of(block):
        return [stats[w, rows_of(block)] for w in range(3)]

    level_units = [
        [
            unit(query, pieces, before_of(block))
            for query, pieces, block in zip(level_queries[0], level_pieces[0], (0, blocks - 1))
        ]
    ]
    for level in range(1, top_level + 1):
        level_units.append(
            [unit(q, pieces) for q, pieces in zip(level_queries[level], level_pieces[level])]
        )

    def stacked(level, which):
        units = [u[which] for u in level_units[level]]
        if level == 0:
            units = [units[0], stats[which, rows_of(1, blocks - 2)], units[1]]
        return jnp.concatenate(units, axis=0)

    run = [stacked(top_level, w) for w in range(3)]
    own_factors, run_factors = [None] * top_level, [None] * top_level
    for level in range(top_level - 1, -1, -1):
        up_peak, up_total, up_sums = [spread(x, pool()) for x in run]
        peak, total, sums = [stacked(level, w) for w in range(3)]
        both = jnp.maximum(peak, up_peak)
        own = jnp.exp2(peak - both)
        up = 2.0 * jnp.exp2(up_peak - both)
        own_factors[level], run_factors[level] = own, up
        run = [both, own * total + up * up_total, own * sums + up * up_sums]

    inverse = 1.0 / run[1]
    attended = run[2] * inverse
    attended_ref[...] = attended.astype(BF16)

    cot = held[3].astype(F32)
    grad, shift = cot * inverse, row_sum(cot * attended) * inverse
    level_grads = []
    for level in range(top_level):
        level_grads.append((own_factors[level] * grad, own_factors[level] * shift))
        grad = pair_sum(run_factors[level] * grad, pool())
        shift = pair_sum(run_factors[level] * shift, pool())
    level_grads.append((grad, shift))
    back[0] = stacked(0, 0)
    back[1], back[2] = level_grads[0]

    for panel_grad in panel_grads:
        panel_grad[...] = jnp.zeros(panel_grad.shape, F32)

    grad_queries = []
    parts_of = [[[[] for _ in range(4)] for _ in range(2)] for _ in range(2)]
    for level in range(top_level, -1, -1):
        grad, shift = level_grads[level]
        step = level_queries[level][0].shape[0]
        level_parts = []
        for a, (query, pieces) in enumerate(zip(level_queries[level], level_pieces[level])):
            at = a if level > 0 else a * (blocks - 1)
            cut = slice(at * step, (at + 1) * step)
            grad_rounded = grad[cut].astype(BF16)
            grad_scaled = (grad[cut] * scale).astype(BF16)
            shift_scaled = shift[cut] * scale
            exps, rounded = level_units[level][a][3:]
            query_parts = []
            for piece, e, r in zip(pieces, exps, rounded):
                key, value, _, where = piece
                score_grad = nt(grad_scaled, value) - across(shift_scaled, e.shape[1])
                score_grad = (e * score_grad).astype(BF16)
                query_parts.append(nn(score_grad, key))
                outs = tn(score_grad, query), tn(r, grad_rounded)
                for i in range(2):
                    if level >= 2:
                        panel_grads[level - 2][i, where] += outs[i]
                        continue
                    lo, hi = where
                    for b in range(lo, hi):
                        parts_of[level][i][b].append(outs[i][rows_of(b - lo)])
            level_parts.append(total_of(query_parts))
        grad_queries.append(level_parts)

    run_grad = grad_queries[0][0]
    for level_parts in grad_queries[1:-1]:
        run_grad = jnp.concatenate(level_parts, axis=0) + 0.5 * spread(run_grad, pool())
    partial_ref[...] = 0.5 * spread(run_grad, pool())
    for a, block in enumerate((0, blocks - 1)):
        partial_ref[rows_of(block)] += grad_queries[-1][a]

    for level in range(top_level, 2, -1):
        for i in range(2):
            panel_grads[level - 3][i] += 0.5 * spread(panel_grads[level - 2][i], panel_scratch)

    near_grads = [[total_of(p) for p in parts_of[1][i]] for i in range(2)]
    halo_grads = [[total_of(p) for p in parts_of[0][i][:2]] for i in range(2)]
    to_prev = [halo_grads[i][0] + 0.5 * spread(near_grads[i][1][EDGE:], pool()) for i in range(2)]
    to_next = [halo_grads[i][1] + 0.5 * spread(near_grads[i][2][:EDGE], pool()) for i in range(2)]
    for d in range(1, seq_count):
        out = sends[d]
        partner = seq_index ^ d
        at = pl.ds(pl.multiple_of(partner * BLOCK, BLOCK), BLOCK)
        if d not in wides:
            for i in range(2):
                out[i] = panel_grads[0][i, at].astype(BF16)
            continue

        @pl.when(partner == seq_index - 1)
        def _():
            for i in range(2):
                out[i, :BLOCK] = to_prev[i].astype(BF16)
                out[i, BLOCK : 2 * BLOCK] = near_grads[i][0].astype(BF16)
                out[i, 2 * BLOCK :] = near_grads[i][1][:EDGE].astype(BF16)

        @pl.when(partner == seq_index + 1)
        def _():
            for i in range(2):
                out[i, :BLOCK] = to_next[i].astype(BF16)
                out[i, BLOCK : BLOCK + EDGE] = near_grads[i][2][EDGE:].astype(BF16)
                out[i, BLOCK + EDGE :] = near_grads[i][3].astype(BF16)

        @pl.when((partner != seq_index + 1) & (partner != seq_index - 1))
        def _():
            for i in range(2):
                out[i, :BLOCK] = panel_grads[0][i, at].astype(BF16)
                out[i, BLOCK:] = jnp.zeros((REST, width), BF16)


def local_kernel(held, back, partial_ref, merged, attended_ref, grad_query_ref, local_ref):
    attended_ref[...] = merged[...]
    blocks, width = held.shape[1] // BLOCK, held.shape[2]
    scale = width ** (-0.5)
    factor = scale * LOG2E
    parts = [[[] for _ in range(blocks)] for _ in range(2)]
    for a in range(blocks):
        lo, hi = own_window(a, blocks)
        window = rows_of(lo, hi - lo)
        query, key, value = held[0, rows_of(a)], held[1, window], held[2, window]
        peak, grad, shift = [back[w, rows_of(a)] for w in range(3)]
        wide = key.shape[0]
        exps = jnp.exp2(nt(query, key) * factor - across(peak, wide))
        score_grad = nt((grad * scale).astype(BF16), value) - across(shift * scale, wide)
        score_grad = (exps * score_grad).astype(BF16)
        grad_query_ref[rows_of(a)] = (nn(score_grad, key) + partial_ref[rows_of(a)]).astype(BF16)
        outs = tn(score_grad, query), tn(exps.astype(BF16), grad.astype(BF16))
        for i in range(2):
            for b in range(lo, hi):
                parts[i][b].append(outs[i][rows_of(b - lo)])
    for i in range(2):
        for b in range(blocks):
            local_ref[i, rows_of(b)] = total_of(parts[i][b])


def combine_kernel(seq_count, head_count, grad_query_ref, local_ref, *refs):
    received, refs = refs[: seq_count - 1], refs[seq_count - 1 :]
    received = dict(zip(seq_order(seq_count), received))
    outs, refs = refs[:head_count], refs[head_count:]
    outs = dict(zip([0] + head_order(head_count), outs))
    total, level_1, level_2 = refs
    seq_index, head_index = lax.axis_index("seq"), lax.axis_index("head")
    wides = wide_distances(seq_count)
    rows, width = local_ref.shape[1:]
    share = rows // head_count

    level_1[...] = jnp.zeros(level_1.shape, F32)
    level_2[...] = jnp.zeros(level_2.shape, F32)
    for i in range(2):
        total[i] = local_ref[i]
    for d in range(1, seq_count):
        got = received[d]
        partner = seq_index ^ d
        if d not in wides:
            for i in range(2):
                level_2[i] += got[i].astype(F32)
            continue

        @pl.when(partner == seq_index - 1)
        def _():
            for i in range(2):
                total[i, :BLOCK] += got[i, :BLOCK].astype(F32)
                level_1[i, EDGE:] += got[i, BLOCK:].astype(F32)

        @pl.when(partner == seq_index + 1)
        def _():
            for i in range(2):
                total[i, rows - BLOCK :] += got[i, :BLOCK].astype(F32)
                level_1[i, :REST] += got[i, BLOCK:].astype(F32)

        @pl.when((partner != seq_index + 1) & (partner != seq_index - 1))
        def _():
            for i in range(2):
                level_2[i] += got[i, :BLOCK].astype(F32)

    for i in range(2):
        half = level_2[i] * 0.5
        for phase in range(2):
            level_1[i, pl.ds(phase, half.shape[0], stride=2), :] += half
        half = level_1[i] * 0.5
        for phase in range(2):
            total[i, pl.ds(phase, half.shape[0], stride=2), :] += half
    for d in range(head_count):
        at = pl.ds(pl.multiple_of((head_index ^ d) * share, share), share)
        outs[d][0] = grad_query_ref[at, :]
        outs[d][1] = total[0, at].astype(BF16)
        outs[d][2] = total[1, at].astype(BF16)


def place_kernel(head_count, *refs):
    parts, outs = refs[:head_count], refs[head_count:]
    parts = dict(zip([0] + head_order(head_count), parts))
    head_index = lax.axis_index("head")
    width = parts[0].shape[-1]
    for d in range(head_count):
        at = pl.ds(pl.multiple_of((head_index ^ d) * width, width), width)
        for i in range(3):
            outs[i][:, at] = parts[d][i]


def call(kernel, outs, scratch, args, space=pltpu.VMEM, flops=0):
    return pl.pallas_call(
        kernel,
        out_shape=outs,
        in_specs=[pl.BlockSpec(memory_space=space)] * len(args),
        out_specs=[VMEM] * len(outs),
        scratch_shapes=scratch,
        compiler_params=pltpu.CompilerParams(vmem_limit_bytes=48 * 2**20),
        cost_estimate=pl.CostEstimate(flops=flops, bytes_accessed=2**20, transcendentals=0),
    )(*args)


def swap_all(arrays, axis, distances):
    size = lax.axis_size(axis)
    return [
        lax.ppermute(x, axis, [(i, i ^ d) for i in range(size)]) for x, d in zip(arrays, distances)
    ]


def per_device(queries, keys, values, grad_out):
    seq_count, head_count = lax.axis_size("seq"), lax.axis_size("head")
    rows, width = queries.shape
    assert rows == 4 * BLOCK and width == BLOCK
    fine_blocks = rows * seq_count // BLOCK
    top_level = (fine_blocks // 4).bit_length() - 1
    wides = wide_distances(seq_count)
    distances = seq_order(seq_count)

    def shape(*dims, dtype=BF16):
        return jax.ShapeDtypeStruct(dims, dtype)

    def f32(*dims):
        return pltpu.VMEM(dims, F32)

    payloads = [shape(2, BLOCK + REST if d in wides else BLOCK, width) for d in distances]
    arguments = [
        pltpu.with_memory_space_constraint(x, pltpu.HBM) for x in (queries, keys, values, grad_out)
    ]
    held, *sends = call(
        functools.partial(prep_kernel, seq_count),
        [shape(4, rows, width)] + payloads,
        [f32(rows, width), f32(rows // 2, width)] * 2 + [pltpu.SemaphoreType.DMA((4,))],
        arguments,
        pltpu.HBM,
    )
    received = swap_all(sends, "seq", distances)

    unit_flops = 2 * BLOCK * BLOCK * width
    stats, *level_queries = call(
        fine_kernel,
        [shape(3, rows, width, dtype=F32)]
        + [shape(rows >> level, width) for level in range(1, top_level + 1)],
        [f32(rows >> level, width) for level in range(top_level)],
        (held,),
        flops=20 * unit_flops,
    )

    panel_rows = [(seq_count >> (level - 2)) * BLOCK for level in range(2, top_level + 1)]
    pools = [f32(BLOCK, width), f32(max(seq_count * BLOCK, rows), width)]
    for level in range(top_level - 1, -1, -1):
        pools += [f32(rows >> level, width)] * 3
    for level in range(top_level):
        pools += [f32(rows >> level, width)] * 2
    for level in range(top_level - 1, -1, -1):
        pools += [f32(rows >> level, width)]
    pools += [f32(BLOCK, width)] * 4
    main = call(
        functools.partial(main_kernel, seq_count, top_level),
        [shape(rows, width)]
        + payloads
        + [shape(3, rows, width, dtype=F32), shape(rows, width, dtype=F32)],
        [pltpu.VMEM((2, 2 * BLOCK, width), BF16), pltpu.VMEM((2, 4 * BLOCK, width), BF16)]
        + [pltpu.VMEM((2, r, width), BF16) for r in panel_rows]
        + [f32(2, r, width) for r in panel_rows]
        + pools,
        (held, stats, *level_queries, *received),
        flops=70 * unit_flops,
    )
    merged, sends, back, partial = main[0], main[1:seq_count], main[-2], main[-1]
    returned = swap_all(sends, "seq", distances)

    attended, grad_query, local = call(
        local_kernel,
        [shape(rows, width), shape(rows, width), shape(2, rows, width, dtype=F32)],
        [],
        (held, back, partial, merged),
        flops=50 * unit_flops,
    )

    share = rows // head_count
    parts = call(
        functools.partial(combine_kernel, seq_count, head_count),
        [shape(3, share, width)] * head_count,
        [f32(2, rows, width), f32(2, rows // 2, width), f32(2, rows // 4, width)],
        (grad_query, local, *returned),
    )
    parts = [parts[0]] + swap_all(parts[1:], "head", head_order(head_count))
    grads = call(
        functools.partial(place_kernel, head_count),
        [shape(share, head_count * width)] * 3,
        [],
        parts,
    )
    return (attended, *grads)


def solution(mesh):
    return jax.shard_map(
        per_device,
        mesh=mesh,
        in_specs=(P("seq", "head"),) * 4,
        out_specs=(P("seq", "head"),) + (P(("seq", "head"), None),) * 3,
        check_vma=False,
    )
```

```python
import functools

import jax
import jax.numpy as jnp
from jax import lax
from jax.experimental import pallas as pl
from jax.experimental.pallas import tpu as pltpu
from jax.sharding import PartitionSpec as P

BLOCK = 128
EDGE = BLOCK // 2
REST = 2 * BLOCK - EDGE
MASKED = -1e30
LOG2E = 1.4426950408889634
F32 = jnp.float32
BF16 = jnp.bfloat16
VMEM = pl.BlockSpec(memory_space=pltpu.VMEM)


def nt(a, b):
    return lax.dot_general(a, b, (((1,), (1,)), ((), ())), preferred_element_type=F32)


def nn(a, b):
    return lax.dot_general(a, b, (((1,), (0,)), ((), ())), preferred_element_type=F32)


def tn(a, b):
    return lax.dot_general(a, b, (((0,), (0,)), ((), ())), preferred_element_type=F32)


def pair_sum(x, scratch):
    rows = x.shape[0]
    scratch[:rows] = x
    return scratch[pl.ds(0, rows // 2, stride=2), :] + scratch[pl.ds(1, rows // 2, stride=2), :]


def coarse(x, scratch):
    return (pair_sum(x.astype(F32), scratch) * 0.5).astype(BF16)


def spread(x, scratch):
    rows = x.shape[0]
    scratch[pl.ds(0, rows, stride=2), :] = x
    scratch[pl.ds(1, rows, stride=2), :] = x
    return scratch[: 2 * rows]


def wide_distances(seq_count):
    return sorted({i ^ (i + 1) for i in range(seq_count - 1)})


def seq_order(seq_count):
    wides = wide_distances(seq_count)
    return wides[::-1] + [d for d in range(1, seq_count) if d not in wides]


def paired(head_count):
    return list(range(4, head_count, 2))


def head_order(head_count):
    return [d for d in [2, 3] + paired(head_count) + [1] if d < head_count]


def prep_kernel(seq_count, *refs):
    sources, refs = refs[:4], refs[4:]
    held, refs = refs[0], refs[1:]
    sends, scratches, sems = refs[: seq_count - 1], refs[seq_count - 1 : -1], refs[-1]
    sends = dict(zip(seq_order(seq_count), sends))
    seq_index = lax.axis_index("seq")
    wides = wide_distances(seq_count)
    rows = held.shape[1]
    copies = [
        pltpu.make_async_copy(source, held.at[i], sems.at[i]) for i, source in enumerate(sources)
    ]
    for i in (1, 2, 0, 3):
        copies[i].start()
    for i in range(2):
        copies[1 + i].wait()
        ref = held.at[1 + i]
        level_1 = coarse(ref[...], scratches[2 * i])
        level_2 = coarse(level_1, scratches[2 * i + 1])
        for d in range(1, seq_count):
            out = sends[d]
            partner = seq_index ^ d
            if d not in wides:
                out[i] = level_2
                continue

            @pl.when(partner == seq_index + 1)
            def _():
                out[i, :BLOCK] = ref[rows - BLOCK :]
                out[i, BLOCK:] = level_1[:REST]

            @pl.when(partner == seq_index - 1)
            def _():
                out[i, :BLOCK] = ref[:BLOCK]
                out[i, BLOCK:] = level_1[EDGE:]

            @pl.when((partner != seq_index + 1) & (partner != seq_index - 1))
            def _():
                out[i, :BLOCK] = level_2
                out[i, BLOCK:] = level_1[:REST]

    copies[0].wait()
    copies[3].wait()


def slots_of(block, block_count):
    parent, odd = block // 2, block % 2
    if block_count == 4:
        first = parent == 0
        return [
            (jnp.where(first, 3, 0), None),
            (jnp.where(first, 2, 1), jnp.where(first, odd == 0, odd == 1)),
        ]
    near = jnp.where(odd == 0, 2 * parent + 2, 2 * parent - 1)
    raw = [2 * parent - 2, near, 2 * parent + 3]
    return [(jnp.clip(j, 0, block_count - 1), (j >= 0) & (j < block_count)) for j in raw]


def across(x, width):
    return jnp.concatenate([x] * (width // x.shape[1]), axis=1)


def lanes(column):
    return jnp.broadcast_to(column, (column.shape[0], BLOCK))


def row_max(x):
    return lanes(jnp.max(x, axis=-1, keepdims=True))


def row_sum(x):
    return lanes(jnp.sum(x, axis=-1, keepdims=True))


def total_of(parts):
    return functools.reduce(jnp.add, parts)


def rows_of(block, count=1):
    return slice(block * BLOCK, (block + count) * BLOCK)


def own_window(a, blocks):
    return max(a - 1, 0), min(a + 2, blocks)


def fine_kernel(held, stats, *refs):
    levels = len(refs) // 2
    blocks, width = held.shape[1] // BLOCK, held.shape[2]
    factor = width ** (-0.5) * LOG2E
    for a in range(blocks):
        lo, hi = own_window(a, blocks)
        window = rows_of(lo, hi - lo)
        scores = nt(held[0, rows_of(a)], held[1, window]) * factor
        peak = row_max(scores)
        exps = jnp.exp2(scores - across(peak, scores.shape[1]))
        stats[0, rows_of(a)] = peak
        stats[1, rows_of(a)] = row_sum(exps)
        stats[2, rows_of(a)] = nn(exps.astype(BF16), held[2, window])
    query = held[0]
    for level in range(levels):
        query = coarse(query, refs[levels + level])
        refs[level][...] = query


def main_kernel(seq_count, top_level, *refs):
    refs = list(refs)

    def take(count):
        taken = refs[:count]
        del refs[:count]
        return taken

    held, stats = take(2)
    query_refs = take(top_level)
    received = dict(zip(seq_order(seq_count), take(seq_count - 1)))
    (attended_ref,) = take(1)
    sends = dict(zip(seq_order(seq_count), take(seq_count - 1)))
    back, partial_ref = take(2)
    halo, near = take(2)
    panels = take(top_level - 1)
    panel_grads = take(top_level - 1)
    pools = refs

    def pool():
        return pools.pop(0)

    seq_index = lax.axis_index("seq")
    wides = wide_distances(seq_count)
    rows, width = held.shape[1:]
    blocks = rows // BLOCK
    scale = width ** (-0.5)
    factor = scale * LOG2E
    has_prev, has_next = seq_index > 0, seq_index < seq_count - 1

    for panel in panels:
        panel[...] = jnp.zeros(panel.shape, BF16)

    @pl.when(seq_index == 0)
    def _():
        halo[:, :BLOCK] = jnp.zeros((2, BLOCK, width), BF16)
        near[:, : 2 * BLOCK] = jnp.zeros((2, 2 * BLOCK, width), BF16)

    @pl.when(seq_index == seq_count - 1)
    def _():
        halo[:, BLOCK:] = jnp.zeros((2, BLOCK, width), BF16)
        near[:, 2 * BLOCK :] = jnp.zeros((2, 2 * BLOCK, width), BF16)

    halo_scratch = pool()
    for d in range(1, seq_count):
        got = received[d]
        partner = seq_index ^ d
        at = pl.ds(pl.multiple_of(partner * BLOCK, BLOCK), BLOCK)
        if d not in wides:
            for i in range(2):
                panels[0][i, at] = got[i]
            continue

        @pl.when(partner == seq_index - 1)
        def _():
            for i in range(2):
                halo[i, :BLOCK] = got[i, :BLOCK]
                near[i, :REST] = got[i, BLOCK:]
                near[i, REST : 2 * BLOCK] = coarse(got[i, :BLOCK], halo_scratch)

        @pl.when(partner == seq_index + 1)
        def _():
            for i in range(2):
                halo[i, BLOCK:] = got[i, :BLOCK]
                near[i, 2 * BLOCK : 2 * BLOCK + EDGE] = coarse(got[i, :BLOCK], halo_scratch)
                near[i, 2 * BLOCK + EDGE :] = got[i, BLOCK:]

        @pl.when((partner != seq_index + 1) & (partner != seq_index - 1))
        def _():
            for i in range(2):
                panels[0][i, at] = got[i, :BLOCK]

    panel_scratch = pool()
    for level in range(3, top_level + 1):
        for i in range(2):
            panels[level - 2][i] = coarse(panels[level - 3][i], panel_scratch)

    def window(ref, lo, hi, valid):
        return ref[0, rows_of(lo, hi - lo)], ref[1, rows_of(lo, hi - lo)], valid, (lo, hi)

    level_pieces = [
        [[window(halo, 0, 1, has_prev)], [window(halo, 1, 2, has_next)]],
        [
            [window(near, 0, 1, has_prev), window(near, 2, 4, has_next)],
            [window(near, 0, 2, has_prev), window(near, 3, 4, has_next)],
        ],
    ]
    for level in range(2, top_level + 1):
        pieces = []
        for index, valid in slots_of(seq_index >> (level - 2), seq_count >> (level - 2)):
            at = pl.ds(pl.multiple_of(index * BLOCK, BLOCK), BLOCK)
            panel = panels[level - 2]
            pieces.append((panel[0, at], panel[1, at], valid, at))
        level_pieces.append([pieces])
    level_queries = [[held[0, rows_of(0)], held[0, rows_of(blocks - 1)]]]
    for level in range(1, top_level + 1):
        query = query_refs[level - 1][...]
        step = query.shape[0] // len(level_pieces[level])
        level_queries.append(
            [query[a * step : (a + 1) * step] for a in range(len(level_pieces[level]))]
        )

    def unit(query, pieces, before=None):
        scores = []
        for key, _, valid, _ in pieces:
            score = nt(query, key) * factor
            scores.append(score if valid is None else jnp.where(valid, score, MASKED))
        peak = functools.reduce(jnp.maximum, [row_max(score) for score in scores])
        if before is not None:
            peak = jnp.maximum(peak, before[0])
        exps = [jnp.exp2(score - across(peak, score.shape[1])) for score in scores]
        rounded = [e.astype(BF16) for e in exps]
        ones = jnp.ones((BLOCK, width), BF16)
        both = []
        for r, piece in zip(rounded, pieces):
            count = piece[1].shape[0] // BLOCK
            both.append(nn(r, jnp.concatenate([piece[1], jnp.concatenate([ones] * count, axis=0)], axis=1)))
        both = total_of(both)
        sums, total = both[:, :width], both[:, width:]
        if before is not None:
            keep = jnp.exp2(before[0] - peak)
            total, sums = total + keep * before[1], sums + keep * before[2]
        return peak, total, sums, exps, rounded

    def before_of(block):
        return [stats[w, rows_of(block)] for w in range(3)]

    level_units = [
        [
            unit(query, pieces, before_of(block))
            for query, pieces, block in zip(level_queries[0], level_pieces[0], (0, blocks - 1))
        ]
    ]
    for level in range(1, top_level + 1):
        level_units.append(
            [unit(q, pieces) for q, pieces in zip(level_queries[level], level_pieces[level])]
        )

    def stacked(level, which):
        units = [u[which] for u in level_units[level]]
        if level == 0:
            units = [units[0], stats[which, rows_of(1, blocks - 2)], units[1]]
        return jnp.concatenate(units, axis=0)

    run = [stacked(top_level, w) for w in range(3)]
    own_factors, run_factors = [None] * top_level, [None] * top_level
    for level in range(top_level - 1, -1, -1):
        up_peak, up_total, up_sums = [spread(x, pool()) for x in run]
        peak, total, sums = [stacked(level, w) for w in range(3)]
        both = jnp.maximum(peak, up_peak)
        own = jnp.exp2(peak - both)
        up = 2.0 * jnp.exp2(up_peak - both)
        own_factors[level], run_factors[level] = own, up
        run = [both, own * total + up * up_total, own * sums + up * up_sums]

    inverse = 1.0 / run[1]
    attended = run[2] * inverse
    attended_ref[...] = attended.astype(BF16)

    cot = held[3].astype(F32)
    grad, shift = cot * inverse, row_sum(cot * attended) * inverse
    level_grads = []
    for level in range(top_level):
        level_grads.append((own_factors[level] * grad, own_factors[level] * shift))
        grad = pair_sum(run_factors[level] * grad, pool())
        shift = pair_sum(run_factors[level] * shift, pool())
    level_grads.append((grad, shift))
    back[0] = stacked(0, 0)
    back[1], back[2] = level_grads[0]

    for panel_grad in panel_grads:
        panel_grad[...] = jnp.zeros(panel_grad.shape, F32)

    grad_queries = []
    parts_of = [[[[] for _ in range(4)] for _ in range(2)] for _ in range(2)]
    for level in range(top_level, -1, -1):
        grad, shift = level_grads[level]
        step = level_queries[level][0].shape[0]
        level_parts = []
        for a, (query, pieces) in enumerate(zip(level_queries[level], level_pieces[level])):
            at = a if level > 0 else a * (blocks - 1)
            cut = slice(at * step, (at + 1) * step)
            grad_rounded = grad[cut].astype(BF16)
            grad_scaled = (grad[cut] * scale).astype(BF16)
            shift_scaled = shift[cut] * scale
            exps, rounded = level_units[level][a][3:]
            query_parts = []
            for piece, e, r in zip(pieces, exps, rounded):
                key, value, _, where = piece
                score_grad = nt(grad_scaled, value) - across(shift_scaled, e.shape[1])
                score_grad = (e * score_grad).astype(BF16)
                query_parts.append(nn(score_grad, key))
                outs = tn(score_grad, query), tn(r, grad_rounded)
                for i in range(2):
                    if level >= 2:
                        panel_grads[level - 2][i, where] += outs[i]
                        continue
                    lo, hi = where
                    for b in range(lo, hi):
                        parts_of[level][i][b].append(outs[i][rows_of(b - lo)])
            level_parts.append(total_of(query_parts))
        grad_queries.append(level_parts)

    run_grad = grad_queries[0][0]
    for level_parts in grad_queries[1:-1]:
        run_grad = jnp.concatenate(level_parts, axis=0) + 0.5 * spread(run_grad, pool())
    partial_ref[...] = 0.5 * spread(run_grad, pool())
    for a, block in enumerate((0, blocks - 1)):
        partial_ref[rows_of(block)] += grad_queries[-1][a]

    for level in range(top_level, 2, -1):
        for i in range(2):
            panel_grads[level - 3][i] += 0.5 * spread(panel_grads[level - 2][i], panel_scratch)

    near_grads = [[total_of(p) for p in parts_of[1][i]] for i in range(2)]
    halo_grads = [[total_of(p) for p in parts_of[0][i][:2]] for i in range(2)]
    to_prev = [halo_grads[i][0] + 0.5 * spread(near_grads[i][1][EDGE:], pool()) for i in range(2)]
    to_next = [halo_grads[i][1] + 0.5 * spread(near_grads[i][2][:EDGE], pool()) for i in range(2)]
    for d in range(1, seq_count):
        out = sends[d]
        partner = seq_index ^ d
        at = pl.ds(pl.multiple_of(partner * BLOCK, BLOCK), BLOCK)
        if d not in wides:
            for i in range(2):
                out[i] = panel_grads[0][i, at].astype(BF16)
            continue

        @pl.when(partner == seq_index - 1)
        def _():
            for i in range(2):
                out[i, :BLOCK] = to_prev[i].astype(BF16)
                out[i, BLOCK : 2 * BLOCK] = near_grads[i][0].astype(BF16)
                out[i, 2 * BLOCK :] = near_grads[i][1][:EDGE].astype(BF16)

        @pl.when(partner == seq_index + 1)
        def _():
            for i in range(2):
                out[i, :BLOCK] = to_next[i].astype(BF16)
                out[i, BLOCK : BLOCK + EDGE] = near_grads[i][2][EDGE:].astype(BF16)
                out[i, BLOCK + EDGE :] = near_grads[i][3].astype(BF16)

        @pl.when((partner != seq_index + 1) & (partner != seq_index - 1))
        def _():
            for i in range(2):
                out[i, :BLOCK] = panel_grads[0][i, at].astype(BF16)
                out[i, BLOCK:] = jnp.zeros((REST, width), BF16)


def local_kernel(held, back, partial_ref, merged, attended_hbm, local_ref, grad_query_ref, sem):
    copy = pltpu.make_async_copy(merged, attended_hbm, sem)
    copy.start()
    blocks, width = held.shape[1] // BLOCK, held.shape[2]
    scale = width ** (-0.5)
    factor = scale * LOG2E
    parts = [[[] for _ in range(blocks)] for _ in range(2)]
    for a in range(blocks):
        lo, hi = own_window(a, blocks)
        window = rows_of(lo, hi - lo)
        query, key, value = held[0, rows_of(a)], held[1, window], held[2, window]
        peak, grad, shift = [back[w, rows_of(a)] for w in range(3)]
        wide = key.shape[0]
        exps = jnp.exp2(nt(query, key) * factor - across(peak, wide))
        score_grad = nt((grad * scale).astype(BF16), value) - across(shift * scale, wide)
        score_grad = (exps * score_grad).astype(BF16)
        grad_query_ref[rows_of(a)] = (nn(score_grad, key) + partial_ref[rows_of(a)]).astype(BF16)
        outs = tn(score_grad, query), tn(exps.astype(BF16), grad.astype(BF16))
        for i in range(2):
            for b in range(lo, hi):
                parts[i][b].append(outs[i][rows_of(b - lo)])
    for i in range(2):
        for b in range(blocks):
            local_ref[i, rows_of(b)] = total_of(parts[i][b])
    copy.wait()


def combine_kernel(seq_count, head_count, grad_query_ref, local_ref, *refs):
    received, refs = refs[: seq_count - 1], refs[seq_count - 1 :]
    received = dict(zip(seq_order(seq_count), received))
    outs, refs = refs[:-3], refs[-3:]
    outs = dict(zip([0] + head_order(head_count), outs))
    total, level_1, level_2 = refs
    seq_index, head_index = lax.axis_index("seq"), lax.axis_index("head")
    wides = wide_distances(seq_count)
    rows, width = local_ref.shape[1:]
    share = rows // head_count

    level_1[...] = jnp.zeros(level_1.shape, F32)
    level_2[...] = jnp.zeros(level_2.shape, F32)
    for i in range(2):
        total[i] = local_ref[i]
    for d in range(1, seq_count):
        got = received[d]
        partner = seq_index ^ d
        if d not in wides:
            for i in range(2):
                level_2[i] += got[i].astype(F32)
            continue

        @pl.when(partner == seq_index - 1)
        def _():
            for i in range(2):
                total[i, :BLOCK] += got[i, :BLOCK].astype(F32)
                level_1[i, EDGE:] += got[i, BLOCK:].astype(F32)

        @pl.when(partner == seq_index + 1)
        def _():
            for i in range(2):
                total[i, rows - BLOCK :] += got[i, :BLOCK].astype(F32)
                level_1[i, :REST] += got[i, BLOCK:].astype(F32)

        @pl.when((partner != seq_index + 1) & (partner != seq_index - 1))
        def _():
            for i in range(2):
                level_2[i] += got[i, :BLOCK].astype(F32)

    for i in range(2):
        half = level_2[i] * 0.5
        for phase in range(2):
            level_1[i, pl.ds(phase, half.shape[0], stride=2), :] += half
        half = level_1[i] * 0.5
        for phase in range(2):
            total[i, pl.ds(phase, half.shape[0], stride=2), :] += half
    for d in range(head_count):
        at = pl.ds(pl.multiple_of((head_index ^ d) * share, share), share)
        out = outs[d & ~1].at[d & 1] if d & ~1 in paired(head_count) else outs[d]
        out[0] = grad_query_ref[at, :]
        out[1] = total[0, at].astype(BF16)
        out[2] = total[1, at].astype(BF16)


def place_kernel(head_count, *refs):
    parts, outs = refs[:-3], refs[-3:]
    head_index = lax.axis_index("head")
    width = parts[0].shape[-1]
    for d, part in zip([0] + head_order(head_count), parts):
        at = pl.ds(pl.multiple_of((head_index ^ d) * width, width), width)
        for i in range(3):
            outs[i][:, at] = part[0, i] if d in paired(head_count) else part[i]


def place_late_kernel(head_count, *refs):
    late, outs, sems = refs[3], refs[4:7], refs[7]
    head_index = lax.axis_index("head")
    width = late.shape[-1]
    far = [d for d in head_order(head_count) if d in paired(head_count)]
    copies = []
    for row, d in enumerate(far):
        at = pl.ds(pl.multiple_of((head_index ^ d ^ 1) * width, width), width)
        for i in range(3):
            k = 3 * row + i
            copies.append(pltpu.make_async_copy(late.at[k], outs[i].at[:, at], sems.at[k]))
            copies[-1].start()
    for copy in copies:
        copy.wait()


def call(kernel, outs, scratch, args, in_hbm=0, hbm_outs=0, aliases={}, flops=0):
    return pl.pallas_call(
        kernel,
        out_shape=outs,
        in_specs=[pl.BlockSpec(memory_space=pltpu.HBM)] * in_hbm + [VMEM] * (len(args) - in_hbm),
        out_specs=[pl.BlockSpec(memory_space=pltpu.HBM)] * hbm_outs
        + [VMEM] * (len(outs) - hbm_outs),
        scratch_shapes=scratch,
        input_output_aliases=aliases,
        compiler_params=pltpu.CompilerParams(vmem_limit_bytes=48 * 2**20),
        cost_estimate=pl.CostEstimate(flops=flops, bytes_accessed=2**20, transcendentals=0),
    )(*args)


def swap_all(arrays, axis, distances):
    size = lax.axis_size(axis)
    return [
        lax.ppermute(x, axis, [(i, i ^ d) for i in range(size)]) for x, d in zip(arrays, distances)
    ]


def per_device(queries, keys, values, grad_out):
    seq_count, head_count = lax.axis_size("seq"), lax.axis_size("head")
    rows, width = queries.shape
    assert rows == 4 * BLOCK and width == BLOCK
    fine_blocks = rows * seq_count // BLOCK
    top_level = (fine_blocks // 4).bit_length() - 1
    wides = wide_distances(seq_count)
    distances = seq_order(seq_count)

    def shape(*dims, dtype=BF16):
        return jax.ShapeDtypeStruct(dims, dtype)

    def f32(*dims):
        return pltpu.VMEM(dims, F32)

    payloads = [shape(2, BLOCK + REST if d in wides else BLOCK, width) for d in distances]
    arguments = [
        pltpu.with_memory_space_constraint(x, pltpu.HBM) for x in (queries, keys, values, grad_out)
    ]
    held, *sends = call(
        functools.partial(prep_kernel, seq_count),
        [shape(4, rows, width)] + payloads,
        [f32(rows, width), f32(rows // 2, width)] * 2 + [pltpu.SemaphoreType.DMA((4,))],
        arguments,
        in_hbm=4,
    )
    received = swap_all(sends, "seq", distances)

    unit_flops = 2 * BLOCK * BLOCK * width
    stats, *level_queries = call(
        fine_kernel,
        [shape(3, rows, width, dtype=F32)]
        + [shape(rows >> level, width) for level in range(1, top_level + 1)],
        [f32(rows >> level, width) for level in range(top_level)],
        (held,),
        flops=20 * unit_flops,
    )

    panel_rows = [(seq_count >> (level - 2)) * BLOCK for level in range(2, top_level + 1)]
    pools = [f32(BLOCK, width), f32(max(seq_count * BLOCK, rows), width)]
    for level in range(top_level - 1, -1, -1):
        pools += [f32(rows >> level, width)] * 3
    for level in range(top_level):
        pools += [f32(rows >> level, width)] * 2
    for level in range(top_level - 1, -1, -1):
        pools += [f32(rows >> level, width)]
    pools += [f32(BLOCK, width)] * 4
    main = call(
        functools.partial(main_kernel, seq_count, top_level),
        [shape(rows, width)]
        + payloads
        + [shape(3, rows, width, dtype=F32), shape(rows, width, dtype=F32)],
        [pltpu.VMEM((2, 2 * BLOCK, width), BF16), pltpu.VMEM((2, 4 * BLOCK, width), BF16)]
        + [pltpu.VMEM((2, r, width), BF16) for r in panel_rows]
        + [f32(2, r, width) for r in panel_rows]
        + pools,
        (held, stats, *level_queries, *received),
        flops=70 * unit_flops,
    )
    merged, sends, back, partial = main[0], main[1:seq_count], main[-2], main[-1]
    returned = swap_all(sends, "seq", distances)

    share = rows // head_count
    attended, local, grad_query = call(
        local_kernel,
        [shape(rows, width), shape(2, rows, width, dtype=F32), shape(rows, width)],
        [pltpu.SemaphoreType.DMA],
        (held, back, partial, merged),
        hbm_outs=1,
        flops=50 * unit_flops,
    )

    order = head_order(head_count)
    own, *parts = call(
        functools.partial(combine_kernel, seq_count, head_count),
        [
            shape(*((2,) if d in paired(head_count) else ()), 3, share, width)
            for d in [0] + order
        ],
        [f32(2, rows, width), f32(2, rows // 2, width), f32(2, rows // 4, width)],
        (grad_query, local, *returned),
    )
    parts = lax.optimization_barrier(swap_all(parts, "head", order))
    far = [part[1] for d, part in zip(order, parts) if d in paired(head_count)]
    late = swap_all([jnp.concatenate(far, axis=0)] if far else [], "head", [1])
    grads = call(
        functools.partial(place_kernel, head_count),
        [shape(share, head_count * width)] * 3,
        [],
        (own, *parts),
        flops=50 * unit_flops,
    )
    if late:
        grads = call(
            functools.partial(place_late_kernel, head_count),
            [shape(share, head_count * width)] * 3,
            [pltpu.SemaphoreType.DMA((3 * len(far),))],
            (*grads, *late),
            in_hbm=3,
            hbm_outs=3,
            aliases={0: 0, 1: 1, 2: 2},
        )
    return (attended, *grads)


def solution(mesh):
    return jax.shard_map(
        per_device,
        mesh=mesh,
        in_specs=(P("seq", "head"),) * 4,
        out_specs=(P("seq", "head"),) + (P(("seq", "head"), None),) * 3,
        check_vma=False,
    )
```

```python
import functools

import jax
import jax.numpy as jnp
from jax import lax
from jax.experimental import pallas as pl
from jax.experimental.pallas import tpu as pltpu
from jax.sharding import PartitionSpec as P

BLOCK = 128
EDGE = BLOCK // 2
REST = 2 * BLOCK - EDGE
MASKED = -1e30
LOG2E = 1.4426950408889634
F32 = jnp.float32
BF16 = jnp.bfloat16
VMEM = pl.BlockSpec(memory_space=pltpu.VMEM)


def nt(a, b):
    return lax.dot_general(a, b, (((1,), (1,)), ((), ())), preferred_element_type=F32)


def nn(a, b):
    return lax.dot_general(a, b, (((1,), (0,)), ((), ())), preferred_element_type=F32)


def tn(a, b):
    return lax.dot_general(a, b, (((0,), (0,)), ((), ())), preferred_element_type=F32)


def pair_sum(x, scratch):
    rows = x.shape[0]
    scratch[:rows] = x
    return scratch[pl.ds(0, rows // 2, stride=2), :] + scratch[pl.ds(1, rows // 2, stride=2), :]


def coarse(x, scratch):
    return (pair_sum(x.astype(F32), scratch) * 0.5).astype(BF16)


def spread(x, scratch):
    rows = x.shape[0]
    scratch[pl.ds(0, rows, stride=2), :] = x
    scratch[pl.ds(1, rows, stride=2), :] = x
    return scratch[: 2 * rows]


def wide_distances(seq_count):
    return sorted({i ^ (i + 1) for i in range(seq_count - 1)})


def seq_order(seq_count):
    wides = wide_distances(seq_count)
    return wides[::-1] + [d for d in range(1, seq_count) if d not in wides]


def paired(head_count):
    return list(range(4, head_count - 2, 2))


def head_order(head_count):
    far = [d for d in (head_count - 2, head_count - 1) if d >= 4]
    return [d for d in paired(head_count) + [2, 3] + far + [1] if d < head_count]


def last_heads(head_count):
    return [d for d in head_order(head_count) if d in (1, head_count - 2, head_count - 1)]


def prep_kernel(seq_count, *refs):
    sources, refs = refs[:4], refs[4:]
    held, refs = refs[0], refs[1:]
    sends, scratches, sems = refs[: seq_count - 1], refs[seq_count - 1 : -1], refs[-1]
    sends = dict(zip(seq_order(seq_count), sends))
    seq_index = lax.axis_index("seq")
    wides = wide_distances(seq_count)
    rows = held.shape[1]
    copies = [
        pltpu.make_async_copy(source, held.at[i], sems.at[i]) for i, source in enumerate(sources)
    ]
    for i in (1, 2, 0, 3):
        copies[i].start()
    for i in range(2):
        copies[1 + i].wait()
        ref = held.at[1 + i]
        level_1 = coarse(ref[...], scratches[2 * i])
        level_2 = coarse(level_1, scratches[2 * i + 1])
        for d in range(1, seq_count):
            out = sends[d]
            partner = seq_index ^ d
            if d not in wides:
                out[i] = level_2
                continue

            @pl.when(partner == seq_index + 1)
            def _():
                out[i, :BLOCK] = ref[rows - BLOCK :]
                out[i, BLOCK:] = level_1[:REST]

            @pl.when(partner == seq_index - 1)
            def _():
                out[i, :BLOCK] = ref[:BLOCK]
                out[i, BLOCK:] = level_1[EDGE:]

            @pl.when((partner != seq_index + 1) & (partner != seq_index - 1))
            def _():
                out[i, :BLOCK] = level_2
                out[i, BLOCK:] = level_1[:REST]

    copies[0].wait()
    copies[3].wait()


def slots_of(block, block_count):
    parent, odd = block // 2, block % 2
    if block_count == 4:
        first = parent == 0
        return [
            (jnp.where(first, 3, 0), None),
            (jnp.where(first, 2, 1), jnp.where(first, odd == 0, odd == 1)),
        ]
    near = jnp.where(odd == 0, 2 * parent + 2, 2 * parent - 1)
    raw = [2 * parent - 2, near, 2 * parent + 3]
    return [(jnp.clip(j, 0, block_count - 1), (j >= 0) & (j < block_count)) for j in raw]


def across(x, width):
    return jnp.concatenate([x] * (width // x.shape[1]), axis=1)


def lanes(column):
    return jnp.broadcast_to(column, (column.shape[0], BLOCK))


def row_max(x):
    return lanes(jnp.max(x, axis=-1, keepdims=True))


def row_sum(x):
    return lanes(jnp.sum(x, axis=-1, keepdims=True))


def total_of(parts):
    return functools.reduce(jnp.add, parts)


def rows_of(block, count=1):
    return slice(block * BLOCK, (block + count) * BLOCK)


def own_window(a, blocks):
    return max(a - 1, 0), min(a + 2, blocks)


def fine_kernel(held, stats, *refs):
    levels = len(refs) // 2
    blocks, width = held.shape[1] // BLOCK, held.shape[2]
    factor = width ** (-0.5) * LOG2E
    for a in range(blocks):
        lo, hi = own_window(a, blocks)
        window = rows_of(lo, hi - lo)
        scores = nt(held[0, rows_of(a)], held[1, window]) * factor
        peak = row_max(scores)
        exps = jnp.exp2(scores - across(peak, scores.shape[1]))
        stats[0, rows_of(a)] = peak
        stats[1, rows_of(a)] = row_sum(exps)
        stats[2, rows_of(a)] = nn(exps.astype(BF16), held[2, window])
    query = held[0]
    for level in range(levels):
        query = coarse(query, refs[levels + level])
        refs[level][...] = query


def main_kernel(seq_count, top_level, *refs):
    refs = list(refs)

    def take(count):
        taken = refs[:count]
        del refs[:count]
        return taken

    held, stats = take(2)
    query_refs = take(top_level)
    received = dict(zip(seq_order(seq_count), take(seq_count - 1)))
    (attended_ref,) = take(1)
    sends = dict(zip(seq_order(seq_count), take(seq_count - 1)))
    back, partial_ref = take(2)
    halo, near = take(2)
    panels = take(top_level - 1)
    panel_grads = take(top_level - 1)
    pools = refs

    def pool():
        return pools.pop(0)

    seq_index = lax.axis_index("seq")
    wides = wide_distances(seq_count)
    rows, width = held.shape[1:]
    blocks = rows // BLOCK
    scale = width ** (-0.5)
    factor = scale * LOG2E
    has_prev, has_next = seq_index > 0, seq_index < seq_count - 1

    for panel in panels:
        panel[...] = jnp.zeros(panel.shape, BF16)

    @pl.when(seq_index == 0)
    def _():
        halo[:, :BLOCK] = jnp.zeros((2, BLOCK, width), BF16)
        near[:, : 2 * BLOCK] = jnp.zeros((2, 2 * BLOCK, width), BF16)

    @pl.when(seq_index == seq_count - 1)
    def _():
        halo[:, BLOCK:] = jnp.zeros((2, BLOCK, width), BF16)
        near[:, 2 * BLOCK :] = jnp.zeros((2, 2 * BLOCK, width), BF16)

    halo_scratch = pool()
    for d in range(1, seq_count):
        got = received[d]
        partner = seq_index ^ d
        at = pl.ds(pl.multiple_of(partner * BLOCK, BLOCK), BLOCK)
        if d not in wides:
            for i in range(2):
                panels[0][i, at] = got[i]
            continue

        @pl.when(partner == seq_index - 1)
        def _():
            for i in range(2):
                halo[i, :BLOCK] = got[i, :BLOCK]
                near[i, :REST] = got[i, BLOCK:]
                near[i, REST : 2 * BLOCK] = coarse(got[i, :BLOCK], halo_scratch)

        @pl.when(partner == seq_index + 1)
        def _():
            for i in range(2):
                halo[i, BLOCK:] = got[i, :BLOCK]
                near[i, 2 * BLOCK : 2 * BLOCK + EDGE] = coarse(got[i, :BLOCK], halo_scratch)
                near[i, 2 * BLOCK + EDGE :] = got[i, BLOCK:]

        @pl.when((partner != seq_index + 1) & (partner != seq_index - 1))
        def _():
            for i in range(2):
                panels[0][i, at] = got[i, :BLOCK]

    panel_scratch = pool()
    for level in range(3, top_level + 1):
        for i in range(2):
            panels[level - 2][i] = coarse(panels[level - 3][i], panel_scratch)

    def window(ref, lo, hi, valid):
        return ref[0, rows_of(lo, hi - lo)], ref[1, rows_of(lo, hi - lo)], valid, (lo, hi)

    level_pieces = [
        [[window(halo, 0, 1, has_prev)], [window(halo, 1, 2, has_next)]],
        [
            [window(near, 0, 1, has_prev), window(near, 2, 4, has_next)],
            [window(near, 0, 2, has_prev), window(near, 3, 4, has_next)],
        ],
    ]
    for level in range(2, top_level + 1):
        pieces = []
        for index, valid in slots_of(seq_index >> (level - 2), seq_count >> (level - 2)):
            at = pl.ds(pl.multiple_of(index * BLOCK, BLOCK), BLOCK)
            panel = panels[level - 2]
            pieces.append((panel[0, at], panel[1, at], valid, at))
        level_pieces.append([pieces])
    level_queries = [[held[0, rows_of(0)], held[0, rows_of(blocks - 1)]]]
    for level in range(1, top_level + 1):
        query = query_refs[level - 1][...]
        step = query.shape[0] // len(level_pieces[level])
        level_queries.append(
            [query[a * step : (a + 1) * step] for a in range(len(level_pieces[level]))]
        )

    def unit(query, pieces, before=None):
        scores = []
        for key, _, valid, _ in pieces:
            score = nt(query, key) * factor
            scores.append(score if valid is None else jnp.where(valid, score, MASKED))
        peak = functools.reduce(jnp.maximum, [row_max(score) for score in scores])
        if before is not None:
            peak = jnp.maximum(peak, before[0])
        exps = [jnp.exp2(score - across(peak, score.shape[1])) for score in scores]
        rounded = [e.astype(BF16) for e in exps]
        ones = jnp.ones((BLOCK, width), BF16)
        both = []
        for r, piece in zip(rounded, pieces):
            count = piece[1].shape[0] // BLOCK
            both.append(nn(r, jnp.concatenate([piece[1], jnp.concatenate([ones] * count, axis=0)], axis=1)))
        both = total_of(both)
        sums, total = both[:, :width], both[:, width:]
        if before is not None:
            keep = jnp.exp2(before[0] - peak)
            total, sums = total + keep * before[1], sums + keep * before[2]
        return peak, total, sums, exps, rounded

    def before_of(block):
        return [stats[w, rows_of(block)] for w in range(3)]

    level_units = [
        [
            unit(query, pieces, before_of(block))
            for query, pieces, block in zip(level_queries[0], level_pieces[0], (0, blocks - 1))
        ]
    ]
    for level in range(1, top_level + 1):
        level_units.append(
            [unit(q, pieces) for q, pieces in zip(level_queries[level], level_pieces[level])]
        )

    def stacked(level, which):
        units = [u[which] for u in level_units[level]]
        if level == 0:
            units = [units[0], stats[which, rows_of(1, blocks - 2)], units[1]]
        return jnp.concatenate(units, axis=0)

    run = [stacked(top_level, w) for w in range(3)]
    own_factors, run_factors = [None] * top_level, [None] * top_level
    for level in range(top_level - 1, -1, -1):
        up_peak, up_total, up_sums = [spread(x, pool()) for x in run]
        peak, total, sums = [stacked(level, w) for w in range(3)]
        both = jnp.maximum(peak, up_peak)
        own = jnp.exp2(peak - both)
        up = 2.0 * jnp.exp2(up_peak - both)
        own_factors[level], run_factors[level] = own, up
        run = [both, own * total + up * up_total, own * sums + up * up_sums]

    inverse = 1.0 / run[1]
    attended = run[2] * inverse
    attended_ref[...] = attended.astype(BF16)

    cot = held[3].astype(F32)
    grad, shift = cot * inverse, row_sum(cot * attended) * inverse
    level_grads = []
    for level in range(top_level):
        level_grads.append((own_factors[level] * grad, own_factors[level] * shift))
        grad = pair_sum(run_factors[level] * grad, pool())
        shift = pair_sum(run_factors[level] * shift, pool())
    level_grads.append((grad, shift))
    back[0] = stacked(0, 0)
    back[1], back[2] = level_grads[0]

    for panel_grad in panel_grads:
        panel_grad[...] = jnp.zeros(panel_grad.shape, F32)

    grad_queries = []
    parts_of = [[[[] for _ in range(4)] for _ in range(2)] for _ in range(2)]
    for level in range(top_level, -1, -1):
        grad, shift = level_grads[level]
        step = level_queries[level][0].shape[0]
        level_parts = []
        for a, (query, pieces) in enumerate(zip(level_queries[level], level_pieces[level])):
            at = a if level > 0 else a * (blocks - 1)
            cut = slice(at * step, (at + 1) * step)
            grad_rounded = grad[cut].astype(BF16)
            grad_scaled = (grad[cut] * scale).astype(BF16)
            shift_scaled = shift[cut] * scale
            exps, rounded = level_units[level][a][3:]
            query_parts = []
            for piece, e, r in zip(pieces, exps, rounded):
                key, value, _, where = piece
                score_grad = nt(grad_scaled, value) - across(shift_scaled, e.shape[1])
                score_grad = (e * score_grad).astype(BF16)
                query_parts.append(nn(score_grad, key))
                outs = tn(score_grad, query), tn(r, grad_rounded)
                for i in range(2):
                    if level >= 2:
                        panel_grads[level - 2][i, where] += outs[i]
                        continue
                    lo, hi = where
                    for b in range(lo, hi):
                        parts_of[level][i][b].append(outs[i][rows_of(b - lo)])
            level_parts.append(total_of(query_parts))
        grad_queries.append(level_parts)

    run_grad = grad_queries[0][0]
    for level_parts in grad_queries[1:-1]:
        run_grad = jnp.concatenate(level_parts, axis=0) + 0.5 * spread(run_grad, pool())
    partial_ref[...] = 0.5 * spread(run_grad, pool())
    for a, block in enumerate((0, blocks - 1)):
        partial_ref[rows_of(block)] += grad_queries[-1][a]

    for level in range(top_level, 2, -1):
        for i in range(2):
            panel_grads[level - 3][i] += 0.5 * spread(panel_grads[level - 2][i], panel_scratch)

    near_grads = [[total_of(p) for p in parts_of[1][i]] for i in range(2)]
    halo_grads = [[total_of(p) for p in parts_of[0][i][:2]] for i in range(2)]
    to_prev = [halo_grads[i][0] + 0.5 * spread(near_grads[i][1][EDGE:], pool()) for i in range(2)]
    to_next = [halo_grads[i][1] + 0.5 * spread(near_grads[i][2][:EDGE], pool()) for i in range(2)]
    for d in range(1, seq_count):
        out = sends[d]
        partner = seq_index ^ d
        at = pl.ds(pl.multiple_of(partner * BLOCK, BLOCK), BLOCK)
        if d not in wides:
            for i in range(2):
                out[i] = panel_grads[0][i, at].astype(BF16)
            continue

        @pl.when(partner == seq_index - 1)
        def _():
            for i in range(2):
                out[i, :BLOCK] = to_prev[i].astype(BF16)
                out[i, BLOCK : 2 * BLOCK] = near_grads[i][0].astype(BF16)
                out[i, 2 * BLOCK :] = near_grads[i][1][:EDGE].astype(BF16)

        @pl.when(partner == seq_index + 1)
        def _():
            for i in range(2):
                out[i, :BLOCK] = to_next[i].astype(BF16)
                out[i, BLOCK : BLOCK + EDGE] = near_grads[i][2][EDGE:].astype(BF16)
                out[i, BLOCK + EDGE :] = near_grads[i][3].astype(BF16)

        @pl.when((partner != seq_index + 1) & (partner != seq_index - 1))
        def _():
            for i in range(2):
                out[i, :BLOCK] = panel_grads[0][i, at].astype(BF16)
                out[i, BLOCK:] = jnp.zeros((REST, width), BF16)


def local_kernel(held, back, partial_ref, merged, attended_hbm, local_ref, grad_query_ref, sem):
    copy = pltpu.make_async_copy(merged, attended_hbm, sem)
    copy.start()
    blocks, width = held.shape[1] // BLOCK, held.shape[2]
    scale = width ** (-0.5)
    factor = scale * LOG2E
    parts = [[[] for _ in range(blocks)] for _ in range(2)]
    for a in range(blocks):
        lo, hi = own_window(a, blocks)
        window = rows_of(lo, hi - lo)
        query, key, value = held[0, rows_of(a)], held[1, window], held[2, window]
        peak, grad, shift = [back[w, rows_of(a)] for w in range(3)]
        wide = key.shape[0]
        exps = jnp.exp2(nt(query, key) * factor - across(peak, wide))
        score_grad = nt((grad * scale).astype(BF16), value) - across(shift * scale, wide)
        score_grad = (exps * score_grad).astype(BF16)
        grad_query_ref[rows_of(a)] = (nn(score_grad, key) + partial_ref[rows_of(a)]).astype(BF16)
        outs = tn(score_grad, query), tn(exps.astype(BF16), grad.astype(BF16))
        for i in range(2):
            for b in range(lo, hi):
                parts[i][b].append(outs[i][rows_of(b - lo)])
    for i in range(2):
        for b in range(blocks):
            local_ref[i, rows_of(b)] = total_of(parts[i][b])
    copy.wait()


def combine_kernel(seq_count, head_count, grad_query_ref, local_ref, *refs):
    received, refs = refs[: seq_count - 1], refs[seq_count - 1 :]
    received = dict(zip(seq_order(seq_count), received))
    outs, refs = refs[:-3], refs[-3:]
    outs = dict(zip([0] + head_order(head_count), outs))
    total, level_1, level_2 = refs
    seq_index, head_index = lax.axis_index("seq"), lax.axis_index("head")
    wides = wide_distances(seq_count)
    rows, width = local_ref.shape[1:]
    share = rows // head_count

    level_1[...] = jnp.zeros(level_1.shape, F32)
    level_2[...] = jnp.zeros(level_2.shape, F32)
    for i in range(2):
        total[i] = local_ref[i]
    for d in range(1, seq_count):
        got = received[d]
        partner = seq_index ^ d
        if d not in wides:
            for i in range(2):
                level_2[i] += got[i].astype(F32)
            continue

        @pl.when(partner == seq_index - 1)
        def _():
            for i in range(2):
                total[i, :BLOCK] += got[i, :BLOCK].astype(F32)
                level_1[i, EDGE:] += got[i, BLOCK:].astype(F32)

        @pl.when(partner == seq_index + 1)
        def _():
            for i in range(2):
                total[i, rows - BLOCK :] += got[i, :BLOCK].astype(F32)
                level_1[i, :REST] += got[i, BLOCK:].astype(F32)

        @pl.when((partner != seq_index + 1) & (partner != seq_index - 1))
        def _():
            for i in range(2):
                level_2[i] += got[i, :BLOCK].astype(F32)

    for i in range(2):
        half = level_2[i] * 0.5
        for phase in range(2):
            level_1[i, pl.ds(phase, half.shape[0], stride=2), :] += half
        half = level_1[i] * 0.5
        for phase in range(2):
            total[i, pl.ds(phase, half.shape[0], stride=2), :] += half
    for d in range(head_count):
        at = pl.ds(pl.multiple_of((head_index ^ d) * share, share), share)
        out = outs[d & ~1].at[d & 1] if d & ~1 in paired(head_count) else outs[d]
        out[0] = grad_query_ref[at, :]
        out[1] = total[0, at].astype(BF16)
        out[2] = total[1, at].astype(BF16)


def place_kernel(head_count, *refs):
    parts, outs = refs[:-3], refs[-3:]
    head_index = lax.axis_index("head")
    width = parts[0].shape[-1]
    first = [d for d in head_order(head_count) if d not in last_heads(head_count)]
    for d, part in zip([0] + first, parts):
        at = pl.ds(pl.multiple_of((head_index ^ d) * width, width), width)
        for i in range(3):
            outs[i][:, at] = part[0, i] if d in paired(head_count) else part[i]


def place_late_kernel(head_count, *refs):
    parts, outs, sems = refs[3:-4], refs[-4:-1], refs[-1]
    head_index = lax.axis_index("head")
    width = parts[0].shape[-1]
    copies = []
    far = [d + 1 for d in head_order(head_count) if d in paired(head_count)]
    for k, (d, part) in enumerate(zip(last_heads(head_count) + far, parts)):
        at = pl.ds(pl.multiple_of((head_index ^ d) * width, width), width)
        for i in range(3):
            copies.append(pltpu.make_async_copy(part.at[i], outs[i].at[:, at], sems.at[k, i]))
            copies[-1].start()
    for copy in copies:
        copy.wait()


def call(kernel, outs, scratch, args, in_hbm=0, hbm_outs=0, aliases={}, flops=0):
    return pl.pallas_call(
        kernel,
        out_shape=outs,
        in_specs=[pl.BlockSpec(memory_space=pltpu.HBM)] * in_hbm + [VMEM] * (len(args) - in_hbm),
        out_specs=[pl.BlockSpec(memory_space=pltpu.HBM)] * hbm_outs
        + [VMEM] * (len(outs) - hbm_outs),
        scratch_shapes=scratch,
        input_output_aliases=aliases,
        compiler_params=pltpu.CompilerParams(vmem_limit_bytes=48 * 2**20),
        cost_estimate=pl.CostEstimate(flops=flops, bytes_accessed=2**20, transcendentals=0),
    )(*args)


def swap_all(arrays, axis, distances):
    size = lax.axis_size(axis)
    return [
        lax.ppermute(x, axis, [(i, i ^ d) for i in range(size)]) for x, d in zip(arrays, distances)
    ]


def per_device(queries, keys, values, grad_out):
    seq_count, head_count = lax.axis_size("seq"), lax.axis_size("head")
    rows, width = queries.shape
    assert rows == 4 * BLOCK and width == BLOCK
    fine_blocks = rows * seq_count // BLOCK
    top_level = (fine_blocks // 4).bit_length() - 1
    wides = wide_distances(seq_count)
    distances = seq_order(seq_count)

    def shape(*dims, dtype=BF16):
        return jax.ShapeDtypeStruct(dims, dtype)

    def f32(*dims):
        return pltpu.VMEM(dims, F32)

    payloads = [shape(2, BLOCK + REST if d in wides else BLOCK, width) for d in distances]
    arguments = [
        pltpu.with_memory_space_constraint(x, pltpu.HBM) for x in (queries, keys, values, grad_out)
    ]
    held, *sends = call(
        functools.partial(prep_kernel, seq_count),
        [shape(4, rows, width)] + payloads,
        [f32(rows, width), f32(rows // 2, width)] * 2 + [pltpu.SemaphoreType.DMA((4,))],
        arguments,
        in_hbm=4,
    )
    received = swap_all(sends, "seq", distances)

    unit_flops = 2 * BLOCK * BLOCK * width
    stats, *level_queries = call(
        fine_kernel,
        [shape(3, rows, width, dtype=F32)]
        + [shape(rows >> level, width) for level in range(1, top_level + 1)],
        [f32(rows >> level, width) for level in range(top_level)],
        (held,),
        flops=20 * unit_flops,
    )

    panel_rows = [(seq_count >> (level - 2)) * BLOCK for level in range(2, top_level + 1)]
    pools = [f32(BLOCK, width), f32(max(seq_count * BLOCK, rows), width)]
    for level in range(top_level - 1, -1, -1):
        pools += [f32(rows >> level, width)] * 3
    for level in range(top_level):
        pools += [f32(rows >> level, width)] * 2
    for level in range(top_level - 1, -1, -1):
        pools += [f32(rows >> level, width)]
    pools += [f32(BLOCK, width)] * 4
    main = call(
        functools.partial(main_kernel, seq_count, top_level),
        [shape(rows, width)]
        + payloads
        + [shape(3, rows, width, dtype=F32), shape(rows, width, dtype=F32)],
        [pltpu.VMEM((2, 2 * BLOCK, width), BF16), pltpu.VMEM((2, 4 * BLOCK, width), BF16)]
        + [pltpu.VMEM((2, r, width), BF16) for r in panel_rows]
        + [f32(2, r, width) for r in panel_rows]
        + pools,
        (held, stats, *level_queries, *received),
        flops=70 * unit_flops,
    )
    merged, sends, back, partial = main[0], main[1:seq_count], main[-2], main[-1]
    returned = swap_all(sends, "seq", distances)

    share = rows // head_count
    attended, local, grad_query = call(
        local_kernel,
        [shape(rows, width), shape(2, rows, width, dtype=F32), shape(rows, width)],
        [pltpu.SemaphoreType.DMA],
        (held, back, partial, merged),
        hbm_outs=1,
        flops=50 * unit_flops,
    )

    order = head_order(head_count)
    own, *parts = call(
        functools.partial(combine_kernel, seq_count, head_count),
        [
            shape(*((2,) if d in paired(head_count) else ()), 3, share, width)
            for d in [0] + order
        ],
        [f32(2, rows, width), f32(2, rows // 2, width), f32(2, rows // 4, width)],
        (grad_query, local, *returned),
    )
    parts = dict(zip(order, swap_all(parts, "head", order)))
    far = [parts[d][1] for d in order if d in paired(head_count)]
    late = swap_all(far, "head", [1] * len(far))
    last = [parts.pop(d) for d in last_heads(head_count)] + late
    grads = call(
        functools.partial(place_kernel, head_count),
        [shape(share, head_count * width)] * 3,
        [],
        (own, *parts.values()),
        flops=50 * unit_flops,
    )
    if last:
        grads = call(
            functools.partial(place_late_kernel, head_count),
            [shape(share, head_count * width)] * 3,
            [pltpu.SemaphoreType.DMA((len(last), 3))],
            (*grads, *last),
            in_hbm=3,
            hbm_outs=3,
            aliases={0: 0, 1: 1, 2: 2},
        )
    return (attended, *grads)


def solution(mesh):
    return jax.shard_map(
        per_device,
        mesh=mesh,
        in_specs=(P("seq", "head"),) * 4,
        out_specs=(P("seq", "head"),) + (P(("seq", "head"), None),) * 3,
        check_vma=False,
    )
```

```python
import functools

import jax
import jax.numpy as jnp
from jax import lax
from jax.experimental import pallas as pl
from jax.experimental.pallas import tpu as pltpu
from jax.sharding import PartitionSpec as P

BLOCK = 128
EDGE = BLOCK // 2
REST = 2 * BLOCK - EDGE
MASKED = -1e30
LOG2E = 1.4426950408889634
F32 = jnp.float32
BF16 = jnp.bfloat16
VMEM = pl.BlockSpec(memory_space=pltpu.VMEM)


def nt(a, b):
    return lax.dot_general(a, b, (((1,), (1,)), ((), ())), preferred_element_type=F32)


def nn(a, b):
    return lax.dot_general(a, b, (((1,), (0,)), ((), ())), preferred_element_type=F32)


def tn(a, b):
    return lax.dot_general(a, b, (((0,), (0,)), ((), ())), preferred_element_type=F32)


def pair_sum(x, scratch):
    rows = x.shape[0]
    scratch[:rows] = x
    return scratch[pl.ds(0, rows // 2, stride=2), :] + scratch[pl.ds(1, rows // 2, stride=2), :]


def coarse(x, scratch):
    return (pair_sum(x.astype(F32), scratch) * 0.5).astype(BF16)


def spread(x, scratch):
    rows = x.shape[0]
    scratch[pl.ds(0, rows, stride=2), :] = x
    scratch[pl.ds(1, rows, stride=2), :] = x
    return scratch[: 2 * rows]


def wide_distances(seq_count):
    return sorted({i ^ (i + 1) for i in range(seq_count - 1)})


def seq_order(seq_count):
    wides = wide_distances(seq_count)
    return wides[::-1] + [d for d in range(1, seq_count) if d not in wides]


def paired(head_count):
    return list(range(4, head_count - 2, 2))


def head_order(head_count):
    far = [d for d in (head_count - 2, head_count - 1) if d >= 4]
    return [d for d in paired(head_count) + far[:1] + [2] + far[1:] + [3, 1] if d < head_count]


def last_heads(head_count):
    return [d for d in head_order(head_count) if d in (1, 3, head_count - 1)]


def prep_kernel(seq_count, top_level, *refs):
    sources, refs = refs[:4], refs[4:]
    (held, stats), refs = refs[:2], refs[2:]
    queries, refs = refs[:top_level], refs[top_level:]
    sends, scratches, sems = refs[: seq_count - 1], refs[seq_count - 1 : -1], refs[-1]
    sends = dict(zip(seq_order(seq_count), sends))
    seq_index = lax.axis_index("seq")
    wides = wide_distances(seq_count)
    rows = held.shape[1]
    copies = [
        pltpu.make_async_copy(source, held.at[i], sems.at[i]) for i, source in enumerate(sources)
    ]
    for i in (1, 2, 0, 3):
        copies[i].start()
    for i in range(2):
        copies[1 + i].wait()
        ref = held.at[1 + i]
        level_1 = coarse(ref[...], scratches[2 * i])
        level_2 = coarse(level_1, scratches[2 * i + 1])
        for d in range(1, seq_count):
            out = sends[d]
            partner = seq_index ^ d
            if d not in wides:
                out[i] = level_2
                continue

            @pl.when(partner == seq_index + 1)
            def _():
                out[i, :BLOCK] = ref[rows - BLOCK :]
                out[i, BLOCK:] = level_1[:REST]

            @pl.when(partner == seq_index - 1)
            def _():
                out[i, :BLOCK] = ref[:BLOCK]
                out[i, BLOCK:] = level_1[EDGE:]

            @pl.when((partner != seq_index + 1) & (partner != seq_index - 1))
            def _():
                out[i, :BLOCK] = level_2
                out[i, BLOCK:] = level_1[:REST]

    copies[0].wait()

    @pl.when(goes_first())
    def _():
        fine_work(held, stats, queries, scratches[4:])

    copies[3].wait()


def slots_of(block, block_count):
    parent, odd = block // 2, block % 2
    if block_count == 4:
        first = parent == 0
        return [
            (jnp.where(first, 3, 0), None),
            (jnp.where(first, 2, 1), jnp.where(first, odd == 0, odd == 1)),
        ]
    near = jnp.where(odd == 0, 2 * parent + 2, 2 * parent - 1)
    raw = [2 * parent - 2, near, 2 * parent + 3]
    return [(jnp.clip(j, 0, block_count - 1), (j >= 0) & (j < block_count)) for j in raw]


def across(x, width):
    return jnp.concatenate([x] * (width // x.shape[1]), axis=1)


def lanes(column):
    return jnp.broadcast_to(column, (column.shape[0], BLOCK))


def row_max(x):
    return lanes(jnp.max(x, axis=-1, keepdims=True))


def row_sum(x):
    return lanes(jnp.sum(x, axis=-1, keepdims=True))


def total_of(parts):
    return functools.reduce(jnp.add, parts)


def rows_of(block, count=1):
    return slice(block * BLOCK, (block + count) * BLOCK)


def own_window(a, blocks):
    return max(a - 1, 0), min(a + 2, blocks)


def fine_work(held, stats, queries, scratches):
    blocks, width = held.shape[1] // BLOCK, held.shape[2]
    factor = width ** (-0.5) * LOG2E
    for a in range(blocks):
        lo, hi = own_window(a, blocks)
        window = rows_of(lo, hi - lo)
        scores = nt(held[0, rows_of(a)], held[1, window]) * factor
        peak = row_max(scores)
        exps = jnp.exp2(scores - across(peak, scores.shape[1]))
        stats[0, rows_of(a)] = peak
        stats[1, rows_of(a)] = row_sum(exps)
        stats[2, rows_of(a)] = nn(exps.astype(BF16), held[2, window])
    query = held[0]
    for ref, scratch in zip(queries, scratches):
        query = coarse(query, scratch)
        ref[...] = query


def goes_first():
    return lax.axis_index("head") % 2 == 0


def fine_kernel(held, *refs):
    count = len(refs) // 3
    done, (stats, *queries), scratches = refs[: count + 1], refs[count + 1 : -count], refs[-count:]

    @pl.when(goes_first())
    def _():
        for ref, source in zip((stats, *queries), done):
            ref[...] = source[...]

    @pl.when(~goes_first())
    def _():
        fine_work(held, stats, queries, scratches)


def main_kernel(seq_count, top_level, *refs):
    refs = list(refs)

    def take(count):
        taken = refs[:count]
        del refs[:count]
        return taken

    held, stats = take(2)
    query_refs = take(top_level)
    received = dict(zip(seq_order(seq_count), take(seq_count - 1)))
    (attended_ref,) = take(1)
    sends = dict(zip(seq_order(seq_count), take(seq_count - 1)))
    back, partial_ref = take(2)
    panels = take(top_level - 1 if top_level > 2 else 0)
    panel_grads = take(len(panels))
    pools = refs

    def pool():
        return pools.pop(0)

    seq_index = lax.axis_index("seq")
    wides = wide_distances(seq_count)
    rows, width = held.shape[1:]
    blocks = rows // BLOCK
    scale = width ** (-0.5)
    factor = scale * LOG2E
    has_prev, has_next = seq_index > 0, seq_index < seq_count - 1

    odd = seq_index % 2 == 1
    further = wides[1:] or wides

    def is_neighbour(d):
        return jnp.abs((seq_index ^ d) - seq_index) == 1

    def by_side(near, far):
        return jnp.where(odd, near, far), jnp.where(odd, far, near)

    edges, nears = [], []
    for i in range(2):
        far = received[further[0]][i]
        for d in further[1:]:
            far = jnp.where(is_neighbour(d), received[d][i], far)
        before, after = by_side(received[1][i], far)
        edges.append((before[:BLOCK], after[:BLOCK]))
        nears.append(
            jnp.concatenate(
                [
                    before[BLOCK:],
                    coarse(before[:BLOCK], pool()),
                    coarse(after[:BLOCK], pool()),
                    after[BLOCK:],
                ],
                axis=0,
            )
        )

    def window(lo, hi, valid):
        return nears[0][rows_of(lo, hi - lo)], nears[1][rows_of(lo, hi - lo)], valid, (lo, hi)

    level_pieces = [
        [
            [(edges[0][side], edges[1][side], valid, (side, side + 1))]
            for side, valid in enumerate((has_prev, has_next))
        ],
        [
            [window(0, 1, has_prev), window(2, 4, has_next)],
            [window(0, 2, has_prev), window(3, 4, has_next)],
        ],
    ]
    if top_level == 2:
        pieces = []
        for d in range(2, seq_count):
            valid = ~is_neighbour(d) if d in wides else None
            pieces.append((received[d][0, :BLOCK], received[d][1, :BLOCK], valid, d))
        level_pieces.append([pieces])
    else:
        for panel in panels:
            panel[...] = jnp.zeros(panel.shape, BF16)
        for d in range(2, seq_count):
            at = pl.ds(pl.multiple_of((seq_index ^ d) * BLOCK, BLOCK), BLOCK)
            for i in range(2):
                panels[0][i, at] = received[d][i, :BLOCK]
        panel_scratch = pool()
        for level in range(2, top_level + 1):
            panel, pieces = panels[level - 2], []
            for i in range(2):
                if level > 2:
                    panel[i] = coarse(panels[level - 3][i], panel_scratch)
            for index, valid in slots_of(seq_index >> (level - 2), seq_count >> (level - 2)):
                at = pl.ds(pl.multiple_of(index * BLOCK, BLOCK), BLOCK)
                pieces.append((panel[0, at], panel[1, at], valid, at))
            level_pieces.append([pieces])
    level_queries = [[held[0, rows_of(0)], held[0, rows_of(blocks - 1)]]]
    for level in range(1, top_level + 1):
        query = query_refs[level - 1][...]
        step = query.shape[0] // len(level_pieces[level])
        level_queries.append(
            [query[a * step : (a + 1) * step] for a in range(len(level_pieces[level]))]
        )

    def unit(query, pieces, before=None):
        scores = []
        for key, _, valid, _ in pieces:
            score = nt(query, key) * factor
            scores.append(score if valid is None else jnp.where(valid, score, MASKED))
        peak = functools.reduce(jnp.maximum, [row_max(score) for score in scores])
        if before is not None:
            peak = jnp.maximum(peak, before[0])
        exps = [jnp.exp2(score - across(peak, score.shape[1])) for score in scores]
        rounded = [e.astype(BF16) for e in exps]
        ones = jnp.ones((BLOCK, width), BF16)
        both = []
        for r, piece in zip(rounded, pieces):
            count = piece[1].shape[0] // BLOCK
            both.append(nn(r, jnp.concatenate([piece[1], jnp.concatenate([ones] * count, axis=0)], axis=1)))
        both = total_of(both)
        sums, total = both[:, :width], both[:, width:]
        if before is not None:
            keep = jnp.exp2(before[0] - peak)
            total, sums = total + keep * before[1], sums + keep * before[2]
        return peak, total, sums, exps, rounded

    def before_of(block):
        return [stats[w, rows_of(block)] for w in range(3)]

    level_units = [
        [
            unit(query, pieces, before_of(block))
            for query, pieces, block in zip(level_queries[0], level_pieces[0], (0, blocks - 1))
        ]
    ]
    for level in range(1, top_level + 1):
        level_units.append(
            [unit(q, pieces) for q, pieces in zip(level_queries[level], level_pieces[level])]
        )

    def stacked(level, which):
        units = [u[which] for u in level_units[level]]
        if level == 0:
            units = [units[0], stats[which, rows_of(1, blocks - 2)], units[1]]
        return jnp.concatenate(units, axis=0)

    run = [stacked(top_level, w) for w in range(3)]
    own_factors, run_factors = [None] * top_level, [None] * top_level
    for level in range(top_level - 1, -1, -1):
        up_peak, up_total, up_sums = [spread(x, pool()) for x in run]
        peak, total, sums = [stacked(level, w) for w in range(3)]
        both = jnp.maximum(peak, up_peak)
        own = jnp.exp2(peak - both)
        up = 2.0 * jnp.exp2(up_peak - both)
        own_factors[level], run_factors[level] = own, up
        run = [both, own * total + up * up_total, own * sums + up * up_sums]

    inverse = 1.0 / run[1]
    attended = run[2] * inverse
    attended_ref[...] = attended.astype(BF16)

    cot = held[3].astype(F32)
    grad, shift = cot * inverse, row_sum(cot * attended) * inverse
    level_grads = []
    for level in range(top_level):
        level_grads.append((own_factors[level] * grad, own_factors[level] * shift))
        grad = pair_sum(run_factors[level] * grad, pool())
        shift = pair_sum(run_factors[level] * shift, pool())
    level_grads.append((grad, shift))
    back[0] = stacked(0, 0)
    back[1], back[2] = level_grads[0]

    for panel_grad in panel_grads:
        panel_grad[...] = jnp.zeros(panel_grad.shape, F32)

    device_grads = {d: [None, None] for d in range(2, seq_count)}
    grad_queries = []
    parts_of = [[[[] for _ in range(4)] for _ in range(2)] for _ in range(2)]
    for level in range(top_level, -1, -1):
        grad, shift = level_grads[level]
        step = level_queries[level][0].shape[0]
        level_parts = []
        for a, (query, pieces) in enumerate(zip(level_queries[level], level_pieces[level])):
            at = a if level > 0 else a * (blocks - 1)
            cut = slice(at * step, (at + 1) * step)
            grad_rounded = grad[cut].astype(BF16)
            grad_scaled = (grad[cut] * scale).astype(BF16)
            shift_scaled = shift[cut] * scale
            exps, rounded = level_units[level][a][3:]
            query_parts = []
            for piece, e, r in zip(pieces, exps, rounded):
                key, value, _, where = piece
                score_grad = nt(grad_scaled, value) - across(shift_scaled, e.shape[1])
                score_grad = (e * score_grad).astype(BF16)
                query_parts.append(nn(score_grad, key))
                outs = tn(score_grad, query), tn(r, grad_rounded)
                for i in range(2):
                    if level >= 2 and top_level == 2:
                        device_grads[where][i] = outs[i]
                        continue
                    if level >= 2:
                        panel_grads[level - 2][i, where] += outs[i]
                        continue
                    lo, hi = where
                    for b in range(lo, hi):
                        parts_of[level][i][b].append(outs[i][rows_of(b - lo)])
            level_parts.append(total_of(query_parts))
        grad_queries.append(level_parts)

    run_grad = grad_queries[0][0]
    for level_parts in grad_queries[1:-1]:
        run_grad = jnp.concatenate(level_parts, axis=0) + 0.5 * spread(run_grad, pool())
    partial_ref[...] = 0.5 * spread(run_grad, pool())
    for a, block in enumerate((0, blocks - 1)):
        partial_ref[rows_of(block)] += grad_queries[-1][a]

    if top_level > 2:
        for level in range(top_level, 2, -1):
            for i in range(2):
                panel_grads[level - 3][i] += 0.5 * spread(panel_grads[level - 2][i], panel_scratch)
        for d in device_grads:
            at = pl.ds(pl.multiple_of((seq_index ^ d) * BLOCK, BLOCK), BLOCK)
            device_grads[d] = [panel_grads[0][i, at] for i in range(2)]

    for i in range(2):
        near_grads = [total_of(p) for p in parts_of[1][i]]
        edge_grads = [total_of(p) for p in parts_of[0][i][:2]]
        before = [
            edge_grads[0] + 0.5 * spread(near_grads[1][EDGE:], pool()),
            near_grads[0],
            near_grads[1][:EDGE],
        ]
        after = [
            edge_grads[1] + 0.5 * spread(near_grads[2][:EDGE], pool()),
            near_grads[2][EDGE:],
            near_grads[3],
        ]
        before, after = [jnp.concatenate(p, axis=0).astype(BF16) for p in (before, after)]
        sends[1][i] = jnp.where(odd, before, after)
        far = jnp.where(odd, after, before)
        for d in range(2, seq_count):
            device_grad = device_grads[d][i].astype(BF16)
            if d in wides:
                sends[d][i, :BLOCK] = jnp.where(is_neighbour(d), far[:BLOCK], device_grad)
                sends[d][i, BLOCK:] = far[BLOCK:]
            else:
                sends[d][i] = device_grad


def local_kernel(held, back, partial_ref, merged, attended_hbm, local_ref, grad_query_ref, sem):
    copy = pltpu.make_async_copy(merged, attended_hbm, sem)
    copy.start()
    blocks, width = held.shape[1] // BLOCK, held.shape[2]
    scale = width ** (-0.5)
    factor = scale * LOG2E
    parts = [[[] for _ in range(blocks)] for _ in range(2)]
    for a in range(blocks):
        lo, hi = own_window(a, blocks)
        window = rows_of(lo, hi - lo)
        query, key, value = held[0, rows_of(a)], held[1, window], held[2, window]
        peak, grad, shift = [back[w, rows_of(a)] for w in range(3)]
        wide = key.shape[0]
        exps = jnp.exp2(nt(query, key) * factor - across(peak, wide))
        score_grad = nt((grad * scale).astype(BF16), value) - across(shift * scale, wide)
        score_grad = (exps * score_grad).astype(BF16)
        grad_query_ref[rows_of(a)] = (nn(score_grad, key) + partial_ref[rows_of(a)]).astype(BF16)
        outs = tn(score_grad, query), tn(exps.astype(BF16), grad.astype(BF16))
        for i in range(2):
            for b in range(lo, hi):
                parts[i][b].append(outs[i][rows_of(b - lo)])
    for i in range(2):
        for b in range(blocks):
            local_ref[i, rows_of(b)] = total_of(parts[i][b])
    copy.wait()


def combine_kernel(seq_count, head_count, grad_query_ref, local_ref, *refs):
    received, refs = refs[: seq_count - 1], refs[seq_count - 1 :]
    received = dict(zip(seq_order(seq_count), received))
    outs, refs = refs[:-3], refs[-3:]
    outs = dict(zip([0] + head_order(head_count), outs))
    total, level_1, level_2 = refs
    seq_index, head_index = lax.axis_index("seq"), lax.axis_index("head")
    wides = wide_distances(seq_count)
    rows, width = local_ref.shape[1:]
    share = rows // head_count

    level_1[...] = jnp.zeros(level_1.shape, F32)
    level_2[...] = jnp.zeros(level_2.shape, F32)
    for i in range(2):
        total[i] = local_ref[i]
    for d in range(1, seq_count):
        got = received[d]
        partner = seq_index ^ d
        if d not in wides:
            for i in range(2):
                level_2[i] += got[i].astype(F32)
            continue

        @pl.when(partner == seq_index - 1)
        def _():
            for i in range(2):
                total[i, :BLOCK] += got[i, :BLOCK].astype(F32)
                level_1[i, EDGE:] += got[i, BLOCK:].astype(F32)

        @pl.when(partner == seq_index + 1)
        def _():
            for i in range(2):
                total[i, rows - BLOCK :] += got[i, :BLOCK].astype(F32)
                level_1[i, :REST] += got[i, BLOCK:].astype(F32)

        @pl.when((partner != seq_index + 1) & (partner != seq_index - 1))
        def _():
            for i in range(2):
                level_2[i] += got[i, :BLOCK].astype(F32)

    for i in range(2):
        half = level_2[i] * 0.5
        for phase in range(2):
            level_1[i, pl.ds(phase, half.shape[0], stride=2), :] += half
        half = level_1[i] * 0.5
        for phase in range(2):
            total[i, pl.ds(phase, half.shape[0], stride=2), :] += half
    for d in range(head_count):
        at = pl.ds(pl.multiple_of((head_index ^ d) * share, share), share)
        out = outs[d & ~1].at[d & 1] if d & ~1 in paired(head_count) else outs[d]
        out[0] = grad_query_ref[at, :]
        out[1] = total[0, at].astype(BF16)
        out[2] = total[1, at].astype(BF16)


def place_kernel(head_count, *refs):
    parts, outs = refs[:-3], refs[-3:]
    head_index = lax.axis_index("head")
    width = parts[0].shape[-1]
    first = [d for d in head_order(head_count) if d not in last_heads(head_count)]
    for d, part in zip([0] + first, parts):
        at = pl.ds(pl.multiple_of((head_index ^ d) * width, width), width)
        for i in range(3):
            outs[i][:, at] = part[0, i] if d in paired(head_count) else part[i]


def place_late_kernel(head_count, *refs):
    parts, outs, sems = refs[3:-4], refs[-4:-1], refs[-1]
    head_index = lax.axis_index("head")
    width = parts[0].shape[-1]
    copies = []
    far = [d + 1 for d in head_order(head_count) if d in paired(head_count)]
    for k, (d, part) in enumerate(zip(last_heads(head_count) + far, parts)):
        at = pl.ds(pl.multiple_of((head_index ^ d) * width, width), width)
        for i in range(3):
            copies.append(pltpu.make_async_copy(part.at[i], outs[i].at[:, at], sems.at[k, i]))
            copies[-1].start()
    for copy in copies:
        copy.wait()


def call(kernel, outs, scratch, args, in_hbm=0, hbm_outs=0, aliases={}, flops=0):
    return pl.pallas_call(
        kernel,
        out_shape=outs,
        in_specs=[pl.BlockSpec(memory_space=pltpu.HBM)] * in_hbm + [VMEM] * (len(args) - in_hbm),
        out_specs=[pl.BlockSpec(memory_space=pltpu.HBM)] * hbm_outs
        + [VMEM] * (len(outs) - hbm_outs),
        scratch_shapes=scratch,
        input_output_aliases=aliases,
        compiler_params=pltpu.CompilerParams(vmem_limit_bytes=48 * 2**20),
        cost_estimate=pl.CostEstimate(flops=flops, bytes_accessed=2**20, transcendentals=0),
    )(*args)


def swap_all(arrays, axis, distances):
    size = lax.axis_size(axis)
    return [
        lax.ppermute(x, axis, [(i, i ^ d) for i in range(size)]) for x, d in zip(arrays, distances)
    ]


def per_device(queries, keys, values, grad_out):
    seq_count, head_count = lax.axis_size("seq"), lax.axis_size("head")
    rows, width = queries.shape
    assert rows == 4 * BLOCK and width == BLOCK
    fine_blocks = rows * seq_count // BLOCK
    top_level = (fine_blocks // 4).bit_length() - 1
    wides = wide_distances(seq_count)
    distances = seq_order(seq_count)

    def shape(*dims, dtype=BF16):
        return jax.ShapeDtypeStruct(dims, dtype)

    def f32(*dims):
        return pltpu.VMEM(dims, F32)

    payloads = [shape(2, BLOCK + REST if d in wides else BLOCK, width) for d in distances]
    arguments = [
        pltpu.with_memory_space_constraint(x, pltpu.HBM) for x in (queries, keys, values, grad_out)
    ]
    fine_shapes = [shape(3, rows, width, dtype=F32)]
    fine_shapes += [shape(rows >> level, width) for level in range(1, top_level + 1)]
    fine_scratch = [f32(rows >> level, width) for level in range(top_level)]
    held, *outs = call(
        functools.partial(prep_kernel, seq_count, top_level),
        [shape(4, rows, width)] + fine_shapes + payloads,
        [f32(rows, width), f32(rows // 2, width)] * 2
        + fine_scratch
        + [pltpu.SemaphoreType.DMA((4,))],
        arguments,
        in_hbm=4,
    )
    done, sends = outs[: 1 + top_level], outs[1 + top_level :]
    received = swap_all(sends, "seq", distances)

    unit_flops = 2 * BLOCK * BLOCK * width
    stats, *level_queries = call(
        fine_kernel, fine_shapes, fine_scratch, (held, *done), flops=20 * unit_flops
    )

    panel_rows = [(seq_count >> (level - 2)) * BLOCK for level in range(2, top_level + 1)]
    panel_rows = panel_rows if top_level > 2 else []
    pools = [f32(BLOCK, width)] * 4 + [f32(r, width) for r in panel_rows[:1]]
    for level in range(top_level - 1, -1, -1):
        pools += [f32(rows >> level, width)] * 3
    for level in range(top_level):
        pools += [f32(rows >> level, width)] * 2
    for level in range(top_level - 1, -1, -1):
        pools += [f32(rows >> level, width)]
    pools += [f32(BLOCK, width)] * 4
    main = call(
        functools.partial(main_kernel, seq_count, top_level),
        [shape(rows, width)]
        + payloads
        + [shape(3, rows, width, dtype=F32), shape(rows, width, dtype=F32)],
        [pltpu.VMEM((2, r, width), BF16) for r in panel_rows]
        + [f32(2, r, width) for r in panel_rows]
        + pools,
        (held, stats, *level_queries, *received),
        flops=70 * unit_flops,
    )
    merged, sends, back, partial = main[0], main[1:seq_count], main[-2], main[-1]
    returned = swap_all(sends, "seq", distances)

    share = rows // head_count
    attended, local, grad_query = call(
        local_kernel,
        [shape(rows, width), shape(2, rows, width, dtype=F32), shape(rows, width)],
        [pltpu.SemaphoreType.DMA],
        (held, back, partial, merged),
        hbm_outs=1,
        flops=50 * unit_flops,
    )

    order = head_order(head_count)
    own, *parts = call(
        functools.partial(combine_kernel, seq_count, head_count),
        [
            shape(*((2,) if d in paired(head_count) else ()), 3, share, width)
            for d in [0] + order
        ],
        [f32(2, rows, width), f32(2, rows // 2, width), f32(2, rows // 4, width)],
        (grad_query, local, *returned),
    )
    parts = dict(zip(order, swap_all(parts, "head", order)))
    far = [parts[d][1] for d in order if d in paired(head_count)]
    late = swap_all(far, "head", [1] * len(far))
    last = [parts.pop(d) for d in last_heads(head_count)] + late
    grads = call(
        functools.partial(place_kernel, head_count),
        [shape(share, head_count * width)] * 3,
        [],
        (own, *parts.values()),
        flops=50 * unit_flops,
    )
    if last:
        grads = call(
            functools.partial(place_late_kernel, head_count),
            [shape(share, head_count * width)] * 3,
            [pltpu.SemaphoreType.DMA((len(last), 3))],
            (*grads, *last),
            in_hbm=3,
            hbm_outs=3,
            aliases={0: 0, 1: 1, 2: 2},
        )
    return (attended, *grads)


def solution(mesh):
    return jax.shard_map(
        per_device,
        mesh=mesh,
        in_specs=(P("seq", "head"),) * 4,
        out_specs=(P("seq", "head"),) + (P(("seq", "head"), None),) * 3,
        check_vma=False,
    )
```

```python
import functools

import jax
import jax.numpy as jnp
from jax import lax
from jax.experimental import pallas as pl
from jax.experimental.pallas import tpu as pltpu
from jax.sharding import PartitionSpec as P

BLOCK = 128
EDGE = BLOCK // 2
REST = 2 * BLOCK - EDGE
MASKED = -1e30
LOG2E = 1.4426950408889634
F32 = jnp.float32
BF16 = jnp.bfloat16
VMEM = pl.BlockSpec(memory_space=pltpu.VMEM)


def nt(a, b):
    return lax.dot_general(a, b, (((1,), (1,)), ((), ())), preferred_element_type=F32)


def nn(a, b):
    return lax.dot_general(a, b, (((1,), (0,)), ((), ())), preferred_element_type=F32)


def tn(a, b):
    return lax.dot_general(a, b, (((0,), (0,)), ((), ())), preferred_element_type=F32)


def pair_sum(x, scratch):
    rows = x.shape[0]
    scratch[:rows] = x
    return scratch[pl.ds(0, rows // 2, stride=2), :] + scratch[pl.ds(1, rows // 2, stride=2), :]


def coarse(x, scratch):
    return (pair_sum(x.astype(F32), scratch) * 0.5).astype(BF16)


def spread(x, scratch):
    rows = x.shape[0]
    scratch[pl.ds(0, rows, stride=2), :] = x
    scratch[pl.ds(1, rows, stride=2), :] = x
    return scratch[: 2 * rows]


def wide_distances(seq_count):
    return sorted({i ^ (i + 1) for i in range(seq_count - 1)})


def seq_order(seq_count):
    wides = wide_distances(seq_count)
    return wides[::-1] + [d for d in range(1, seq_count) if d not in wides]


def paired(head_count):
    return list(range(4, head_count - 2, 2))


def head_order(head_count):
    far = [d for d in (head_count - 2, head_count - 1) if d >= 4]
    return [d for d in paired(head_count) + far[:1] + [2] + far[1:] + [3, 1] if d < head_count]


def last_heads(head_count):
    return [d for d in head_order(head_count) if d in (1, 3, head_count - 1)]


def prep_kernel(seq_count, top_level, *refs):
    sources, refs = refs[:4], refs[4:]
    (held, stats), refs = refs[:2], refs[2:]
    queries, refs = refs[:top_level], refs[top_level:]
    sends, scratches, sems = refs[: seq_count - 1], refs[seq_count - 1 : -1], refs[-1]
    sends = dict(zip(seq_order(seq_count), sends))
    seq_index = lax.axis_index("seq")
    wides = wide_distances(seq_count)
    rows = held.shape[1]
    copies = [
        pltpu.make_async_copy(source, held.at[i], sems.at[i]) for i, source in enumerate(sources)
    ]
    for i in (1, 2, 0, 3):
        copies[i].start()
    for i in range(2):
        copies[1 + i].wait()
        ref = held.at[1 + i]
        level_1 = coarse(ref[...], scratches[2 * i])
        level_2 = coarse(level_1, scratches[2 * i + 1])
        for d in range(1, seq_count):
            out = sends[d]
            partner = seq_index ^ d
            if d not in wides:
                out[i] = level_2
                continue

            @pl.when(partner == seq_index + 1)
            def _():
                out[i, :BLOCK] = ref[rows - BLOCK :]
                out[i, BLOCK:] = level_1[:REST]

            @pl.when(partner == seq_index - 1)
            def _():
                out[i, :BLOCK] = ref[:BLOCK]
                out[i, BLOCK:] = level_1[EDGE:]

            @pl.when((partner != seq_index + 1) & (partner != seq_index - 1))
            def _():
                out[i, :BLOCK] = level_2
                out[i, BLOCK:] = level_1[:REST]

    copies[0].wait()

    @pl.when(goes_first())
    def _():
        fine_work(held, stats, queries, scratches[4:])

    copies[3].wait()


def slots_of(block, block_count):
    parent, odd = block // 2, block % 2
    if block_count == 4:
        first = parent == 0
        return [
            (jnp.where(first, 3, 0), None),
            (jnp.where(first, 2, 1), jnp.where(first, odd == 0, odd == 1)),
        ]
    near = jnp.where(odd == 0, 2 * parent + 2, 2 * parent - 1)
    raw = [2 * parent - 2, near, 2 * parent + 3]
    return [(jnp.clip(j, 0, block_count - 1), (j >= 0) & (j < block_count)) for j in raw]


def across(x, width):
    return jnp.concatenate([x] * (width // x.shape[1]), axis=1)


def lanes(column):
    return jnp.broadcast_to(column, (column.shape[0], BLOCK))


def row_max(x):
    return lanes(jnp.max(x, axis=-1, keepdims=True))


def row_sum(x):
    return lanes(jnp.sum(x, axis=-1, keepdims=True))


def total_of(parts):
    return functools.reduce(jnp.add, parts)


def rows_of(block, count=1):
    return slice(block * BLOCK, (block + count) * BLOCK)


def own_window(a, blocks):
    return max(a - 1, 0), min(a + 2, blocks)


def fine_work(held, stats, queries, scratches):
    blocks, width = held.shape[1] // BLOCK, held.shape[2]
    factor = width ** (-0.5) * LOG2E

    @pl.loop(0, blocks)
    def _(a):
        lo = jnp.clip(a - 1, 0, blocks - 3)
        own = pl.ds(pl.multiple_of(a * BLOCK, BLOCK), BLOCK)
        window = pl.ds(pl.multiple_of(lo * BLOCK, BLOCK), 3 * BLOCK)
        scores = nt(held[0, own], held[1, window]) * factor
        parts = [
            jnp.where(jnp.abs(lo + b - a) <= 1, scores[:, rows_of(b)], MASKED) for b in range(3)
        ]
        scores = jnp.concatenate(parts, axis=1)
        peak = row_max(scores)
        exps = jnp.exp2(scores - across(peak, scores.shape[1]))
        stats[0, own] = peak
        stats[1, own] = row_sum(exps)
        stats[2, own] = nn(exps.astype(BF16), held[2, window])

    query = held[0]
    for ref, scratch in zip(queries, scratches):
        query = coarse(query, scratch)
        ref[...] = query


def goes_first():
    return lax.axis_index("head") % 2 == 0


def fine_kernel(held, *refs):
    count = len(refs) // 3
    done, (stats, *queries), scratches = refs[: count + 1], refs[count + 1 : -count], refs[-count:]

    @pl.when(goes_first())
    def _():
        for ref, source in zip((stats, *queries), done):
            ref[...] = source[...]

    @pl.when(~goes_first())
    def _():
        fine_work(held, stats, queries, scratches)


def main_kernel(seq_count, top_level, *refs):
    refs = list(refs)

    def take(count):
        taken = refs[:count]
        del refs[:count]
        return taken

    held, stats = take(2)
    query_refs = take(top_level)
    received = dict(zip(seq_order(seq_count), take(seq_count - 1)))
    (attended_ref,) = take(1)
    sends = dict(zip(seq_order(seq_count), take(seq_count - 1)))
    back, partial_ref = take(2)
    panels = take(top_level - 1 if top_level > 2 else 0)
    panel_grads = take(len(panels))
    pools = refs

    def pool():
        return pools.pop(0)

    seq_index = lax.axis_index("seq")
    wides = wide_distances(seq_count)
    rows, width = held.shape[1:]
    blocks = rows // BLOCK
    scale = width ** (-0.5)
    factor = scale * LOG2E
    has_prev, has_next = seq_index > 0, seq_index < seq_count - 1

    odd = seq_index % 2 == 1
    further = wides[1:] or wides

    def is_neighbour(d):
        return jnp.abs((seq_index ^ d) - seq_index) == 1

    def by_side(near, far):
        return jnp.where(odd, near, far), jnp.where(odd, far, near)

    edges, nears = [], []
    for i in range(2):
        far = received[further[0]][i]
        for d in further[1:]:
            far = jnp.where(is_neighbour(d), received[d][i], far)
        before, after = by_side(received[1][i], far)
        edges.append((before[:BLOCK], after[:BLOCK]))
        nears.append(
            jnp.concatenate(
                [
                    before[BLOCK:],
                    coarse(before[:BLOCK], pool()),
                    coarse(after[:BLOCK], pool()),
                    after[BLOCK:],
                ],
                axis=0,
            )
        )

    def window(lo, hi, valid):
        return nears[0][rows_of(lo, hi - lo)], nears[1][rows_of(lo, hi - lo)], valid, (lo, hi)

    level_pieces = [
        [
            [(edges[0][side], edges[1][side], valid, (side, side + 1))]
            for side, valid in enumerate((has_prev, has_next))
        ],
        [
            [window(0, 1, has_prev), window(2, 4, has_next)],
            [window(0, 2, has_prev), window(3, 4, has_next)],
        ],
    ]
    if top_level == 2:
        pieces = []
        for d in range(2, seq_count):
            valid = ~is_neighbour(d) if d in wides else None
            pieces.append((received[d][0, :BLOCK], received[d][1, :BLOCK], valid, d))
        level_pieces.append([pieces])
    else:
        for panel in panels:
            panel[...] = jnp.zeros(panel.shape, BF16)
        for d in range(2, seq_count):
            at = pl.ds(pl.multiple_of((seq_index ^ d) * BLOCK, BLOCK), BLOCK)
            for i in range(2):
                panels[0][i, at] = received[d][i, :BLOCK]
        panel_scratch = pool()
        for level in range(2, top_level + 1):
            panel, pieces = panels[level - 2], []
            for i in range(2):
                if level > 2:
                    panel[i] = coarse(panels[level - 3][i], panel_scratch)
            for index, valid in slots_of(seq_index >> (level - 2), seq_count >> (level - 2)):
                at = pl.ds(pl.multiple_of(index * BLOCK, BLOCK), BLOCK)
                pieces.append((panel[0, at], panel[1, at], valid, at))
            level_pieces.append([pieces])
    level_queries = [[held[0, rows_of(0)], held[0, rows_of(blocks - 1)]]]
    for level in range(1, top_level + 1):
        query = query_refs[level - 1][...]
        step = query.shape[0] // len(level_pieces[level])
        level_queries.append(
            [query[a * step : (a + 1) * step] for a in range(len(level_pieces[level]))]
        )

    def unit(query, pieces, before=None):
        scores = []
        for key, _, valid, _ in pieces:
            score = nt(query, key) * factor
            scores.append(score if valid is None else jnp.where(valid, score, MASKED))
        peak = functools.reduce(jnp.maximum, [row_max(score) for score in scores])
        if before is not None:
            peak = jnp.maximum(peak, before[0])
        exps = [jnp.exp2(score - across(peak, score.shape[1])) for score in scores]
        rounded = [e.astype(BF16) for e in exps]
        ones = jnp.ones((BLOCK, width), BF16)
        both = []
        for r, piece in zip(rounded, pieces):
            count = piece[1].shape[0] // BLOCK
            both.append(nn(r, jnp.concatenate([piece[1], jnp.concatenate([ones] * count, axis=0)], axis=1)))
        both = total_of(both)
        sums, total = both[:, :width], both[:, width:]
        if before is not None:
            keep = jnp.exp2(before[0] - peak)
            total, sums = total + keep * before[1], sums + keep * before[2]
        return peak, total, sums, exps, rounded

    def before_of(block):
        return [stats[w, rows_of(block)] for w in range(3)]

    level_units = [
        [
            unit(query, pieces, before_of(block))
            for query, pieces, block in zip(level_queries[0], level_pieces[0], (0, blocks - 1))
        ]
    ]
    for level in range(1, top_level + 1):
        level_units.append(
            [unit(q, pieces) for q, pieces in zip(level_queries[level], level_pieces[level])]
        )

    def stacked(level, which):
        units = [u[which] for u in level_units[level]]
        if level == 0:
            units = [units[0], stats[which, rows_of(1, blocks - 2)], units[1]]
        return jnp.concatenate(units, axis=0)

    run = [stacked(top_level, w) for w in range(3)]
    own_factors, run_factors = [None] * top_level, [None] * top_level
    for level in range(top_level - 1, -1, -1):
        up_peak, up_total, up_sums = [spread(x, pool()) for x in run]
        peak, total, sums = [stacked(level, w) for w in range(3)]
        both = jnp.maximum(peak, up_peak)
        own = jnp.exp2(peak - both)
        up = 2.0 * jnp.exp2(up_peak - both)
        own_factors[level], run_factors[level] = own, up
        run = [both, own * total + up * up_total, own * sums + up * up_sums]

    inverse = 1.0 / run[1]
    attended = run[2] * inverse
    attended_ref[...] = attended.astype(BF16)

    cot = held[3].astype(F32)
    grad, shift = cot * inverse, row_sum(cot * attended) * inverse
    level_grads = []
    for level in range(top_level):
        level_grads.append((own_factors[level] * grad, own_factors[level] * shift))
        grad = pair_sum(run_factors[level] * grad, pool())
        shift = pair_sum(run_factors[level] * shift, pool())
    level_grads.append((grad, shift))
    back[0] = stacked(0, 0)
    back[1], back[2] = level_grads[0]

    for panel_grad in panel_grads:
        panel_grad[...] = jnp.zeros(panel_grad.shape, F32)

    device_grads = {d: [None, None] for d in range(2, seq_count)}
    grad_queries = []
    parts_of = [[[[] for _ in range(4)] for _ in range(2)] for _ in range(2)]
    for level in range(top_level, -1, -1):
        grad, shift = level_grads[level]
        step = level_queries[level][0].shape[0]
        level_parts = []
        for a, (query, pieces) in enumerate(zip(level_queries[level], level_pieces[level])):
            at = a if level > 0 else a * (blocks - 1)
            cut = slice(at * step, (at + 1) * step)
            grad_rounded = grad[cut].astype(BF16)
            grad_scaled = (grad[cut] * scale).astype(BF16)
            shift_scaled = shift[cut] * scale
            exps, rounded = level_units[level][a][3:]
            query_parts = []
            for piece, e, r in zip(pieces, exps, rounded):
                key, value, _, where = piece
                score_grad = nt(grad_scaled, value) - across(shift_scaled, e.shape[1])
                score_grad = (e * score_grad).astype(BF16)
                query_parts.append(nn(score_grad, key))
                outs = tn(score_grad, query), tn(r, grad_rounded)
                for i in range(2):
                    if level >= 2 and top_level == 2:
                        device_grads[where][i] = outs[i]
                        continue
                    if level >= 2:
                        panel_grads[level - 2][i, where] += outs[i]
                        continue
                    lo, hi = where
                    for b in range(lo, hi):
                        parts_of[level][i][b].append(outs[i][rows_of(b - lo)])
            level_parts.append(total_of(query_parts))
        grad_queries.append(level_parts)

    run_grad = grad_queries[0][0]
    for level_parts in grad_queries[1:-1]:
        run_grad = jnp.concatenate(level_parts, axis=0) + 0.5 * spread(run_grad, pool())
    partial_ref[...] = 0.5 * spread(run_grad, pool())
    for a, block in enumerate((0, blocks - 1)):
        partial_ref[rows_of(block)] += grad_queries[-1][a]

    if top_level > 2:
        for level in range(top_level, 2, -1):
            for i in range(2):
                panel_grads[level - 3][i] += 0.5 * spread(panel_grads[level - 2][i], panel_scratch)
        for d in device_grads:
            at = pl.ds(pl.multiple_of((seq_index ^ d) * BLOCK, BLOCK), BLOCK)
            device_grads[d] = [panel_grads[0][i, at] for i in range(2)]

    for i in range(2):
        near_grads = [total_of(p) for p in parts_of[1][i]]
        edge_grads = [total_of(p) for p in parts_of[0][i][:2]]
        before = [
            edge_grads[0] + 0.5 * spread(near_grads[1][EDGE:], pool()),
            near_grads[0],
            near_grads[1][:EDGE],
        ]
        after = [
            edge_grads[1] + 0.5 * spread(near_grads[2][:EDGE], pool()),
            near_grads[2][EDGE:],
            near_grads[3],
        ]
        before, after = [jnp.concatenate(p, axis=0).astype(BF16) for p in (before, after)]
        sends[1][i] = jnp.where(odd, before, after)
        far = jnp.where(odd, after, before)
        for d in range(2, seq_count):
            device_grad = device_grads[d][i].astype(BF16)
            if d in wides:
                sends[d][i, :BLOCK] = jnp.where(is_neighbour(d), far[:BLOCK], device_grad)
                sends[d][i, BLOCK:] = far[BLOCK:]
            else:
                sends[d][i] = device_grad


def local_kernel(held, back, partial_ref, merged, attended_hbm, local_ref, grad_query_ref, sem):
    copy = pltpu.make_async_copy(merged, attended_hbm, sem)
    copy.start()
    blocks, width = held.shape[1] // BLOCK, held.shape[2]
    scale = width ** (-0.5)
    factor = scale * LOG2E
    parts = [[[] for _ in range(blocks)] for _ in range(2)]
    for a in range(blocks):
        lo, hi = own_window(a, blocks)
        window = rows_of(lo, hi - lo)
        query, key, value = held[0, rows_of(a)], held[1, window], held[2, window]
        peak, grad, shift = [back[w, rows_of(a)] for w in range(3)]
        wide = key.shape[0]
        exps = jnp.exp2(nt(query, key) * factor - across(peak, wide))
        score_grad = nt((grad * scale).astype(BF16), value) - across(shift * scale, wide)
        score_grad = (exps * score_grad).astype(BF16)
        grad_query_ref[rows_of(a)] = (nn(score_grad, key) + partial_ref[rows_of(a)]).astype(BF16)
        outs = tn(score_grad, query), tn(exps.astype(BF16), grad.astype(BF16))
        for i in range(2):
            for b in range(lo, hi):
                parts[i][b].append(outs[i][rows_of(b - lo)])
    for i in range(2):
        for b in range(blocks):
            local_ref[i, rows_of(b)] = total_of(parts[i][b])
    copy.wait()


def combine_kernel(seq_count, head_count, grad_query_ref, local_ref, *refs):
    received, refs = refs[: seq_count - 1], refs[seq_count - 1 :]
    received = dict(zip(seq_order(seq_count), received))
    outs, refs = refs[:-3], refs[-3:]
    outs = dict(zip([0] + head_order(head_count), outs))
    total, level_1, level_2 = refs
    seq_index, head_index = lax.axis_index("seq"), lax.axis_index("head")
    wides = wide_distances(seq_count)
    rows, width = local_ref.shape[1:]
    share = rows // head_count

    level_1[...] = jnp.zeros(level_1.shape, F32)
    level_2[...] = jnp.zeros(level_2.shape, F32)
    for i in range(2):
        total[i] = local_ref[i]
    for d in range(1, seq_count):
        got = received[d]
        partner = seq_index ^ d
        if d not in wides:
            for i in range(2):
                level_2[i] += got[i].astype(F32)
            continue

        @pl.when(partner == seq_index - 1)
        def _():
            for i in range(2):
                total[i, :BLOCK] += got[i, :BLOCK].astype(F32)
                level_1[i, EDGE:] += got[i, BLOCK:].astype(F32)

        @pl.when(partner == seq_index + 1)
        def _():
            for i in range(2):
                total[i, rows - BLOCK :] += got[i, :BLOCK].astype(F32)
                level_1[i, :REST] += got[i, BLOCK:].astype(F32)

        @pl.when((partner != seq_index + 1) & (partner != seq_index - 1))
        def _():
            for i in range(2):
                level_2[i] += got[i, :BLOCK].astype(F32)

    for i in range(2):
        half = level_2[i] * 0.5
        for phase in range(2):
            level_1[i, pl.ds(phase, half.shape[0], stride=2), :] += half
        half = level_1[i] * 0.5
        for phase in range(2):
            total[i, pl.ds(phase, half.shape[0], stride=2), :] += half
    for d in range(head_count):
        at = pl.ds(pl.multiple_of((head_index ^ d) * share, share), share)
        out = outs[d & ~1].at[d & 1] if d & ~1 in paired(head_count) else outs[d]
        out[0] = grad_query_ref[at, :]
        out[1] = total[0, at].astype(BF16)
        out[2] = total[1, at].astype(BF16)


def place_kernel(head_count, *refs):
    parts, outs = refs[:-3], refs[-3:]
    head_index = lax.axis_index("head")
    width = parts[0].shape[-1]
    first = [d for d in head_order(head_count) if d not in last_heads(head_count)]
    for d, part in zip([0] + first, parts):
        at = pl.ds(pl.multiple_of((head_index ^ d) * width, width), width)
        for i in range(3):
            outs[i][:, at] = part[0, i] if d in paired(head_count) else part[i]


def place_late_kernel(head_count, *refs):
    parts, outs, sems = refs[3:-4], refs[-4:-1], refs[-1]
    head_index = lax.axis_index("head")
    width = parts[0].shape[-1]
    copies = []
    far = [d + 1 for d in head_order(head_count) if d in paired(head_count)]
    for k, (d, part) in enumerate(zip(last_heads(head_count) + far, parts)):
        at = pl.ds(pl.multiple_of((head_index ^ d) * width, width), width)
        for i in range(3):
            copies.append(pltpu.make_async_copy(part.at[i], outs[i].at[:, at], sems.at[k, i]))
            copies[-1].start()
    for copy in copies:
        copy.wait()


def call(kernel, outs, scratch, args, in_hbm=0, hbm_outs=0, aliases={}, flops=0):
    return pl.pallas_call(
        kernel,
        out_shape=outs,
        in_specs=[pl.BlockSpec(memory_space=pltpu.HBM)] * in_hbm + [VMEM] * (len(args) - in_hbm),
        out_specs=[pl.BlockSpec(memory_space=pltpu.HBM)] * hbm_outs
        + [VMEM] * (len(outs) - hbm_outs),
        scratch_shapes=scratch,
        input_output_aliases=aliases,
        compiler_params=pltpu.CompilerParams(vmem_limit_bytes=48 * 2**20),
        cost_estimate=pl.CostEstimate(flops=flops, bytes_accessed=2**20, transcendentals=0),
    )(*args)


def swap_all(arrays, axis, distances):
    size = lax.axis_size(axis)
    return [
        lax.ppermute(x, axis, [(i, i ^ d) for i in range(size)]) for x, d in zip(arrays, distances)
    ]


def per_device(queries, keys, values, grad_out):
    seq_count, head_count = lax.axis_size("seq"), lax.axis_size("head")
    rows, width = queries.shape
    assert rows == 4 * BLOCK and width == BLOCK
    fine_blocks = rows * seq_count // BLOCK
    top_level = (fine_blocks // 4).bit_length() - 1
    wides = wide_distances(seq_count)
    distances = seq_order(seq_count)

    def shape(*dims, dtype=BF16):
        return jax.ShapeDtypeStruct(dims, dtype)

    def f32(*dims):
        return pltpu.VMEM(dims, F32)

    payloads = [shape(2, BLOCK + REST if d in wides else BLOCK, width) for d in distances]
    arguments = [
        pltpu.with_memory_space_constraint(x, pltpu.HBM) for x in (queries, keys, values, grad_out)
    ]
    fine_shapes = [shape(3, rows, width, dtype=F32)]
    fine_shapes += [shape(rows >> level, width) for level in range(1, top_level + 1)]
    fine_scratch = [f32(rows >> level, width) for level in range(top_level)]
    held, *outs = call(
        functools.partial(prep_kernel, seq_count, top_level),
        [shape(4, rows, width)] + fine_shapes + payloads,
        [f32(rows, width), f32(rows // 2, width)] * 2
        + fine_scratch
        + [pltpu.SemaphoreType.DMA((4,))],
        arguments,
        in_hbm=4,
    )
    done, sends = outs[: 1 + top_level], outs[1 + top_level :]
    received = swap_all(sends, "seq", distances)

    unit_flops = 2 * BLOCK * BLOCK * width
    stats, *level_queries = call(
        fine_kernel, fine_shapes, fine_scratch, (held, *done), flops=20 * unit_flops
    )

    panel_rows = [(seq_count >> (level - 2)) * BLOCK for level in range(2, top_level + 1)]
    panel_rows = panel_rows if top_level > 2 else []
    pools = [f32(BLOCK, width)] * 4 + [f32(r, width) for r in panel_rows[:1]]
    for level in range(top_level - 1, -1, -1):
        pools += [f32(rows >> level, width)] * 3
    for level in range(top_level):
        pools += [f32(rows >> level, width)] * 2
    for level in range(top_level - 1, -1, -1):
        pools += [f32(rows >> level, width)]
    pools += [f32(BLOCK, width)] * 4
    main = call(
        functools.partial(main_kernel, seq_count, top_level),
        [shape(rows, width)]
        + payloads
        + [shape(3, rows, width, dtype=F32), shape(rows, width, dtype=F32)],
        [pltpu.VMEM((2, r, width), BF16) for r in panel_rows]
        + [f32(2, r, width) for r in panel_rows]
        + pools,
        (held, stats, *level_queries, *received),
        flops=70 * unit_flops,
    )
    merged, sends, back, partial = main[0], main[1:seq_count], main[-2], main[-1]
    returned = swap_all(sends, "seq", distances)

    share = rows // head_count
    attended, local, grad_query = call(
        local_kernel,
        [shape(rows, width), shape(2, rows, width, dtype=F32), shape(rows, width)],
        [pltpu.SemaphoreType.DMA],
        (held, back, partial, merged),
        hbm_outs=1,
        flops=50 * unit_flops,
    )

    order = head_order(head_count)
    own, *parts = call(
        functools.partial(combine_kernel, seq_count, head_count),
        [
            shape(*((2,) if d in paired(head_count) else ()), 3, share, width)
            for d in [0] + order
        ],
        [f32(2, rows, width), f32(2, rows // 2, width), f32(2, rows // 4, width)],
        (grad_query, local, *returned),
    )
    parts = dict(zip(order, swap_all(parts, "head", order)))
    far = [parts[d][1] for d in order if d in paired(head_count)]
    late = swap_all(far, "head", [1] * len(far))
    last = [parts.pop(d) for d in last_heads(head_count)] + late
    grads = call(
        functools.partial(place_kernel, head_count),
        [shape(share, head_count * width)] * 3,
        [],
        (own, *parts.values()),
        flops=50 * unit_flops,
    )
    if last:
        grads = call(
            functools.partial(place_late_kernel, head_count),
            [shape(share, head_count * width)] * 3,
            [pltpu.SemaphoreType.DMA((len(last), 3))],
            (*grads, *last),
            in_hbm=3,
            hbm_outs=3,
            aliases={0: 0, 1: 1, 2: 2},
        )
    return (attended, *grads)


def solution(mesh):
    return jax.shard_map(
        per_device,
        mesh=mesh,
        in_specs=(P("seq", "head"),) * 4,
        out_specs=(P("seq", "head"),) + (P(("seq", "head"), None),) * 3,
        check_vma=False,
    )
```

```python
import functools

import jax
import jax.numpy as jnp
from jax import lax
from jax.experimental import pallas as pl
from jax.experimental.pallas import tpu as pltpu
from jax.sharding import PartitionSpec as P

BLOCK = 128
EDGE = BLOCK // 2
SPARE = 8
REST = 2 * BLOCK - EDGE
MASKED = -1e30
LOG2E = 1.4426950408889634
F32 = jnp.float32
BF16 = jnp.bfloat16
VMEM = pl.BlockSpec(memory_space=pltpu.VMEM)


def nt(a, b):
    return lax.dot_general(a, b, (((1,), (1,)), ((), ())), preferred_element_type=F32)


def nn(a, b):
    return lax.dot_general(a, b, (((1,), (0,)), ((), ())), preferred_element_type=F32)


def tn(a, b):
    return lax.dot_general(a, b, (((0,), (0,)), ((), ())), preferred_element_type=F32)


def pair_sum(x, scratch):
    rows = x.shape[0]
    scratch[:rows] = x
    return scratch[pl.ds(0, rows // 2, stride=2), :] + scratch[pl.ds(1, rows // 2, stride=2), :]


def coarse(x, scratch):
    return (pair_sum(x.astype(F32), scratch) * 0.5).astype(BF16)


def spread(x, scratch):
    rows = x.shape[0]
    scratch[pl.ds(0, rows, stride=2), :] = x
    scratch[pl.ds(1, rows, stride=2), :] = x
    return scratch[: 2 * rows]


def wide_distances(seq_count):
    return sorted({i ^ (i + 1) for i in range(seq_count - 1)})


def seq_order(seq_count):
    wides = wide_distances(seq_count)
    return wides[::-1] + [d for d in range(1, seq_count) if d not in wides]


def paired(head_count):
    return list(range(4, head_count - 2, 2))


def head_order(head_count):
    far = [d for d in (head_count - 2, head_count - 1) if d >= 4]
    return [d for d in paired(head_count) + far[:1] + [2] + far[1:] + [3, 1] if d < head_count]


def last_heads(head_count):
    return [d for d in head_order(head_count) if d in (1, 3, head_count - 1)]


def prep_kernel(seq_count, top_level, *refs):
    sources, refs = refs[:4], refs[4:]
    (held, stats), refs = refs[:2], refs[2:]
    queries, refs = refs[:top_level], refs[top_level:]
    sends, scratches, sems = refs[: seq_count - 1], refs[seq_count - 1 : -1], refs[-1]
    sends = dict(zip(seq_order(seq_count), sends))
    seq_index = lax.axis_index("seq")
    wides = wide_distances(seq_count)
    rows = held.shape[1]
    copies = [
        pltpu.make_async_copy(source, held.at[i], sems.at[i]) for i, source in enumerate(sources)
    ]
    for i in (1, 2, 0, 3):
        copies[i].start()
    for i in range(2):
        copies[1 + i].wait()
        ref = held.at[1 + i]
        level_1 = coarse(ref[...], scratches[2 * i])
        level_2 = coarse(level_1, scratches[2 * i + 1])
        for d in range(1, seq_count):
            out = sends[d]
            partner = seq_index ^ d
            if d not in wides:
                out[i] = level_2
                continue

            @pl.when(partner == seq_index + 1)
            def _():
                out[i, :BLOCK] = ref[rows - BLOCK :]
                out[i, BLOCK:] = level_1[:REST]

            @pl.when(partner == seq_index - 1)
            def _():
                out[i, :BLOCK] = ref[:BLOCK]
                out[i, BLOCK:] = level_1[EDGE:]

            @pl.when((partner != seq_index + 1) & (partner != seq_index - 1))
            def _():
                out[i, :BLOCK] = level_2
                out[i, BLOCK:] = level_1[:REST]

    copies[0].wait()

    @pl.when(goes_first())
    def _():
        fine_work(held, stats, queries, scratches[4:])

    copies[3].wait()


def slots_of(block, block_count):
    parent, odd = block // 2, block % 2
    if block_count == 4:
        first = parent == 0
        return [
            (jnp.where(first, 3, 0), None),
            (jnp.where(first, 2, 1), jnp.where(first, odd == 0, odd == 1)),
        ]
    near = jnp.where(odd == 0, 2 * parent + 2, 2 * parent - 1)
    raw = [2 * parent - 2, near, 2 * parent + 3]
    return [(jnp.clip(j, 0, block_count - 1), (j >= 0) & (j < block_count)) for j in raw]


def across(x, width):
    return jnp.concatenate([x] * (width // x.shape[1]), axis=1)


def lanes(column):
    return jnp.broadcast_to(column, (column.shape[0], BLOCK))


def row_max(x):
    return lanes(jnp.max(x, axis=-1, keepdims=True))


def row_sum(x):
    return lanes(jnp.sum(x, axis=-1, keepdims=True))


def total_of(parts):
    return functools.reduce(jnp.add, parts)


def rows_of(block, count=1):
    return slice(block * BLOCK, (block + count) * BLOCK)


def own_window(a, blocks):
    return max(a - 1, 0), min(a + 2, blocks)


def fine_work(held, stats, queries, scratches):
    blocks, width = held.shape[1] // BLOCK, held.shape[2]
    factor = width ** (-0.5) * LOG2E

    @pl.loop(0, blocks)
    def _(a):
        lo = jnp.clip(a - 1, 0, blocks - 3)
        own = pl.ds(pl.multiple_of(a * BLOCK, BLOCK), BLOCK)
        window = pl.ds(pl.multiple_of(lo * BLOCK, BLOCK), 3 * BLOCK)
        scores = nt(held[0, own], held[1, window]) * factor
        parts = [
            jnp.where(jnp.abs(lo + b - a) <= 1, scores[:, rows_of(b)], MASKED) for b in range(3)
        ]
        scores = jnp.concatenate(parts, axis=1)
        peak = row_max(scores)
        exps = jnp.exp2(scores - across(peak, scores.shape[1]))
        stats[0, own] = peak
        stats[1, own] = row_sum(exps)
        stats[2, own] = nn(exps.astype(BF16), held[2, window])

    query = held[0]
    for ref, scratch in zip(queries, scratches):
        query = coarse(query, scratch)
        ref[...] = query


def goes_first():
    return lax.axis_index("head") % 2 == 0


def fine_kernel(held, *refs):
    count = len(refs) // 3
    done, (stats, *queries), scratches = refs[: count + 1], refs[count + 1 : -count], refs[-count:]

    @pl.when(goes_first())
    def _():
        for ref, source in zip((stats, *queries), done):
            ref[...] = source[...]

    @pl.when(~goes_first())
    def _():
        fine_work(held, stats, queries, scratches)


def main_kernel(seq_count, top_level, *refs):
    refs = list(refs)

    def take(count):
        taken = refs[:count]
        del refs[:count]
        return taken

    held, stats = take(2)
    query_refs = take(top_level)
    received = dict(zip(seq_order(seq_count), take(seq_count - 1)))
    (attended_ref,) = take(1)
    sends = dict(zip(seq_order(seq_count), take(seq_count - 1)))
    back, partial_ref = take(2)
    panels = take(top_level - 1 if top_level > 2 else 0)
    panel_grads = take(len(panels))
    pools = refs

    def pool():
        return pools.pop(0)

    seq_index = lax.axis_index("seq")
    wides = wide_distances(seq_count)
    rows, width = held.shape[1:]
    blocks = rows // BLOCK
    scale = width ** (-0.5)
    factor = scale * LOG2E
    has_prev, has_next = seq_index > 0, seq_index < seq_count - 1

    odd = seq_index % 2 == 1
    further = wides[1:] or wides

    def is_neighbour(d):
        return jnp.abs((seq_index ^ d) - seq_index) == 1

    def by_side(near, far):
        return jnp.where(odd, near, far), jnp.where(odd, far, near)

    edges, nears = [], []
    for i in range(2):
        far = received[further[0]][i]
        for d in further[1:]:
            far = jnp.where(is_neighbour(d), received[d][i], far)
        before, after = by_side(received[1][i], far)
        edges.append((before[:BLOCK], after[:BLOCK]))
        nears.append(
            jnp.concatenate(
                [
                    before[BLOCK:],
                    coarse(before[:BLOCK], pool()),
                    coarse(after[:BLOCK], pool()),
                    after[BLOCK:],
                ],
                axis=0,
            )
        )

    def window(lo, hi, valid):
        return nears[0][rows_of(lo, hi - lo)], nears[1][rows_of(lo, hi - lo)], valid, (lo, hi)

    level_pieces = [
        [
            [(edges[0][side], edges[1][side], valid, (side, side + 1))]
            for side, valid in enumerate((has_prev, has_next))
        ],
        [
            [window(0, 1, has_prev), window(2, 4, has_next)],
            [window(0, 2, has_prev), window(3, 4, has_next)],
        ],
    ]
    if top_level == 2:
        pieces = []
        for d in range(2, seq_count):
            valid = ~is_neighbour(d) if d in wides else None
            pieces.append((received[d][0, :BLOCK], received[d][1, :BLOCK], valid, d))
        level_pieces.append([pieces])
    else:
        for panel in panels:
            panel[...] = jnp.zeros(panel.shape, BF16)
        for d in range(2, seq_count):
            at = pl.ds(pl.multiple_of((seq_index ^ d) * BLOCK, BLOCK), BLOCK)
            for i in range(2):
                panels[0][i, at] = received[d][i, :BLOCK]
        panel_scratch = pool()
        for level in range(2, top_level + 1):
            panel, pieces = panels[level - 2], []
            for i in range(2):
                if level > 2:
                    panel[i] = coarse(panels[level - 3][i], panel_scratch)
            for index, valid in slots_of(seq_index >> (level - 2), seq_count >> (level - 2)):
                at = pl.ds(pl.multiple_of(index * BLOCK, BLOCK), BLOCK)
                pieces.append((panel[0, at], panel[1, at], valid, at))
            level_pieces.append([pieces])
    level_queries = [[held[0, rows_of(0)], held[0, rows_of(blocks - 1)]]]
    for level in range(1, top_level + 1):
        query = query_refs[level - 1][...]
        step = query.shape[0] // len(level_pieces[level])
        level_queries.append(
            [query[a * step : (a + 1) * step] for a in range(len(level_pieces[level]))]
        )

    def unit(query, pieces, before=None):
        scores = []
        for key, _, valid, _ in pieces:
            score = nt(query, key) * factor
            scores.append(score if valid is None else jnp.where(valid, score, MASKED))
        peak = functools.reduce(jnp.maximum, [row_max(score) for score in scores])
        if before is not None:
            peak = jnp.maximum(peak, before[0])
        exps = [jnp.exp2(score - across(peak, score.shape[1])) for score in scores]
        rounded = [e.astype(BF16) for e in exps]
        ones = jnp.ones((BLOCK, width), BF16)
        both = []
        for r, piece in zip(rounded, pieces):
            count = piece[1].shape[0] // BLOCK
            both.append(nn(r, jnp.concatenate([piece[1], jnp.concatenate([ones] * count, axis=0)], axis=1)))
        both = total_of(both)
        sums, total = both[:, :width], both[:, width:]
        if before is not None:
            keep = jnp.exp2(before[0] - peak)
            total, sums = total + keep * before[1], sums + keep * before[2]
        return peak, total, sums, exps, rounded

    def before_of(block):
        return [stats[w, rows_of(block)] for w in range(3)]

    level_units = [
        [
            unit(query, pieces, before_of(block))
            for query, pieces, block in zip(level_queries[0], level_pieces[0], (0, blocks - 1))
        ]
    ]
    for level in range(1, top_level + 1):
        level_units.append(
            [unit(q, pieces) for q, pieces in zip(level_queries[level], level_pieces[level])]
        )

    def stacked(level, which):
        units = [u[which] for u in level_units[level]]
        if level == 0:
            units = [units[0], stats[which, rows_of(1, blocks - 2)], units[1]]
        return jnp.concatenate(units, axis=0)

    run = [stacked(top_level, w) for w in range(3)]
    own_factors, run_factors = [None] * top_level, [None] * top_level
    for level in range(top_level - 1, -1, -1):
        up_peak, up_total, up_sums = [spread(x, pool()) for x in run]
        peak, total, sums = [stacked(level, w) for w in range(3)]
        both = jnp.maximum(peak, up_peak)
        own = jnp.exp2(peak - both)
        up = 2.0 * jnp.exp2(up_peak - both)
        own_factors[level], run_factors[level] = own, up
        run = [both, own * total + up * up_total, own * sums + up * up_sums]

    inverse = 1.0 / run[1]
    attended = run[2] * inverse
    attended_ref[...] = attended.astype(BF16)

    cot = held[3].astype(F32)
    grad, shift = cot * inverse, row_sum(cot * attended) * inverse
    level_grads = []
    for level in range(top_level):
        level_grads.append((own_factors[level] * grad, own_factors[level] * shift))
        grad = pair_sum(run_factors[level] * grad, pool())
        shift = pair_sum(run_factors[level] * shift, pool())
    level_grads.append((grad, shift))
    back[0] = stacked(0, 0)
    back[1], back[2] = level_grads[0]

    for panel_grad in panel_grads:
        panel_grad[...] = jnp.zeros(panel_grad.shape, F32)

    device_grads = {d: [None, None] for d in range(2, seq_count)}
    grad_queries = []
    parts_of = [[[[] for _ in range(4)] for _ in range(2)] for _ in range(2)]
    for level in range(top_level, -1, -1):
        grad, shift = level_grads[level]
        step = level_queries[level][0].shape[0]
        level_parts = []
        for a, (query, pieces) in enumerate(zip(level_queries[level], level_pieces[level])):
            at = a if level > 0 else a * (blocks - 1)
            cut = slice(at * step, (at + 1) * step)
            grad_rounded = grad[cut].astype(BF16)
            grad_scaled = (grad[cut] * scale).astype(BF16)
            shift_scaled = shift[cut] * scale
            exps, rounded = level_units[level][a][3:]
            query_parts = []
            for piece, e, r in zip(pieces, exps, rounded):
                key, value, _, where = piece
                score_grad = nt(grad_scaled, value) - across(shift_scaled, e.shape[1])
                score_grad = (e * score_grad).astype(BF16)
                query_parts.append(nn(score_grad, key))
                outs = tn(score_grad, query), tn(r, grad_rounded)
                for i in range(2):
                    if level >= 2 and top_level == 2:
                        device_grads[where][i] = outs[i]
                        continue
                    if level >= 2:
                        panel_grads[level - 2][i, where] += outs[i]
                        continue
                    lo, hi = where
                    for b in range(lo, hi):
                        parts_of[level][i][b].append(outs[i][rows_of(b - lo)])
            level_parts.append(total_of(query_parts))
        grad_queries.append(level_parts)

    run_grad = grad_queries[0][0]
    for level_parts in grad_queries[1:-1]:
        run_grad = jnp.concatenate(level_parts, axis=0) + 0.5 * spread(run_grad, pool())
    partial_ref[...] = 0.5 * spread(run_grad, pool())
    for a, block in enumerate((0, blocks - 1)):
        partial_ref[rows_of(block)] += grad_queries[-1][a]

    if top_level > 2:
        for level in range(top_level, 2, -1):
            for i in range(2):
                panel_grads[level - 3][i] += 0.5 * spread(panel_grads[level - 2][i], panel_scratch)
        for d in device_grads:
            at = pl.ds(pl.multiple_of((seq_index ^ d) * BLOCK, BLOCK), BLOCK)
            device_grads[d] = [panel_grads[0][i, at] for i in range(2)]

    for i in range(2):
        near_grads = [total_of(p) for p in parts_of[1][i]]
        edge_grads = [total_of(p) for p in parts_of[0][i][:2]]
        before = [
            edge_grads[0] + 0.5 * spread(near_grads[1][EDGE:], pool()),
            near_grads[0],
            near_grads[1][:EDGE],
        ]
        after = [
            edge_grads[1] + 0.5 * spread(near_grads[2][:EDGE], pool()),
            near_grads[2][EDGE:],
            near_grads[3],
        ]
        before, after = [jnp.concatenate(p, axis=0).astype(BF16) for p in (before, after)]
        sends[1][i] = jnp.where(odd, before, after)
        far = jnp.where(odd, after, before)
        for d in range(2, seq_count):
            device_grad = device_grads[d][i].astype(BF16)
            if d in wides:
                sends[d][i, :BLOCK] = jnp.where(is_neighbour(d), far[:BLOCK], device_grad)
                sends[d][i, BLOCK:] = far[BLOCK:]
            else:
                sends[d][i] = device_grad


def local_kernel(held, back, partial_ref, merged, attended_hbm, local_ref, grad_query_ref, sem):
    copy = pltpu.make_async_copy(merged, attended_hbm, sem)
    copy.start()
    blocks, width = held.shape[1] // BLOCK, held.shape[2]
    scale = width ** (-0.5)
    factor = scale * LOG2E
    parts = [[[] for _ in range(blocks)] for _ in range(2)]
    for a in range(blocks):
        lo, hi = own_window(a, blocks)
        window = rows_of(lo, hi - lo)
        query, key, value = held[0, rows_of(a)], held[1, window], held[2, window]
        peak, grad, shift = [back[w, rows_of(a)] for w in range(3)]
        wide = key.shape[0]
        exps = jnp.exp2(nt(query, key) * factor - across(peak, wide))
        score_grad = nt((grad * scale).astype(BF16), value) - across(shift * scale, wide)
        score_grad = (exps * score_grad).astype(BF16)
        grad_query_ref[rows_of(a)] = (nn(score_grad, key) + partial_ref[rows_of(a)]).astype(BF16)
        outs = tn(score_grad, query), tn(exps.astype(BF16), grad.astype(BF16))
        for i in range(2):
            for b in range(lo, hi):
                parts[i][b].append(outs[i][rows_of(b - lo)])
    for i in range(2):
        for b in range(blocks):
            local_ref[i, rows_of(b)] = total_of(parts[i][b])
    copy.wait()


def combine_kernel(seq_count, head_count, grad_query_ref, local_ref, *refs):
    received, refs = refs[: seq_count - 1], refs[seq_count - 1 :]
    received = dict(zip(seq_order(seq_count), received))
    outs, refs = refs[:-3], refs[-3:]
    outs = dict(zip([0] + head_order(head_count), outs))
    total, level_1, level_2 = refs
    seq_index, head_index = lax.axis_index("seq"), lax.axis_index("head")
    wides = wide_distances(seq_count)
    rows, width = local_ref.shape[1:]
    share = rows // head_count

    level_1[...] = jnp.zeros(level_1.shape, F32)
    level_2[...] = jnp.zeros(level_2.shape, F32)
    for i in range(2):
        total[i, :rows] = local_ref[i]
    for d in range(1, seq_count):
        got = received[d]
        partner = seq_index ^ d
        if d not in wides:
            for i in range(2):
                level_2[i] += got[i].astype(F32)
            continue

        @pl.when(partner == seq_index - 1)
        def _():
            for i in range(2):
                total[i, :BLOCK] += got[i, :BLOCK].astype(F32)
                level_1[i, EDGE : EDGE + REST] += got[i, BLOCK:].astype(F32)

        @pl.when(partner == seq_index + 1)
        def _():
            for i in range(2):
                total[i, rows - BLOCK : rows] += got[i, :BLOCK].astype(F32)
                level_1[i, :REST] += got[i, BLOCK:].astype(F32)

        @pl.when((partner != seq_index + 1) & (partner != seq_index - 1))
        def _():
            for i in range(2):
                level_2[i] += got[i, :BLOCK].astype(F32)

    for i in range(2):
        half = level_2[i] * 0.5
        for phase in range(2):
            level_1[i, pl.ds(phase, half.shape[0], stride=2), :] += half
        half = level_1[i, : rows // 2] * 0.5
        for phase in range(2):
            total[i, pl.ds(phase, half.shape[0], stride=2), :] += half
    for d in range(head_count):
        at = pl.ds(pl.multiple_of((head_index ^ d) * share, share), share)
        out = outs[d & ~1].at[d & 1] if d & ~1 in paired(head_count) else outs[d]
        out[0] = grad_query_ref[at, :]
        out[1] = total[0, at].astype(BF16)
        out[2] = total[1, at].astype(BF16)


def place_kernel(head_count, *refs):
    parts, outs = refs[:-3], refs[-3:]
    head_index = lax.axis_index("head")
    width = parts[0].shape[-1]
    first = [d for d in head_order(head_count) if d not in last_heads(head_count)]
    for d, part in zip([0] + first, parts):
        at = pl.ds(pl.multiple_of((head_index ^ d) * width, width), width)
        for i in range(3):
            outs[i][:, at] = part[0, i] if d in paired(head_count) else part[i]


def place_late_kernel(head_count, *refs):
    parts, outs, sems = refs[3:-4], refs[-4:-1], refs[-1]
    head_index = lax.axis_index("head")
    width = parts[0].shape[-1]
    copies = []
    far = [d + 1 for d in head_order(head_count) if d in paired(head_count)]
    for k, (d, part) in enumerate(zip(last_heads(head_count) + far, parts)):
        at = pl.ds(pl.multiple_of((head_index ^ d) * width, width), width)
        for i in range(3):
            copies.append(pltpu.make_async_copy(part.at[i], outs[i].at[:, at], sems.at[k, i]))
            copies[-1].start()
    for copy in copies:
        copy.wait()


def call(kernel, outs, scratch, args, in_hbm=0, hbm_outs=0, aliases={}, flops=0):
    return pl.pallas_call(
        kernel,
        out_shape=outs,
        in_specs=[pl.BlockSpec(memory_space=pltpu.HBM)] * in_hbm + [VMEM] * (len(args) - in_hbm),
        out_specs=[pl.BlockSpec(memory_space=pltpu.HBM)] * hbm_outs
        + [VMEM] * (len(outs) - hbm_outs),
        scratch_shapes=scratch,
        input_output_aliases=aliases,
        compiler_params=pltpu.CompilerParams(vmem_limit_bytes=48 * 2**20),
        cost_estimate=pl.CostEstimate(flops=flops, bytes_accessed=2**20, transcendentals=0),
    )(*args)


def swap_all(arrays, axis, distances):
    size = lax.axis_size(axis)
    return [
        lax.ppermute(x, axis, [(i, i ^ d) for i in range(size)]) for x, d in zip(arrays, distances)
    ]


def per_device(queries, keys, values, grad_out):
    seq_count, head_count = lax.axis_size("seq"), lax.axis_size("head")
    rows, width = queries.shape
    assert rows == 4 * BLOCK and width == BLOCK
    fine_blocks = rows * seq_count // BLOCK
    top_level = (fine_blocks // 4).bit_length() - 1
    wides = wide_distances(seq_count)
    distances = seq_order(seq_count)

    def shape(*dims, dtype=BF16):
        return jax.ShapeDtypeStruct(dims, dtype)

    def f32(*dims):
        return pltpu.VMEM(dims, F32)

    def strided(rows):
        return f32(rows + SPARE, width)

    payloads = [shape(2, BLOCK + REST if d in wides else BLOCK, width) for d in distances]
    arguments = [
        pltpu.with_memory_space_constraint(x, pltpu.HBM) for x in (queries, keys, values, grad_out)
    ]
    fine_shapes = [shape(3, rows, width, dtype=F32)]
    fine_shapes += [shape(rows >> level, width) for level in range(1, top_level + 1)]
    fine_scratch = [strided(rows >> level) for level in range(top_level)]
    held, *outs = call(
        functools.partial(prep_kernel, seq_count, top_level),
        [shape(4, rows, width)] + fine_shapes + payloads,
        [strided(rows), strided(rows // 2)] * 2
        + fine_scratch
        + [pltpu.SemaphoreType.DMA((4,))],
        arguments,
        in_hbm=4,
    )
    done, sends = outs[: 1 + top_level], outs[1 + top_level :]
    received = swap_all(sends, "seq", distances)

    unit_flops = 2 * BLOCK * BLOCK * width
    stats, *level_queries = call(
        fine_kernel, fine_shapes, fine_scratch, (held, *done), flops=20 * unit_flops
    )

    panel_rows = [(seq_count >> (level - 2)) * BLOCK for level in range(2, top_level + 1)]
    panel_rows = panel_rows if top_level > 2 else []
    pools = [strided(BLOCK)] * 4 + [strided(r) for r in panel_rows[:1]]
    for level in range(top_level - 1, -1, -1):
        pools += [strided(rows >> level)] * 3
    for level in range(top_level):
        pools += [strided(rows >> level)] * 2
    for level in range(top_level - 1, -1, -1):
        pools += [strided(rows >> level)]
    pools += [strided(BLOCK)] * 4
    main = call(
        functools.partial(main_kernel, seq_count, top_level),
        [shape(rows, width)]
        + payloads
        + [shape(3, rows, width, dtype=F32), shape(rows, width, dtype=F32)],
        [pltpu.VMEM((2, r, width), BF16) for r in panel_rows]
        + [f32(2, r, width) for r in panel_rows]
        + pools,
        (held, stats, *level_queries, *received),
        flops=70 * unit_flops,
    )
    merged, sends, back, partial = main[0], main[1:seq_count], main[-2], main[-1]
    returned = swap_all(sends, "seq", distances)

    share = rows // head_count
    attended, local, grad_query = call(
        local_kernel,
        [shape(rows, width), shape(2, rows, width, dtype=F32), shape(rows, width)],
        [pltpu.SemaphoreType.DMA],
        (held, back, partial, merged),
        hbm_outs=1,
        flops=50 * unit_flops,
    )

    order = head_order(head_count)
    own, *parts = call(
        functools.partial(combine_kernel, seq_count, head_count),
        [
            shape(*((2,) if d in paired(head_count) else ()), 3, share, width)
            for d in [0] + order
        ],
        [
            f32(2, rows + SPARE, width),
            f32(2, rows // 2 + SPARE, width),
            f32(2, rows // 4, width),
        ],
        (grad_query, local, *returned),
    )
    parts = dict(zip(order, swap_all(parts, "head", order)))
    far = [parts[d][1] for d in order if d in paired(head_count)]
    late = swap_all(far, "head", [1] * len(far))
    last = [parts.pop(d) for d in last_heads(head_count)] + late
    grads = call(
        functools.partial(place_kernel, head_count),
        [shape(share, head_count * width)] * 3,
        [],
        (own, *parts.values()),
        flops=50 * unit_flops,
    )
    if last:
        grads = call(
            functools.partial(place_late_kernel, head_count),
            [shape(share, head_count * width)] * 3,
            [pltpu.SemaphoreType.DMA((len(last), 3))],
            (*grads, *last),
            in_hbm=3,
            hbm_outs=3,
            aliases={0: 0, 1: 1, 2: 2},
        )
    return (attended, *grads)


def solution(mesh):
    return jax.shard_map(
        per_device,
        mesh=mesh,
        in_specs=(P("seq", "head"),) * 4,
        out_specs=(P("seq", "head"),) + (P(("seq", "head"), None),) * 3,
        check_vma=False,
    )
```

```python
import functools

import jax
import jax.numpy as jnp
from jax import lax
from jax.experimental import pallas as pl
from jax.experimental.pallas import tpu as pltpu
from jax.sharding import PartitionSpec as P

BLOCK = 128
EDGE = BLOCK // 2
SPARE = 8
REST = 2 * BLOCK - EDGE
MASKED = -1e30
LOG2E = 1.4426950408889634
F32 = jnp.float32
BF16 = jnp.bfloat16
VMEM = pl.BlockSpec(memory_space=pltpu.VMEM)


def nt(a, b):
    return lax.dot_general(a, b, (((1,), (1,)), ((), ())), preferred_element_type=F32)


def nn(a, b):
    return lax.dot_general(a, b, (((1,), (0,)), ((), ())), preferred_element_type=F32)


def tn(a, b):
    return lax.dot_general(a, b, (((0,), (0,)), ((), ())), preferred_element_type=F32)


def pair_sum(x, scratch):
    rows = x.shape[0]
    scratch[:rows] = x
    return scratch[pl.ds(0, rows // 2, stride=2), :] + scratch[pl.ds(1, rows // 2, stride=2), :]


def coarse(x, scratch):
    return (pair_sum(x.astype(F32), scratch) * 0.5).astype(BF16)


def spread(x, scratch):
    rows = x.shape[0]
    scratch[pl.ds(0, rows, stride=2), :] = x
    scratch[pl.ds(1, rows, stride=2), :] = x
    return scratch[: 2 * rows]


def wide_distances(seq_count):
    return sorted({i ^ (i + 1) for i in range(seq_count - 1)})


def seq_order(seq_count):
    wides = wide_distances(seq_count)
    return wides[::-1] + [d for d in range(1, seq_count) if d not in wides]


def paired(head_count):
    return list(range(4, head_count - 2, 2))


def head_order(head_count):
    far = [d for d in (head_count - 2, head_count - 1) if d >= 4]
    return [d for d in paired(head_count) + far[:1] + [2] + far[1:] + [3, 1] if d < head_count]


def last_heads(head_count):
    return [d for d in head_order(head_count) if d in (1, 3, head_count - 1)]


def prep_kernel(seq_count, top_level, *refs):
    sources, refs = refs[:4], refs[4:]
    (held, stats), refs = refs[:2], refs[2:]
    queries, refs = refs[:top_level], refs[top_level:]
    sends, scratches, sems = refs[: seq_count - 1], refs[seq_count - 1 : -1], refs[-1]
    sends = dict(zip(seq_order(seq_count), sends))
    seq_index = lax.axis_index("seq")
    wides = wide_distances(seq_count)
    rows = held.shape[1]
    copies = [
        pltpu.make_async_copy(source, held.at[i], sems.at[i]) for i, source in enumerate(sources)
    ]
    for i in (1, 2, 0, 3):
        copies[i].start()
    for i in range(2):
        copies[1 + i].wait()
        ref = held.at[1 + i]
        level_1 = coarse(ref[...], scratches[2 * i])
        level_2 = coarse(level_1, scratches[2 * i + 1])
        for d in range(1, seq_count):
            out = sends[d]
            partner = seq_index ^ d
            if d not in wides:
                out[i] = level_2
                continue

            @pl.when(partner == seq_index + 1)
            def _():
                out[i, :BLOCK] = ref[rows - BLOCK :]
                out[i, BLOCK:] = level_1[:REST]

            @pl.when(partner == seq_index - 1)
            def _():
                out[i, :BLOCK] = ref[:BLOCK]
                out[i, BLOCK:] = level_1[EDGE:]

            @pl.when((partner != seq_index + 1) & (partner != seq_index - 1))
            def _():
                out[i, :BLOCK] = level_2
                out[i, BLOCK:] = level_1[:REST]

    copies[0].wait()

    @pl.when(goes_first())
    def _():
        fine_work(held, stats, queries, scratches[4:])

    copies[3].wait()


def slots_of(block, block_count):
    parent, odd = block // 2, block % 2
    if block_count == 4:
        first = parent == 0
        return [
            (jnp.where(first, 3, 0), None),
            (jnp.where(first, 2, 1), jnp.where(first, odd == 0, odd == 1)),
        ]
    near = jnp.where(odd == 0, 2 * parent + 2, 2 * parent - 1)
    raw = [2 * parent - 2, near, 2 * parent + 3]
    return [(jnp.clip(j, 0, block_count - 1), (j >= 0) & (j < block_count)) for j in raw]


def across(x, width):
    return jnp.concatenate([x] * (width // x.shape[1]), axis=1)


def lanes(column):
    return jnp.broadcast_to(column, (column.shape[0], BLOCK))


def row_max(x):
    return lanes(jnp.max(x, axis=-1, keepdims=True))


def row_sum(x):
    return lanes(jnp.sum(x, axis=-1, keepdims=True))


def total_of(parts):
    return functools.reduce(jnp.add, parts)


def rows_of(block, count=1):
    return slice(block * BLOCK, (block + count) * BLOCK)


def own_window(a, blocks):
    return max(a - 1, 0), min(a + 2, blocks)


def fine_work(held, stats, queries, scratches):
    blocks, width = held.shape[1] // BLOCK, held.shape[2]
    factor = width ** (-0.5) * LOG2E

    @pl.loop(0, blocks)
    def _(a):
        lo = jnp.clip(a - 1, 0, blocks - 3)
        own = pl.ds(pl.multiple_of(a * BLOCK, BLOCK), BLOCK)
        window = pl.ds(pl.multiple_of(lo * BLOCK, BLOCK), 3 * BLOCK)
        scores = nt(held[0, own], held[1, window]) * factor
        parts = [
            jnp.where(jnp.abs(lo + b - a) <= 1, scores[:, rows_of(b)], MASKED) for b in range(3)
        ]
        scores = jnp.concatenate(parts, axis=1)
        peak = row_max(scores)
        exps = jnp.exp2(scores - across(peak, scores.shape[1]))
        stats[0, own] = peak
        stats[1, own] = row_sum(exps)
        stats[2, own] = nn(exps.astype(BF16), held[2, window])

    query = held[0]
    for ref, scratch in zip(queries, scratches):
        query = coarse(query, scratch)
        ref[...] = query


def goes_first():
    return lax.axis_index("head") % 2 == 0


def fine_kernel(held, *refs):
    count = len(refs) // 3
    done, (stats, *queries), scratches = refs[: count + 1], refs[count + 1 : -count], refs[-count:]

    @pl.when(goes_first())
    def _():
        for ref, source in zip((stats, *queries), done):
            ref[...] = source[...]

    @pl.when(~goes_first())
    def _():
        fine_work(held, stats, queries, scratches)


def unit(query, pieces, before=None):
    width = query.shape[1]
    factor = width ** (-0.5) * LOG2E
    scores = []
    for key, _, valid, _ in pieces:
        score = nt(query, key) * factor
        scores.append(score if valid is None else jnp.where(valid, score, MASKED))
    peak = functools.reduce(jnp.maximum, [row_max(score) for score in scores])
    if before is not None:
        peak = jnp.maximum(peak, before[0])
    exps = [jnp.exp2(score - across(peak, score.shape[1])) for score in scores]
    rounded = [e.astype(BF16) for e in exps]
    ones = jnp.ones((BLOCK, width), BF16)
    both = []
    for r, piece in zip(rounded, pieces):
        count = piece[1].shape[0] // BLOCK
        both.append(nn(r, jnp.concatenate([piece[1], jnp.concatenate([ones] * count, axis=0)], axis=1)))
    both = total_of(both)
    sums, total = both[:, :width], both[:, width:]
    if before is not None:
        keep = jnp.exp2(before[0] - peak)
        total, sums = total + keep * before[1], sums + keep * before[2]
    return peak, total, sums, exps, rounded


def far_pieces(seq_count, received):
    seq_index, wides = lax.axis_index("seq"), wide_distances(seq_count)
    pieces = []
    for d in range(2, seq_count):
        apart = jnp.abs((seq_index ^ d) - seq_index) > 1
        valid = apart if d in wides else None
        pieces.append((received[d][0, :BLOCK], received[d][1, :BLOCK], valid, d))
    return pieces


def far_kernel(seq_count, query_ref, *refs):
    order = [d for d in seq_order(seq_count) if d > 1]
    received, refs = dict(zip(order, refs)), refs[len(order) :]
    up, exps_ref, scratches = refs[0], refs[1], refs[2:]
    peak, total, sums, exps, _ = unit(query_ref[...], far_pieces(seq_count, received))
    for w, value in enumerate((peak, total, sums)):
        up[w] = spread(value, scratches[w])
    for p, e in enumerate(exps):
        exps_ref[p] = e


def main_kernel(seq_count, top_level, *refs):
    refs = list(refs)

    def take(count):
        taken = refs[:count]
        del refs[:count]
        return taken

    held, stats = take(2)
    query_refs = take(top_level)
    up_ref, exps_ref = take(2) if top_level == 2 else (None, None)
    received = dict(zip(seq_order(seq_count), take(seq_count - 1)))
    (attended_ref,) = take(1)
    sends = dict(zip(seq_order(seq_count), take(seq_count - 1)))
    back, partial_ref = take(2)
    panels = take(top_level - 1 if top_level > 2 else 0)
    panel_grads = take(len(panels))
    pools = refs

    def pool():
        return pools.pop(0)

    seq_index = lax.axis_index("seq")
    wides = wide_distances(seq_count)
    rows, width = held.shape[1:]
    blocks = rows // BLOCK
    scale = width ** (-0.5)
    factor = scale * LOG2E
    has_prev, has_next = seq_index > 0, seq_index < seq_count - 1

    odd = seq_index % 2 == 1
    further = wides[1:] or wides

    def is_neighbour(d):
        return jnp.abs((seq_index ^ d) - seq_index) == 1

    def by_side(near, far):
        return jnp.where(odd, near, far), jnp.where(odd, far, near)

    edges, nears = [], []
    for i in range(2):
        far = received[further[0]][i]
        for d in further[1:]:
            far = jnp.where(is_neighbour(d), received[d][i], far)
        before, after = by_side(received[1][i], far)
        edges.append((before[:BLOCK], after[:BLOCK]))
        nears.append(
            jnp.concatenate(
                [
                    before[BLOCK:],
                    coarse(before[:BLOCK], pool()),
                    coarse(after[:BLOCK], pool()),
                    after[BLOCK:],
                ],
                axis=0,
            )
        )

    def window(lo, hi, valid):
        return nears[0][rows_of(lo, hi - lo)], nears[1][rows_of(lo, hi - lo)], valid, (lo, hi)

    level_pieces = [
        [
            [(edges[0][side], edges[1][side], valid, (side, side + 1))]
            for side, valid in enumerate((has_prev, has_next))
        ],
        [
            [window(0, 1, has_prev), window(2, 4, has_next)],
            [window(0, 2, has_prev), window(3, 4, has_next)],
        ],
    ]
    if top_level == 2:
        pieces = far_pieces(seq_count, received)
        level_pieces.append([pieces])
    else:
        for panel in panels:
            panel[...] = jnp.zeros(panel.shape, BF16)
        for d in range(2, seq_count):
            at = pl.ds(pl.multiple_of((seq_index ^ d) * BLOCK, BLOCK), BLOCK)
            for i in range(2):
                panels[0][i, at] = received[d][i, :BLOCK]
        panel_scratch = pool()
        for level in range(2, top_level + 1):
            panel, pieces = panels[level - 2], []
            for i in range(2):
                if level > 2:
                    panel[i] = coarse(panels[level - 3][i], panel_scratch)
            for index, valid in slots_of(seq_index >> (level - 2), seq_count >> (level - 2)):
                at = pl.ds(pl.multiple_of(index * BLOCK, BLOCK), BLOCK)
                pieces.append((panel[0, at], panel[1, at], valid, at))
            level_pieces.append([pieces])
    level_queries = [[held[0, rows_of(0)], held[0, rows_of(blocks - 1)]]]
    for level in range(1, top_level + 1):
        query = query_refs[level - 1][...]
        step = query.shape[0] // len(level_pieces[level])
        level_queries.append(
            [query[a * step : (a + 1) * step] for a in range(len(level_pieces[level]))]
        )

    def before_of(block):
        return [stats[w, rows_of(block)] for w in range(3)]

    level_units = [
        [
            unit(query, pieces, before_of(block))
            for query, pieces, block in zip(level_queries[0], level_pieces[0], (0, blocks - 1))
        ]
    ]
    for level in range(1, top_level + 1):
        if level == 2 and top_level == 2:
            exps = [exps_ref[p] for p in range(exps_ref.shape[0])]
            level_units.append([(None, None, None, exps, [e.astype(BF16) for e in exps])])
            continue
        level_units.append(
            [unit(q, pieces) for q, pieces in zip(level_queries[level], level_pieces[level])]
        )

    def stacked(level, which):
        units = [u[which] for u in level_units[level]]
        if level == 0:
            units = [units[0], stats[which, rows_of(1, blocks - 2)], units[1]]
        return jnp.concatenate(units, axis=0)

    run = None if top_level == 2 else [stacked(top_level, w) for w in range(3)]
    own_factors, run_factors = [None] * top_level, [None] * top_level
    for level in range(top_level - 1, -1, -1):
        if run is None:
            up_peak, up_total, up_sums = [up_ref[w] for w in range(3)]
        else:
            up_peak, up_total, up_sums = [spread(x, pool()) for x in run]
        peak, total, sums = [stacked(level, w) for w in range(3)]
        both = jnp.maximum(peak, up_peak)
        own = jnp.exp2(peak - both)
        up = 2.0 * jnp.exp2(up_peak - both)
        own_factors[level], run_factors[level] = own, up
        run = [both, own * total + up * up_total, own * sums + up * up_sums]

    inverse = 1.0 / run[1]
    attended = run[2] * inverse
    attended_ref[...] = attended.astype(BF16)

    cot = held[3].astype(F32)
    grad, shift = cot * inverse, row_sum(cot * attended) * inverse
    level_grads = []
    for level in range(top_level):
        level_grads.append((own_factors[level] * grad, own_factors[level] * shift))
        grad = pair_sum(run_factors[level] * grad, pool())
        shift = pair_sum(run_factors[level] * shift, pool())
    level_grads.append((grad, shift))
    back[0] = stacked(0, 0)
    back[1], back[2] = level_grads[0]

    for panel_grad in panel_grads:
        panel_grad[...] = jnp.zeros(panel_grad.shape, F32)

    device_grads = {d: [None, None] for d in range(2, seq_count)}
    grad_queries = []
    parts_of = [[[[] for _ in range(4)] for _ in range(2)] for _ in range(2)]
    for level in range(top_level, -1, -1):
        grad, shift = level_grads[level]
        step = level_queries[level][0].shape[0]
        level_parts = []
        for a, (query, pieces) in enumerate(zip(level_queries[level], level_pieces[level])):
            at = a if level > 0 else a * (blocks - 1)
            cut = slice(at * step, (at + 1) * step)
            grad_rounded = grad[cut].astype(BF16)
            grad_scaled = (grad[cut] * scale).astype(BF16)
            shift_scaled = shift[cut] * scale
            exps, rounded = level_units[level][a][3:]
            query_parts = []
            for piece, e, r in zip(pieces, exps, rounded):
                key, value, _, where = piece
                score_grad = nt(grad_scaled, value) - across(shift_scaled, e.shape[1])
                score_grad = (e * score_grad).astype(BF16)
                query_parts.append(nn(score_grad, key))
                outs = tn(score_grad, query), tn(r, grad_rounded)
                for i in range(2):
                    if level >= 2 and top_level == 2:
                        device_grads[where][i] = outs[i]
                        continue
                    if level >= 2:
                        panel_grads[level - 2][i, where] += outs[i]
                        continue
                    lo, hi = where
                    for b in range(lo, hi):
                        parts_of[level][i][b].append(outs[i][rows_of(b - lo)])
            level_parts.append(total_of(query_parts))
        grad_queries.append(level_parts)

    run_grad = grad_queries[0][0]
    for level_parts in grad_queries[1:-1]:
        run_grad = jnp.concatenate(level_parts, axis=0) + 0.5 * spread(run_grad, pool())
    partial_ref[...] = 0.5 * spread(run_grad, pool())
    for a, block in enumerate((0, blocks - 1)):
        partial_ref[rows_of(block)] += grad_queries[-1][a]

    if top_level > 2:
        for level in range(top_level, 2, -1):
            for i in range(2):
                panel_grads[level - 3][i] += 0.5 * spread(panel_grads[level - 2][i], panel_scratch)
        for d in device_grads:
            at = pl.ds(pl.multiple_of((seq_index ^ d) * BLOCK, BLOCK), BLOCK)
            device_grads[d] = [panel_grads[0][i, at] for i in range(2)]

    for i in range(2):
        near_grads = [total_of(p) for p in parts_of[1][i]]
        edge_grads = [total_of(p) for p in parts_of[0][i][:2]]
        before = [
            edge_grads[0] + 0.5 * spread(near_grads[1][EDGE:], pool()),
            near_grads[0],
            near_grads[1][:EDGE],
        ]
        after = [
            edge_grads[1] + 0.5 * spread(near_grads[2][:EDGE], pool()),
            near_grads[2][EDGE:],
            near_grads[3],
        ]
        before, after = [jnp.concatenate(p, axis=0).astype(BF16) for p in (before, after)]
        sends[1][i] = jnp.where(odd, before, after)
        far = jnp.where(odd, after, before)
        for d in range(2, seq_count):
            device_grad = device_grads[d][i].astype(BF16)
            if d in wides:
                sends[d][i, :BLOCK] = jnp.where(is_neighbour(d), far[:BLOCK], device_grad)
                sends[d][i, BLOCK:] = far[BLOCK:]
            else:
                sends[d][i] = device_grad


def local_kernel(held, back, partial_ref, merged, attended_hbm, local_ref, grad_query_ref, sem):
    copy = pltpu.make_async_copy(merged, attended_hbm, sem)
    copy.start()
    blocks, width = held.shape[1] // BLOCK, held.shape[2]
    scale = width ** (-0.5)
    factor = scale * LOG2E
    parts = [[[] for _ in range(blocks)] for _ in range(2)]
    for a in range(blocks):
        lo, hi = own_window(a, blocks)
        window = rows_of(lo, hi - lo)
        query, key, value = held[0, rows_of(a)], held[1, window], held[2, window]
        peak, grad, shift = [back[w, rows_of(a)] for w in range(3)]
        wide = key.shape[0]
        exps = jnp.exp2(nt(query, key) * factor - across(peak, wide))
        score_grad = nt((grad * scale).astype(BF16), value) - across(shift * scale, wide)
        score_grad = (exps * score_grad).astype(BF16)
        grad_query_ref[rows_of(a)] = (nn(score_grad, key) + partial_ref[rows_of(a)]).astype(BF16)
        outs = tn(score_grad, query), tn(exps.astype(BF16), grad.astype(BF16))
        for i in range(2):
            for b in range(lo, hi):
                parts[i][b].append(outs[i][rows_of(b - lo)])
    for i in range(2):
        for b in range(blocks):
            local_ref[i, rows_of(b)] = total_of(parts[i][b])
    copy.wait()


def combine_kernel(seq_count, head_count, grad_query_ref, local_ref, *refs):
    received, refs = refs[: seq_count - 1], refs[seq_count - 1 :]
    received = dict(zip(seq_order(seq_count), received))
    outs, refs = refs[:-3], refs[-3:]
    outs = dict(zip([0] + head_order(head_count), outs))
    total, level_1, level_2 = refs
    seq_index, head_index = lax.axis_index("seq"), lax.axis_index("head")
    wides = wide_distances(seq_count)
    rows, width = local_ref.shape[1:]
    share = rows // head_count

    level_1[...] = jnp.zeros(level_1.shape, F32)
    level_2[...] = jnp.zeros(level_2.shape, F32)
    for i in range(2):
        total[i, :rows] = local_ref[i]
    for d in range(1, seq_count):
        got = received[d]
        partner = seq_index ^ d
        if d not in wides:
            for i in range(2):
                level_2[i] += got[i].astype(F32)
            continue

        @pl.when(partner == seq_index - 1)
        def _():
            for i in range(2):
                total[i, :BLOCK] += got[i, :BLOCK].astype(F32)
                level_1[i, EDGE : EDGE + REST] += got[i, BLOCK:].astype(F32)

        @pl.when(partner == seq_index + 1)
        def _():
            for i in range(2):
                total[i, rows - BLOCK : rows] += got[i, :BLOCK].astype(F32)
                level_1[i, :REST] += got[i, BLOCK:].astype(F32)

        @pl.when((partner != seq_index + 1) & (partner != seq_index - 1))
        def _():
            for i in range(2):
                level_2[i] += got[i, :BLOCK].astype(F32)

    for i in range(2):
        half = level_2[i] * 0.5
        for phase in range(2):
            level_1[i, pl.ds(phase, half.shape[0], stride=2), :] += half
        half = level_1[i, : rows // 2] * 0.5
        for phase in range(2):
            total[i, pl.ds(phase, half.shape[0], stride=2), :] += half
    for d in range(head_count):
        at = pl.ds(pl.multiple_of((head_index ^ d) * share, share), share)
        out = outs[d & ~1].at[d & 1] if d & ~1 in paired(head_count) else outs[d]
        out[0] = grad_query_ref[at, :]
        out[1] = total[0, at].astype(BF16)
        out[2] = total[1, at].astype(BF16)


def place_kernel(head_count, *refs):
    parts, outs = refs[:-3], refs[-3:]
    head_index = lax.axis_index("head")
    width = parts[0].shape[-1]
    first = [d for d in head_order(head_count) if d not in last_heads(head_count)]
    for d, part in zip([0] + first, parts):
        at = pl.ds(pl.multiple_of((head_index ^ d) * width, width), width)
        for i in range(3):
            outs[i][:, at] = part[0, i] if d in paired(head_count) else part[i]


def place_late_kernel(head_count, *refs):
    parts, outs, sems = refs[3:-4], refs[-4:-1], refs[-1]
    head_index = lax.axis_index("head")
    width = parts[0].shape[-1]
    copies = []
    far = [d + 1 for d in head_order(head_count) if d in paired(head_count)]
    for k, (d, part) in enumerate(zip(last_heads(head_count) + far, parts)):
        at = pl.ds(pl.multiple_of((head_index ^ d) * width, width), width)
        for i in range(3):
            copies.append(pltpu.make_async_copy(part.at[i], outs[i].at[:, at], sems.at[k, i]))
            copies[-1].start()
    for copy in copies:
        copy.wait()


def call(kernel, outs, scratch, args, in_hbm=0, hbm_outs=0, aliases={}, flops=0):
    return pl.pallas_call(
        kernel,
        out_shape=outs,
        in_specs=[pl.BlockSpec(memory_space=pltpu.HBM)] * in_hbm + [VMEM] * (len(args) - in_hbm),
        out_specs=[pl.BlockSpec(memory_space=pltpu.HBM)] * hbm_outs
        + [VMEM] * (len(outs) - hbm_outs),
        scratch_shapes=scratch,
        input_output_aliases=aliases,
        compiler_params=pltpu.CompilerParams(vmem_limit_bytes=48 * 2**20),
        cost_estimate=pl.CostEstimate(flops=flops, bytes_accessed=2**20, transcendentals=0),
    )(*args)


def swap_all(arrays, axis, distances):
    size = lax.axis_size(axis)
    return [
        lax.ppermute(x, axis, [(i, i ^ d) for i in range(size)]) for x, d in zip(arrays, distances)
    ]


def per_device(queries, keys, values, grad_out):
    seq_count, head_count = lax.axis_size("seq"), lax.axis_size("head")
    rows, width = queries.shape
    assert rows == 4 * BLOCK and width == BLOCK
    fine_blocks = rows * seq_count // BLOCK
    top_level = (fine_blocks // 4).bit_length() - 1
    wides = wide_distances(seq_count)
    distances = seq_order(seq_count)

    def shape(*dims, dtype=BF16):
        return jax.ShapeDtypeStruct(dims, dtype)

    def f32(*dims):
        return pltpu.VMEM(dims, F32)

    def strided(rows):
        return f32(rows + SPARE, width)

    payloads = [shape(2, BLOCK + REST if d in wides else BLOCK, width) for d in distances]
    arguments = [
        pltpu.with_memory_space_constraint(x, pltpu.HBM) for x in (queries, keys, values, grad_out)
    ]
    fine_shapes = [shape(3, rows, width, dtype=F32)]
    fine_shapes += [shape(rows >> level, width) for level in range(1, top_level + 1)]
    fine_scratch = [strided(rows >> level) for level in range(top_level)]
    held, *outs = call(
        functools.partial(prep_kernel, seq_count, top_level),
        [shape(4, rows, width)] + fine_shapes + payloads,
        [strided(rows), strided(rows // 2)] * 2
        + fine_scratch
        + [pltpu.SemaphoreType.DMA((4,))],
        arguments,
        in_hbm=4,
    )
    done, sends = outs[: 1 + top_level], outs[1 + top_level :]
    received = swap_all(sends, "seq", distances)

    unit_flops = 2 * BLOCK * BLOCK * width
    stats, *level_queries = call(
        fine_kernel, fine_shapes, fine_scratch, (held, *done), flops=20 * unit_flops
    )

    panel_rows = [(seq_count >> (level - 2)) * BLOCK for level in range(2, top_level + 1)]
    panel_rows = panel_rows if top_level > 2 else []
    pools = [strided(BLOCK)] * 4 + [strided(r) for r in panel_rows[:1]]
    for level in range(top_level - 1 - (top_level == 2), -1, -1):
        pools += [strided(rows >> level)] * 3
    for level in range(top_level):
        pools += [strided(rows >> level)] * 2
    for level in range(top_level - 1, -1, -1):
        pools += [strided(rows >> level)]
    pools += [strided(BLOCK)] * 4
    ahead = []
    if top_level == 2:
        count = seq_count - 2
        ahead = call(
            functools.partial(far_kernel, seq_count),
            [shape(3, rows // 2, width, dtype=F32), shape(count, rows // 4, BLOCK, dtype=F32)],
            [strided(rows // 2)] * 3,
            (level_queries[-1], *[x for d, x in zip(distances, received) if d > 1]),
            flops=10 * unit_flops,
        )
    main = call(
        functools.partial(main_kernel, seq_count, top_level),
        [shape(rows, width)]
        + payloads
        + [shape(3, rows, width, dtype=F32), shape(rows, width, dtype=F32)],
        [pltpu.VMEM((2, r, width), BF16) for r in panel_rows]
        + [f32(2, r, width) for r in panel_rows]
        + pools,
        (held, stats, *level_queries, *ahead, *received),
        flops=70 * unit_flops,
    )
    merged, sends, back, partial = main[0], main[1:seq_count], main[-2], main[-1]
    returned = swap_all(sends, "seq", distances)

    share = rows // head_count
    attended, local, grad_query = call(
        local_kernel,
        [shape(rows, width), shape(2, rows, width, dtype=F32), shape(rows, width)],
        [pltpu.SemaphoreType.DMA],
        (held, back, partial, merged),
        hbm_outs=1,
        flops=50 * unit_flops,
    )

    order = head_order(head_count)
    own, *parts = call(
        functools.partial(combine_kernel, seq_count, head_count),
        [
            shape(*((2,) if d in paired(head_count) else ()), 3, share, width)
            for d in [0] + order
        ],
        [
            f32(2, rows + SPARE, width),
            f32(2, rows // 2 + SPARE, width),
            f32(2, rows // 4, width),
        ],
        (grad_query, local, *returned),
    )
    parts = dict(zip(order, swap_all(parts, "head", order)))
    far = [parts[d][1] for d in order if d in paired(head_count)]
    late = swap_all(far, "head", [1] * len(far))
    last = [parts.pop(d) for d in last_heads(head_count)] + late
    grads = call(
        functools.partial(place_kernel, head_count),
        [shape(share, head_count * width)] * 3,
        [],
        (own, *parts.values()),
        flops=50 * unit_flops,
    )
    if last:
        grads = call(
            functools.partial(place_late_kernel, head_count),
            [shape(share, head_count * width)] * 3,
            [pltpu.SemaphoreType.DMA((len(last), 3))],
            (*grads, *last),
            in_hbm=3,
            hbm_outs=3,
            aliases={0: 0, 1: 1, 2: 2},
        )
    return (attended, *grads)


def solution(mesh):
    return jax.shard_map(
        per_device,
        mesh=mesh,
        in_specs=(P("seq", "head"),) * 4,
        out_specs=(P("seq", "head"),) + (P(("seq", "head"), None),) * 3,
        check_vma=False,
    )
```

```python
import functools

import jax
import jax.numpy as jnp
from jax import lax
from jax.experimental import pallas as pl
from jax.experimental.pallas import tpu as pltpu
from jax.sharding import PartitionSpec as P

BLOCK = 128
EDGE = BLOCK // 2
SPARE = 8
REST = 2 * BLOCK - EDGE
MASKED = -1e30
LOG2E = 1.4426950408889634
F32 = jnp.float32
BF16 = jnp.bfloat16
VMEM = pl.BlockSpec(memory_space=pltpu.VMEM)


def nt(a, b):
    return lax.dot_general(a, b, (((1,), (1,)), ((), ())), preferred_element_type=F32)


def nn(a, b):
    return lax.dot_general(a, b, (((1,), (0,)), ((), ())), preferred_element_type=F32)


def tn(a, b):
    return lax.dot_general(a, b, (((0,), (0,)), ((), ())), preferred_element_type=F32)


def pair_sum(x, scratch):
    rows = x.shape[0]
    scratch[:rows] = x
    return scratch[pl.ds(0, rows // 2, stride=2), :] + scratch[pl.ds(1, rows // 2, stride=2), :]


def coarse(x, scratch):
    return (pair_sum(x.astype(F32), scratch) * 0.5).astype(BF16)


def spread(x, scratch):
    rows = x.shape[0]
    scratch[pl.ds(0, rows, stride=2), :] = x
    scratch[pl.ds(1, rows, stride=2), :] = x
    return scratch[: 2 * rows]


def wide_distances(seq_count):
    return sorted({i ^ (i + 1) for i in range(seq_count - 1)})


def seq_order(seq_count):
    wides = wide_distances(seq_count)
    return wides[::-1] + [d for d in range(1, seq_count) if d not in wides]


def paired(head_count):
    return list(range(4, head_count - 2, 2))


def head_order(head_count):
    far = [d for d in (head_count - 2, head_count - 1) if d >= 4]
    return [d for d in paired(head_count) + far[:1] + [2] + far[1:] + [3, 1] if d < head_count]


def last_heads(head_count):
    return [d for d in head_order(head_count) if d in (1, 3, head_count - 1)]


def prep_kernel(seq_count, top_level, *refs):
    sources, refs = refs[:4], refs[4:]
    (held, stats), refs = refs[:2], refs[2:]
    queries, refs = refs[:top_level], refs[top_level:]
    sends, scratches, sems = refs[: seq_count - 1], refs[seq_count - 1 : -1], refs[-1]
    sends = dict(zip(seq_order(seq_count), sends))
    seq_index = lax.axis_index("seq")
    wides = wide_distances(seq_count)
    rows = held.shape[1]
    copies = [
        pltpu.make_async_copy(source, held.at[i], sems.at[i]) for i, source in enumerate(sources)
    ]
    for i in (1, 2, 0, 3):
        copies[i].start()
    for i in range(2):
        copies[1 + i].wait()
        ref = held.at[1 + i]
        level_1 = coarse(ref[...], scratches[2 * i])
        level_2 = coarse(level_1, scratches[2 * i + 1])
        for d in range(1, seq_count):
            out = sends[d]
            partner = seq_index ^ d
            if d not in wides:
                out[i] = level_2
                continue

            @pl.when(partner == seq_index + 1)
            def _():
                out[i, :BLOCK] = ref[rows - BLOCK :]
                out[i, BLOCK:] = level_1[:REST]

            @pl.when(partner == seq_index - 1)
            def _():
                out[i, :BLOCK] = ref[:BLOCK]
                out[i, BLOCK:] = level_1[EDGE:]

            @pl.when((partner != seq_index + 1) & (partner != seq_index - 1))
            def _():
                out[i, :BLOCK] = level_2
                out[i, BLOCK:] = level_1[:REST]

    copies[0].wait()

    @pl.when(goes_first())
    def _():
        fine_work(held, stats, queries, scratches[4:])

    copies[3].wait()


def slots_of(block, block_count):
    parent, odd = block // 2, block % 2
    if block_count == 4:
        first = parent == 0
        return [
            (jnp.where(first, 3, 0), None),
            (jnp.where(first, 2, 1), jnp.where(first, odd == 0, odd == 1)),
        ]
    near = jnp.where(odd == 0, 2 * parent + 2, 2 * parent - 1)
    raw = [2 * parent - 2, near, 2 * parent + 3]
    return [(jnp.clip(j, 0, block_count - 1), (j >= 0) & (j < block_count)) for j in raw]


def across(x, width):
    return jnp.concatenate([x] * (width // x.shape[1]), axis=1)


def lanes(column):
    return jnp.broadcast_to(column, (column.shape[0], BLOCK))


def row_max(x):
    return lanes(jnp.max(x, axis=-1, keepdims=True))


def row_sum(x):
    return lanes(jnp.sum(x, axis=-1, keepdims=True))


def total_of(parts):
    return functools.reduce(jnp.add, parts)


def rows_of(block, count=1):
    return slice(block * BLOCK, (block + count) * BLOCK)


def own_window(a, blocks):
    return max(a - 1, 0), min(a + 2, blocks)


def fine_work(held, stats, queries, scratches):
    blocks, width = held.shape[1] // BLOCK, held.shape[2]
    factor = width ** (-0.5) * LOG2E

    @pl.loop(0, blocks, unroll=2)
    def _(a):
        lo = jnp.clip(a - 1, 0, blocks - 3)
        own = pl.ds(pl.multiple_of(a * BLOCK, BLOCK), BLOCK)
        window = pl.ds(pl.multiple_of(lo * BLOCK, BLOCK), 3 * BLOCK)
        scores = nt(held[0, own], held[1, window]) * factor
        parts = [
            jnp.where(jnp.abs(lo + b - a) <= 1, scores[:, rows_of(b)], MASKED) for b in range(3)
        ]
        scores = jnp.concatenate(parts, axis=1)
        peak = row_max(scores)
        exps = jnp.exp2(scores - across(peak, scores.shape[1]))
        stats[0, own] = peak
        stats[1, own] = row_sum(exps)
        stats[2, own] = nn(exps.astype(BF16), held[2, window])

    query = held[0]
    for ref, scratch in zip(queries, scratches):
        query = coarse(query, scratch)
        ref[...] = query


def goes_first():
    return lax.axis_index("head") % 2 == 0


def fine_kernel(held, *refs):
    count = len(refs) // 3
    done, (stats, *queries), scratches = refs[: count + 1], refs[count + 1 : -count], refs[-count:]

    @pl.when(goes_first())
    def _():
        for ref, source in zip((stats, *queries), done):
            ref[...] = source[...]

    @pl.when(~goes_first())
    def _():
        fine_work(held, stats, queries, scratches)


def unit(query, pieces, before=None):
    width = query.shape[1]
    factor = width ** (-0.5) * LOG2E
    scores = []
    for key, _, valid, _ in pieces:
        score = nt(query, key) * factor
        scores.append(score if valid is None else jnp.where(valid, score, MASKED))
    peak = functools.reduce(jnp.maximum, [row_max(score) for score in scores])
    if before is not None:
        peak = jnp.maximum(peak, before[0])
    exps = [jnp.exp2(score - across(peak, score.shape[1])) for score in scores]
    rounded = [e.astype(BF16) for e in exps]
    ones = jnp.ones((BLOCK, width), BF16)
    both = []
    for r, piece in zip(rounded, pieces):
        count = piece[1].shape[0] // BLOCK
        both.append(nn(r, jnp.concatenate([piece[1], jnp.concatenate([ones] * count, axis=0)], axis=1)))
    both = total_of(both)
    sums, total = both[:, :width], both[:, width:]
    if before is not None:
        keep = jnp.exp2(before[0] - peak)
        total, sums = total + keep * before[1], sums + keep * before[2]
    return peak, total, sums, exps, rounded


def far_pieces(seq_count, received):
    seq_index, wides = lax.axis_index("seq"), wide_distances(seq_count)
    pieces = []
    for d in range(2, seq_count):
        apart = jnp.abs((seq_index ^ d) - seq_index) > 1
        valid = apart if d in wides else None
        pieces.append((received[d][0, :BLOCK], received[d][1, :BLOCK], valid, d))
    return pieces


def far_kernel(seq_count, query_ref, *refs):
    order = [d for d in seq_order(seq_count) if d > 1]
    received, refs = dict(zip(order, refs)), refs[len(order) :]
    up, exps_ref, scratches = refs[0], refs[1], refs[2:]
    peak, total, sums, exps, _ = unit(query_ref[...], far_pieces(seq_count, received))
    for w, value in enumerate((peak, total, sums)):
        up[w] = spread(value, scratches[w])
    for p, e in enumerate(exps):
        exps_ref[p] = e


def main_kernel(seq_count, top_level, *refs):
    refs = list(refs)

    def take(count):
        taken = refs[:count]
        del refs[:count]
        return taken

    held, stats = take(2)
    query_refs = take(top_level)
    up_ref, exps_ref = take(2) if top_level == 2 else (None, None)
    received = dict(zip(seq_order(seq_count), take(seq_count - 1)))
    (attended_ref,) = take(1)
    sends = dict(zip(seq_order(seq_count), take(seq_count - 1)))
    back, partial_ref = take(2)
    panels = take(top_level - 1 if top_level > 2 else 0)
    panel_grads = take(len(panels))
    pools = refs

    def pool():
        return pools.pop(0)

    seq_index = lax.axis_index("seq")
    wides = wide_distances(seq_count)
    rows, width = held.shape[1:]
    blocks = rows // BLOCK
    scale = width ** (-0.5)
    factor = scale * LOG2E
    has_prev, has_next = seq_index > 0, seq_index < seq_count - 1

    odd = seq_index % 2 == 1
    further = wides[1:] or wides

    def is_neighbour(d):
        return jnp.abs((seq_index ^ d) - seq_index) == 1

    def by_side(near, far):
        return jnp.where(odd, near, far), jnp.where(odd, far, near)

    edges, nears = [], []
    for i in range(2):
        far = received[further[0]][i]
        for d in further[1:]:
            far = jnp.where(is_neighbour(d), received[d][i], far)
        before, after = by_side(received[1][i], far)
        edges.append((before[:BLOCK], after[:BLOCK]))
        nears.append(
            jnp.concatenate(
                [
                    before[BLOCK:],
                    coarse(before[:BLOCK], pool()),
                    coarse(after[:BLOCK], pool()),
                    after[BLOCK:],
                ],
                axis=0,
            )
        )

    def window(lo, hi, valid):
        return nears[0][rows_of(lo, hi - lo)], nears[1][rows_of(lo, hi - lo)], valid, (lo, hi)

    level_pieces = [
        [
            [(edges[0][side], edges[1][side], valid, (side, side + 1))]
            for side, valid in enumerate((has_prev, has_next))
        ],
        [
            [window(0, 1, has_prev), window(2, 4, has_next)],
            [window(0, 2, has_prev), window(3, 4, has_next)],
        ],
    ]
    if top_level == 2:
        pieces = far_pieces(seq_count, received)
        level_pieces.append([pieces])
    else:
        for panel in panels:
            panel[...] = jnp.zeros(panel.shape, BF16)
        for d in range(2, seq_count):
            at = pl.ds(pl.multiple_of((seq_index ^ d) * BLOCK, BLOCK), BLOCK)
            for i in range(2):
                panels[0][i, at] = received[d][i, :BLOCK]
        panel_scratch = pool()
        for level in range(2, top_level + 1):
            panel, pieces = panels[level - 2], []
            for i in range(2):
                if level > 2:
                    panel[i] = coarse(panels[level - 3][i], panel_scratch)
            for index, valid in slots_of(seq_index >> (level - 2), seq_count >> (level - 2)):
                at = pl.ds(pl.multiple_of(index * BLOCK, BLOCK), BLOCK)
                pieces.append((panel[0, at], panel[1, at], valid, at))
            level_pieces.append([pieces])
    level_queries = [[held[0, rows_of(0)], held[0, rows_of(blocks - 1)]]]
    for level in range(1, top_level + 1):
        query = query_refs[level - 1][...]
        step = query.shape[0] // len(level_pieces[level])
        level_queries.append(
            [query[a * step : (a + 1) * step] for a in range(len(level_pieces[level]))]
        )

    def before_of(block):
        return [stats[w, rows_of(block)] for w in range(3)]

    level_units = [
        [
            unit(query, pieces, before_of(block))
            for query, pieces, block in zip(level_queries[0], level_pieces[0], (0, blocks - 1))
        ]
    ]
    for level in range(1, top_level + 1):
        if level == 2 and top_level == 2:
            exps = [exps_ref[p] for p in range(exps_ref.shape[0])]
            level_units.append([(None, None, None, exps, [e.astype(BF16) for e in exps])])
            continue
        level_units.append(
            [unit(q, pieces) for q, pieces in zip(level_queries[level], level_pieces[level])]
        )

    def stacked(level, which):
        units = [u[which] for u in level_units[level]]
        if level == 0:
            units = [units[0], stats[which, rows_of(1, blocks - 2)], units[1]]
        return jnp.concatenate(units, axis=0)

    run = None if top_level == 2 else [stacked(top_level, w) for w in range(3)]
    own_factors, run_factors = [None] * top_level, [None] * top_level
    for level in range(top_level - 1, -1, -1):
        if run is None:
            up_peak, up_total, up_sums = [up_ref[w] for w in range(3)]
        else:
            up_peak, up_total, up_sums = [spread(x, pool()) for x in run]
        peak, total, sums = [stacked(level, w) for w in range(3)]
        both = jnp.maximum(peak, up_peak)
        own = jnp.exp2(peak - both)
        up = 2.0 * jnp.exp2(up_peak - both)
        own_factors[level], run_factors[level] = own, up
        run = [both, own * total + up * up_total, own * sums + up * up_sums]

    inverse = 1.0 / run[1]
    attended = run[2] * inverse
    attended_ref[...] = attended.astype(BF16)

    cot = held[3].astype(F32)
    grad, shift = cot * inverse, row_sum(cot * attended) * inverse
    level_grads = []
    for level in range(top_level):
        level_grads.append((own_factors[level] * grad, own_factors[level] * shift))
        grad = pair_sum(run_factors[level] * grad, pool())
        shift = pair_sum(run_factors[level] * shift, pool())
    level_grads.append((grad, shift))
    back[0] = stacked(0, 0)
    back[1], back[2] = level_grads[0]

    for panel_grad in panel_grads:
        panel_grad[...] = jnp.zeros(panel_grad.shape, F32)

    device_grads = {d: [None, None] for d in range(2, seq_count)}
    grad_queries = []
    parts_of = [[[[] for _ in range(4)] for _ in range(2)] for _ in range(2)]
    for level in range(top_level, -1, -1):
        grad, shift = level_grads[level]
        step = level_queries[level][0].shape[0]
        level_parts = []
        for a, (query, pieces) in enumerate(zip(level_queries[level], level_pieces[level])):
            at = a if level > 0 else a * (blocks - 1)
            cut = slice(at * step, (at + 1) * step)
            grad_rounded = grad[cut].astype(BF16)
            grad_scaled = (grad[cut] * scale).astype(BF16)
            shift_scaled = shift[cut] * scale
            exps, rounded = level_units[level][a][3:]
            query_parts = []
            for piece, e, r in zip(pieces, exps, rounded):
                key, value, _, where = piece
                score_grad = nt(grad_scaled, value) - across(shift_scaled, e.shape[1])
                score_grad = (e * score_grad).astype(BF16)
                query_parts.append(nn(score_grad, key))
                outs = tn(score_grad, query), tn(r, grad_rounded)
                for i in range(2):
                    if level >= 2 and top_level == 2:
                        device_grads[where][i] = outs[i]
                        continue
                    if level >= 2:
                        panel_grads[level - 2][i, where] += outs[i]
                        continue
                    lo, hi = where
                    for b in range(lo, hi):
                        parts_of[level][i][b].append(outs[i][rows_of(b - lo)])
            level_parts.append(total_of(query_parts))
        grad_queries.append(level_parts)

    run_grad = grad_queries[0][0]
    for level_parts in grad_queries[1:-1]:
        run_grad = jnp.concatenate(level_parts, axis=0) + 0.5 * spread(run_grad, pool())
    partial_ref[...] = 0.5 * spread(run_grad, pool())
    for a, block in enumerate((0, blocks - 1)):
        partial_ref[rows_of(block)] += grad_queries[-1][a]

    if top_level > 2:
        for level in range(top_level, 2, -1):
            for i in range(2):
                panel_grads[level - 3][i] += 0.5 * spread(panel_grads[level - 2][i], panel_scratch)
        for d in device_grads:
            at = pl.ds(pl.multiple_of((seq_index ^ d) * BLOCK, BLOCK), BLOCK)
            device_grads[d] = [panel_grads[0][i, at] for i in range(2)]

    for i in range(2):
        near_grads = [total_of(p) for p in parts_of[1][i]]
        edge_grads = [total_of(p) for p in parts_of[0][i][:2]]
        before = [
            edge_grads[0] + 0.5 * spread(near_grads[1][EDGE:], pool()),
            near_grads[0],
            near_grads[1][:EDGE],
        ]
        after = [
            edge_grads[1] + 0.5 * spread(near_grads[2][:EDGE], pool()),
            near_grads[2][EDGE:],
            near_grads[3],
        ]
        before, after = [jnp.concatenate(p, axis=0).astype(BF16) for p in (before, after)]
        sends[1][i] = jnp.where(odd, before, after)
        far = jnp.where(odd, after, before)
        for d in range(2, seq_count):
            device_grad = device_grads[d][i].astype(BF16)
            if d in wides:
                sends[d][i, :BLOCK] = jnp.where(is_neighbour(d), far[:BLOCK], device_grad)
                sends[d][i, BLOCK:] = far[BLOCK:]
            else:
                sends[d][i] = device_grad


def local_kernel(held, back, partial_ref, merged, attended_hbm, local_ref, grad_query_ref, sem):
    copy = pltpu.make_async_copy(merged, attended_hbm, sem)
    copy.start()
    blocks, width = held.shape[1] // BLOCK, held.shape[2]
    scale = width ** (-0.5)
    factor = scale * LOG2E
    parts = [[[] for _ in range(blocks)] for _ in range(2)]
    for a in range(blocks):
        lo, hi = own_window(a, blocks)
        window = rows_of(lo, hi - lo)
        query, key, value = held[0, rows_of(a)], held[1, window], held[2, window]
        peak, grad, shift = [back[w, rows_of(a)] for w in range(3)]
        wide = key.shape[0]
        exps = jnp.exp2(nt(query, key) * factor - across(peak, wide))
        score_grad = nt((grad * scale).astype(BF16), value) - across(shift * scale, wide)
        score_grad = (exps * score_grad).astype(BF16)
        grad_query_ref[rows_of(a)] = (nn(score_grad, key) + partial_ref[rows_of(a)]).astype(BF16)
        outs = tn(score_grad, query), tn(exps.astype(BF16), grad.astype(BF16))
        for i in range(2):
            for b in range(lo, hi):
                parts[i][b].append(outs[i][rows_of(b - lo)])
    for i in range(2):
        for b in range(blocks):
            local_ref[i, rows_of(b)] = total_of(parts[i][b])
    copy.wait()


def combine_kernel(seq_count, head_count, grad_query_ref, local_ref, *refs):
    received, refs = refs[: seq_count - 1], refs[seq_count - 1 :]
    received = dict(zip(seq_order(seq_count), received))
    outs, refs = refs[:-3], refs[-3:]
    outs = dict(zip([0] + head_order(head_count), outs))
    total, level_1, level_2 = refs
    seq_index, head_index = lax.axis_index("seq"), lax.axis_index("head")
    wides = wide_distances(seq_count)
    rows, width = local_ref.shape[1:]
    share = rows // head_count

    level_1[...] = jnp.zeros(level_1.shape, F32)
    level_2[...] = jnp.zeros(level_2.shape, F32)
    for i in range(2):
        total[i, :rows] = local_ref[i]
    for d in range(1, seq_count):
        got = received[d]
        partner = seq_index ^ d
        if d not in wides:
            for i in range(2):
                level_2[i] += got[i].astype(F32)
            continue

        @pl.when(partner == seq_index - 1)
        def _():
            for i in range(2):
                total[i, :BLOCK] += got[i, :BLOCK].astype(F32)
                level_1[i, EDGE : EDGE + REST] += got[i, BLOCK:].astype(F32)

        @pl.when(partner == seq_index + 1)
        def _():
            for i in range(2):
                total[i, rows - BLOCK : rows] += got[i, :BLOCK].astype(F32)
                level_1[i, :REST] += got[i, BLOCK:].astype(F32)

        @pl.when((partner != seq_index + 1) & (partner != seq_index - 1))
        def _():
            for i in range(2):
                level_2[i] += got[i, :BLOCK].astype(F32)

    for i in range(2):
        half = level_2[i] * 0.5
        for phase in range(2):
            level_1[i, pl.ds(phase, half.shape[0], stride=2), :] += half
        half = level_1[i, : rows // 2] * 0.5
        for phase in range(2):
            total[i, pl.ds(phase, half.shape[0], stride=2), :] += half
    for d in range(head_count):
        at = pl.ds(pl.multiple_of((head_index ^ d) * share, share), share)
        out = outs[d & ~1].at[d & 1] if d & ~1 in paired(head_count) else outs[d]
        out[0] = grad_query_ref[at, :]
        out[1] = total[0, at].astype(BF16)
        out[2] = total[1, at].astype(BF16)


def place_kernel(head_count, *refs):
    parts, outs = refs[:-3], refs[-3:]
    head_index = lax.axis_index("head")
    width = parts[0].shape[-1]
    first = [d for d in head_order(head_count) if d not in last_heads(head_count)]
    for d, part in zip([0] + first, parts):
        at = pl.ds(pl.multiple_of((head_index ^ d) * width, width), width)
        for i in range(3):
            outs[i][:, at] = part[0, i] if d in paired(head_count) else part[i]


def place_late_kernel(head_count, *refs):
    parts, outs, sems = refs[3:-4], refs[-4:-1], refs[-1]
    head_index = lax.axis_index("head")
    width = parts[0].shape[-1]
    copies = []
    far = [d + 1 for d in head_order(head_count) if d in paired(head_count)]
    for k, (d, part) in enumerate(zip(last_heads(head_count) + far, parts)):
        at = pl.ds(pl.multiple_of((head_index ^ d) * width, width), width)
        for i in range(3):
            copies.append(pltpu.make_async_copy(part.at[i], outs[i].at[:, at], sems.at[k, i]))
            copies[-1].start()
    for copy in copies:
        copy.wait()


def call(kernel, outs, scratch, args, in_hbm=0, hbm_outs=0, aliases={}, flops=0):
    return pl.pallas_call(
        kernel,
        out_shape=outs,
        in_specs=[pl.BlockSpec(memory_space=pltpu.HBM)] * in_hbm + [VMEM] * (len(args) - in_hbm),
        out_specs=[pl.BlockSpec(memory_space=pltpu.HBM)] * hbm_outs
        + [VMEM] * (len(outs) - hbm_outs),
        scratch_shapes=scratch,
        input_output_aliases=aliases,
        compiler_params=pltpu.CompilerParams(vmem_limit_bytes=48 * 2**20),
        cost_estimate=pl.CostEstimate(flops=flops, bytes_accessed=2**20, transcendentals=0),
    )(*args)


def swap_all(arrays, axis, distances):
    size = lax.axis_size(axis)
    return [
        lax.ppermute(x, axis, [(i, i ^ d) for i in range(size)]) for x, d in zip(arrays, distances)
    ]


def per_device(queries, keys, values, grad_out):
    seq_count, head_count = lax.axis_size("seq"), lax.axis_size("head")
    rows, width = queries.shape
    assert rows == 4 * BLOCK and width == BLOCK
    fine_blocks = rows * seq_count // BLOCK
    top_level = (fine_blocks // 4).bit_length() - 1
    wides = wide_distances(seq_count)
    distances = seq_order(seq_count)

    def shape(*dims, dtype=BF16):
        return jax.ShapeDtypeStruct(dims, dtype)

    def f32(*dims):
        return pltpu.VMEM(dims, F32)

    def strided(rows):
        return f32(rows + SPARE, width)

    payloads = [shape(2, BLOCK + REST if d in wides else BLOCK, width) for d in distances]
    arguments = [
        pltpu.with_memory_space_constraint(x, pltpu.HBM) for x in (queries, keys, values, grad_out)
    ]
    fine_shapes = [shape(3, rows, width, dtype=F32)]
    fine_shapes += [shape(rows >> level, width) for level in range(1, top_level + 1)]
    fine_scratch = [strided(rows >> level) for level in range(top_level)]
    held, *outs = call(
        functools.partial(prep_kernel, seq_count, top_level),
        [shape(4, rows, width)] + fine_shapes + payloads,
        [strided(rows), strided(rows // 2)] * 2
        + fine_scratch
        + [pltpu.SemaphoreType.DMA((4,))],
        arguments,
        in_hbm=4,
    )
    done, sends = outs[: 1 + top_level], outs[1 + top_level :]
    received = swap_all(sends, "seq", distances)

    unit_flops = 2 * BLOCK * BLOCK * width
    stats, *level_queries = call(
        fine_kernel, fine_shapes, fine_scratch, (held, *done), flops=20 * unit_flops
    )

    panel_rows = [(seq_count >> (level - 2)) * BLOCK for level in range(2, top_level + 1)]
    panel_rows = panel_rows if top_level > 2 else []
    pools = [strided(BLOCK)] * 4 + [strided(r) for r in panel_rows[:1]]
    for level in range(top_level - 1 - (top_level == 2), -1, -1):
        pools += [strided(rows >> level)] * 3
    for level in range(top_level):
        pools += [strided(rows >> level)] * 2
    for level in range(top_level - 1, -1, -1):
        pools += [strided(rows >> level)]
    pools += [strided(BLOCK)] * 4
    ahead = []
    if top_level == 2:
        count = seq_count - 2
        ahead = call(
            functools.partial(far_kernel, seq_count),
            [shape(3, rows // 2, width, dtype=F32), shape(count, rows // 4, BLOCK, dtype=F32)],
            [strided(rows // 2)] * 3,
            (level_queries[-1], *[x for d, x in zip(distances, received) if d > 1]),
            flops=10 * unit_flops,
        )
    main = call(
        functools.partial(main_kernel, seq_count, top_level),
        [shape(rows, width)]
        + payloads
        + [shape(3, rows, width, dtype=F32), shape(rows, width, dtype=F32)],
        [pltpu.VMEM((2, r, width), BF16) for r in panel_rows]
        + [f32(2, r, width) for r in panel_rows]
        + pools,
        (held, stats, *level_queries, *ahead, *received),
        flops=70 * unit_flops,
    )
    merged, sends, back, partial = main[0], main[1:seq_count], main[-2], main[-1]
    returned = swap_all(sends, "seq", distances)

    share = rows // head_count
    attended, local, grad_query = call(
        local_kernel,
        [shape(rows, width), shape(2, rows, width, dtype=F32), shape(rows, width)],
        [pltpu.SemaphoreType.DMA],
        (held, back, partial, merged),
        hbm_outs=1,
        flops=50 * unit_flops,
    )

    order = head_order(head_count)
    own, *parts = call(
        functools.partial(combine_kernel, seq_count, head_count),
        [
            shape(*((2,) if d in paired(head_count) else ()), 3, share, width)
            for d in [0] + order
        ],
        [
            f32(2, rows + SPARE, width),
            f32(2, rows // 2 + SPARE, width),
            f32(2, rows // 4, width),
        ],
        (grad_query, local, *returned),
    )
    parts = dict(zip(order, swap_all(parts, "head", order)))
    far = [parts[d][1] for d in order if d in paired(head_count)]
    late = swap_all(far, "head", [1] * len(far))
    last = [parts.pop(d) for d in last_heads(head_count)] + late
    grads = call(
        functools.partial(place_kernel, head_count),
        [shape(share, head_count * width)] * 3,
        [],
        (own, *parts.values()),
        flops=50 * unit_flops,
    )
    if last:
        grads = call(
            functools.partial(place_late_kernel, head_count),
            [shape(share, head_count * width)] * 3,
            [pltpu.SemaphoreType.DMA((len(last), 3))],
            (*grads, *last),
            in_hbm=3,
            hbm_outs=3,
            aliases={0: 0, 1: 1, 2: 2},
        )
    return (attended, *grads)


def solution(mesh):
    return jax.shard_map(
        per_device,
        mesh=mesh,
        in_specs=(P("seq", "head"),) * 4,
        out_specs=(P("seq", "head"),) + (P(("seq", "head"), None),) * 3,
        check_vma=False,
    )
```
